32 devices in a mesh: dp: 8 (over y, x, core), mp: 4 (over z).
Axes of the slice: x: 2, y: 2, z: 4, core: 2. Of those that a mesh axis runs over, the one named last changes fastest.
Arguments:
- tokens: bfloat16 [4096, 6144], P(('dp', 'mp')), may hold values from -40 to 40
- norm_gain: float32 [6144], replicated, may hold values from 0.1 to 1.9
- q_gain: float32 [128], replicated, may hold values from 0.5 to 8
- k_gain: float32 [128], replicated, may hold values from 0.5 to 8
- w_query: bfloat16 [6144, 4096], P('dp', 'mp'), may hold values from -0.078125 to 0.078125
- w_key: bfloat16 [6144, 4096], P('dp', 'mp'), may hold values from -0.078125 to 0.078125
- w_value: bfloat16 [6144, 4096], P('dp', 'mp'), may hold values from -0.078125 to 0.078125
- grad_heads: bfloat16 [4096, 4096], P('dp', 'mp'), may hold values from -6 to 6
Outputs:
- grad_tokens: bfloat16 [4096, 6144], P(('dp', 'mp'))
- grad_query_weight: bfloat16 [6144, 4096], P('dp', 'mp')
- grad_key_weight: bfloat16 [6144, 4096], P('dp', 'mp')
- grad_value_weight: bfloat16 [6144, 4096], P('dp', 'mp')
The draws below stay inside these ranges and needn't reach their ends.
All inputs are finite; a program needn't handle non-finite values.
Results may differ from the reference program's by a relative error of at most 0.03.
The reference program's roundings to bfloat16 on the way (of `normed`, `values`, `attention_bf`, `grad_value` and `grad_scores`) count: a program that leaves them out, or rounds other values in their place, can miss the bound.
Values may be sent and summed in bfloat16 or wider, within the bound.
No kernel may reach another device: no remote copies, remote signals or barrier semaphores. Data moves between devices by JAX's collectives and lax.ppermute only.
A program may use at most 192 MiB of HBM per device.

```python
import math
import jax
import jax.numpy as jnp
from jax import lax

D = 6144
H = 32
HD = 128
PATCH = 256
HH = 4096
TOK = 512
TOKENS = 4096
N_DP = 8
N_MP = 4


def draw_tokens(key, part):
    key_rows = jax.random.fold_in(key, 1)
    key_cols = jax.random.fold_in(key, 2)
    key_vals = jax.random.fold_in(key, 3)
    row_scale = jnp.exp(jax.random.uniform(key_rows, (TOKENS, 1), jnp.float32, math.log(0.3), math.log(3.0)))
    col_scale = jnp.exp(jax.random.uniform(key_cols, (1, D), jnp.float32, math.log(0.3), math.log(3.0)))
    entries = jnp.clip(jax.random.normal(key_vals, (TOKENS, D), jnp.float32), -4.0, 4.0)
    return (row_scale * col_scale * entries).astype(jnp.bfloat16)


def gain_table(key, salt):
    base_gain = jnp.exp(jax.random.uniform(jax.random.fold_in(key, salt), (HD,), jnp.float32, math.log(0.6), math.log(1.6)))
    return base_gain


def draw_q_gain(key, part):
    return gain_table(key, 21)


def draw_k_gain(key, part):
    return gain_table(key, 22)


def block_scale(own_key, extent, cuts, smallest, largest):
    gain = 1.0
    for position, shards_of in cuts:
        draws = jax.random.uniform(jax.random.fold_in(jax.random.fold_in(own_key, 6), position), (shards_of,), jnp.float32, smallest / len(cuts), largest / len(cuts))
        gain = gain * jnp.repeat(jnp.exp(draws), extent[position] // shards_of).reshape((-1,) + (1,) * (len(extent) - 1 - position))
    return gain


def noise(rng, extent, width, limit, pieces=(), held_as=jnp.bfloat16):
    result = jax.random.normal(rng, extent, jnp.float32) * width
    if len(pieces) > 0:
        result = block_scale(rng, extent, pieces, -0.22, 0.18) * result
    return jnp.clip(result, min=-limit, max=limit).astype(held_as)


def setup_inputs(seed: int = 0) -> dict:
    key_of = jax.random.split(jax.random.key(seed), 9)
    return {
        "tokens": draw_tokens(jax.random.fold_in(key_of[8], 71), 0),
        "norm_gain": jnp.clip(1.0 + 0.18 * jax.random.normal(key_of[1], (D,), jnp.float32), 0.1, 1.9),
        "q_gain": draw_q_gain(jax.random.fold_in(key_of[8], 71), 0),
        "k_gain": draw_k_gain(jax.random.fold_in(key_of[8], 71), 0),
        "w_query": noise(key_of[4], (D, HH), D ** -0.5, 0.078125, ((0, 8), (1, 4))),
        "w_key": noise(key_of[5], (D, HH), D ** -0.5, 0.078125, ((0, 8), (1, 4))),
        "w_value": noise(key_of[6], (D, HH), D ** -0.5, 0.078125, ((0, 8), (1, 4))),
        "grad_heads": noise(key_of[7], (TOKENS, HH), 1.0, 6.0, ((0, 8), (1, 4))),
    }


def normalize(row_data, gain_vector):
    average = lax.optimization_barrier(jnp.mean(row_data, axis=-1, keepdims=True))
    centred = row_data - average
    inv_spread = lax.rsqrt(lax.optimization_barrier(jnp.mean(centred * centred, axis=-1, keepdims=True)) + 1e-06)
    unit_data = centred * inv_spread
    return (unit_data * gain_vector, unit_data, inv_spread)

def normalize_back(grad_out, unit_data, inv_spread, gain_vector):
    scaled = grad_out * gain_vector
    inner_term = lax.optimization_barrier(jnp.mean(scaled * unit_data, axis=-1, keepdims=True))
    return (scaled - lax.optimization_barrier(jnp.mean(scaled, axis=-1, keepdims=True)) - unit_data * inner_term) * inv_spread

def attend_first(query_bf, key_bf, grad_out):
    factor = query_bf.shape[-1] ** (-0.5)
    scores = jnp.einsum('bqhd,bkhd->bhqk', query_bf.astype(jnp.float32), key_bf.astype(jnp.float32)) * factor
    attention = jax.nn.softmax(scores, axis=-1)
    attention_bf = attention.astype(jnp.bfloat16)
    grad_value = jnp.einsum('bhqk,bqhd->bkhd', attention_bf.astype(jnp.float32), grad_out.astype(jnp.float32)).astype(jnp.bfloat16)
    return (attention, grad_value)

def attend_rest(attention, query_bf, key_bf, value_bf, grad_out):
    factor = query_bf.shape[-1] ** (-0.5)
    grad_probs = jnp.einsum('bqhd,bkhd->bhqk', grad_out.astype(jnp.float32), value_bf.astype(jnp.float32))
    row_delta = lax.optimization_barrier(jnp.sum(attention * grad_probs, axis=-1, keepdims=True))
    grad_scores = (attention * (grad_probs - row_delta) * factor).astype(jnp.bfloat16)
    grad_query = jnp.einsum('bhqk,bkhd->bqhd', grad_scores.astype(jnp.float32), key_bf.astype(jnp.float32))
    grad_key = jnp.einsum('bhqk,bqhd->bkhd', grad_scores.astype(jnp.float32), query_bf.astype(jnp.float32))
    return (grad_query, grad_key)

def reference(tokens, norm_gain, q_gain, k_gain, w_query, w_key, w_value, grad_heads):
    normed, unit_rows, row_spread = normalize(tokens.astype(jnp.float32), norm_gain)
    normed = normed.astype(jnp.bfloat16)
    queries = jnp.dot(normed, w_query, preferred_element_type=jnp.float32)
    key_proj = jnp.dot(normed, w_key, preferred_element_type=jnp.float32)
    values = jnp.dot(normed, w_value, preferred_element_type=jnp.float32).astype(jnp.bfloat16)
    layout = (TOKENS // PATCH, PATCH, H, HD)
    query_normed, query_unit, query_spread = normalize(queries.reshape(layout), q_gain)
    key_normed, key_unit, key_spread = normalize(key_proj.reshape(layout), k_gain)
    query_bf = query_normed.astype(jnp.bfloat16)
    key_bf = key_normed.astype(jnp.bfloat16)
    grad_out = grad_heads.reshape(layout)
    attention, grad_value = attend_first(query_bf, key_bf, grad_out)
    grad_qn, grad_kn = attend_rest(attention, query_bf, key_bf, values.reshape(layout), grad_out)
    grad_query = normalize_back(grad_qn, query_unit, query_spread, q_gain).astype(jnp.bfloat16).reshape(TOKENS, HH)
    grad_key = normalize_back(grad_kn, key_unit, key_spread, k_gain).astype(jnp.bfloat16).reshape(TOKENS, HH)
    grad_value = grad_value.reshape(TOKENS, HH)
    block_cols = HH // N_MP
    grad_parts = (grad_query, grad_key, grad_value)
    weight_parts = (w_query, w_key, w_value)

    def add_block(total, block_index):
        begin_col = (block_index * block_cols).astype(jnp.int32)
        partial_sum = jnp.zeros((TOKENS, D), jnp.float32)
        for grad_item, weight_item in zip(grad_parts, weight_parts):
            grad_cols = lax.dynamic_slice_in_dim(grad_item, begin_col, block_cols, 1)
            weight_cols = lax.dynamic_slice_in_dim(weight_item, begin_col, block_cols, 1)
            partial_sum = partial_sum + jnp.dot(grad_cols, weight_cols.T, preferred_element_type=jnp.float32)
        rounded = lax.optimization_barrier(partial_sum.astype(jnp.bfloat16)).astype(jnp.float32)
        return (total + rounded, None)
    grad_normed, _ = lax.scan(add_block, jnp.zeros((TOKENS, D), jnp.float32), jnp.arange(N_MP, dtype=jnp.int32))
    grad_tokens = normalize_back(grad_normed, unit_rows, row_spread, norm_gain).astype(jnp.bfloat16)
    grouped = (normed.reshape(N_DP, TOK, D), grad_query.reshape(N_DP, TOK, HH), grad_key.reshape(N_DP, TOK, HH), grad_value.reshape(N_DP, TOK, HH))

    def accumulate(carried, group_data):
        row_block = group_data[0]
        updated = tuple((running + lax.optimization_barrier(jnp.dot(row_block.T, grad_item, preferred_element_type=jnp.float32).astype(jnp.bfloat16)).astype(jnp.float32) for running, grad_item in zip(carried, group_data[1:])))
        return (updated, None)
    zero_block = jnp.zeros((D, HH), jnp.float32)
    totals, _ = lax.scan(accumulate, (zero_block, zero_block, zero_block), grouped)
    return (grad_tokens, totals[0].astype(jnp.bfloat16), totals[1].astype(jnp.bfloat16), totals[2].astype(jnp.bfloat16))
```

```python
import functools

import jax
import jax.numpy as jnp
from jax import lax
from jax.experimental import pallas as pl
from jax.experimental.pallas import tpu as pltpu
from jax.sharding import PartitionSpec as P

PATCH = 256
BF = jnp.bfloat16
F32 = jnp.float32


def normalize(row_data, gain_vector):
    average = jnp.mean(row_data, axis=-1, keepdims=True)
    centred = row_data - average
    inv_spread = lax.rsqrt(jnp.mean(centred * centred, axis=-1, keepdims=True) + 1e-06)
    unit_data = centred * inv_spread
    return (unit_data * gain_vector, unit_data, inv_spread)


def normalize_back(grad_out, unit_data, inv_spread, gain_vector):
    scaled = grad_out * gain_vector
    inner_term = jnp.mean(scaled * unit_data, axis=-1, keepdims=True)
    return (scaled - jnp.mean(scaled, axis=-1, keepdims=True) - unit_data * inner_term) * inv_spread


def dot_nt(a, b):
    return lax.dot_general(a, b, (((1,), (1,)), ((), ())), preferred_element_type=F32)


def dot_tn(a, b):
    return lax.dot_general(a, b, (((0,), (0,)), ((), ())), preferred_element_type=F32)


def attention_of(query_bf, key_bf):
    scores = dot_nt(key_bf, query_bf) * query_bf.shape[-1] ** (-0.5)
    raised = jnp.exp(scores - jnp.max(scores, axis=0, keepdims=True))
    return raised * (1.0 / jnp.sum(raised, axis=0, keepdims=True))


def rows_of(ref):
    block = ref[...]
    return block.reshape(-1, block.shape[-1])


def first_kernel(q_ref, k_ref, g_ref, q_gain_ref, k_gain_ref, grad_value_ref):
    query_bf = normalize(rows_of(q_ref), q_gain_ref[...])[0].astype(BF)
    key_bf = normalize(rows_of(k_ref), k_gain_ref[...])[0].astype(BF)
    attention = attention_of(query_bf, key_bf).astype(BF)
    grad_value = jnp.dot(attention, rows_of(g_ref), preferred_element_type=F32)
    grad_value_ref[...] = grad_value.astype(BF).reshape(grad_value_ref.shape)


def rest_kernel(q_ref, k_ref, v_ref, g_ref, q_gain_ref, k_gain_ref, grad_query_ref, grad_key_ref):
    q_gain, k_gain = q_gain_ref[...], k_gain_ref[...]
    query_normed, query_unit, query_spread = normalize(rows_of(q_ref), q_gain)
    key_normed, key_unit, key_spread = normalize(rows_of(k_ref), k_gain)
    query_bf, key_bf = query_normed.astype(BF), key_normed.astype(BF)
    attention = attention_of(query_bf, key_bf)
    grad_probs = dot_nt(rows_of(v_ref), rows_of(g_ref))
    delta = jnp.sum(attention * grad_probs, axis=0, keepdims=True)
    factor = query_bf.shape[-1] ** (-0.5)
    grad_scores = (attention * (grad_probs - delta) * factor).astype(BF)
    grad_kn = jnp.dot(grad_scores, query_bf, preferred_element_type=F32)
    grad_qn = dot_tn(grad_scores, key_bf)
    grad_query = normalize_back(grad_qn, query_unit, query_spread, q_gain)
    grad_key = normalize_back(grad_kn, key_unit, key_spread, k_gain)
    grad_query_ref[...] = grad_query.astype(BF).reshape(grad_query_ref.shape)
    grad_key_ref[...] = grad_key.astype(BF).reshape(grad_key_ref.shape)


def attention_call(kernel, arrays, gains, n_out):
    levels, groups, own, columns = arrays[0].shape
    head = gains[0].shape[-1]
    span = PATCH // own
    block = pl.BlockSpec((span, 1, own, head), lambda g, i, h: (i, g, 0, h))
    gain_block = pl.BlockSpec((1, head), lambda g, i, h: (0, 0))
    pairs = groups * (levels // span) * (columns // head)
    return pl.pallas_call(
        kernel,
        grid=(groups, levels // span, columns // head),
        in_specs=[block] * len(arrays) + [gain_block] * len(gains),
        out_specs=[block] * n_out,
        out_shape=[jax.ShapeDtypeStruct(arrays[0].shape, BF)] * n_out,
        cost_estimate=pl.CostEstimate(
            flops=pairs * 8 * PATCH * PATCH * head,
            bytes_accessed=4 * len(arrays) * arrays[0].size,
            transcendentals=pairs * PATCH * PATCH,
        ),
    )(*arrays, *[gain.reshape(1, head) for gain in gains])


def per_device(n_dp, n_mp, tokens, norm_gain, q_gain, k_gain, w_query, w_key, w_value, grad_heads):
    own, width = tokens.shape
    rows, cols = w_query.shape[0], w_query.shape[1] // 2
    n_chips = n_dp // 2
    place = lax.axis_index("dp")
    core = place & 1

    def swap(array, bit):
        return lax.ppermute(array, "dp", [(i, i ^ bit) for i in range(n_dp)])

    def half(array, which):
        return lax.dynamic_slice_in_dim(array, which * cols, cols, 1)

    def core_order(mine, other, axis):
        return jnp.where(
            core == 0,
            jnp.concatenate([mine, other], axis=axis),
            jnp.concatenate([other, mine], axis=axis),
        )

    def after(array, *others):
        return lax.optimization_barrier((array, *others))[0]

    ring = list(range(0, n_mp, 2)) + list(range(n_mp - 1, 0, -2))
    level = lax.axis_index("mp")
    spot = jnp.where(level % 2 == 0, level // 2, n_mp - 1 - level // 2)
    ring_pairs = [(ring[i], ring[(i + 1) % n_mp]) for i in range(n_mp)]

    def level_at(back):
        at = (spot + 2 * n_mp - back) % n_mp
        return jnp.where(at < n_mp // 2, 2 * at, 2 * (n_mp - 1 - at) + 1)

    def ring_on(array):
        return lax.ppermute(array, "mp", ring_pairs)

    def feature_block(array, r):
        return lax.dynamic_slice_in_dim(array, (place ^ r) * rows, rows, 1)

    normed_own, unit_rows, row_spread = normalize(tokens.astype(F32), norm_gain)
    normed_own = normed_own.astype(BF)
    even = jnp.concatenate([feature_block(normed_own, 2 * j) for j in range(n_chips)], axis=1)
    odd = jnp.concatenate([feature_block(normed_own, 2 * j + 1) for j in range(n_chips)], axis=1)
    block = core_order(even, swap(odd, 1), 0)

    def chip_shard(weight):
        return jnp.concatenate([half(weight, core), swap(half(weight, 1 - core), 1)], axis=0)

    def gather_start(shard):
        held = {0: shard}
        bit = 8
        while bit < n_dp:
            held.update({j ^ (bit // 2): swap(part, bit) for j, part in list(held.items())})
            bit *= 2
        for j, part in list(held.items()):
            held[j ^ 1] = swap(part, 2)
            held[j ^ 2] = swap(part, 4)
        return held

    def gather_rest(held):
        for j in range(0, n_chips, 4):
            upper = swap(held[j ^ 1][:rows], 4)
            lower = swap(held[j ^ 2][rows:], 2)
            held[j ^ 3] = jnp.concatenate([upper, lower], axis=0)
        return [held[j] for j in range(n_chips)]

    shard_query, shard_key, shard_value = (chip_shard(w) for w in (w_query, w_key, w_value))
    held_query, held_key = gather_start(shard_query), gather_start(shard_key)
    full_query = gather_rest(held_query)
    full_key = gather_rest(held_key)
    shard_value = after(shard_value, full_query[3], full_key[3])
    full_value = gather_rest(gather_start(shard_value))
    whole_query, whole_key, whole_value = (
        jnp.concatenate(parts, axis=0) for parts in (full_query, full_key, full_value)
    )

    step_rows = 2 * own
    normed = jnp.zeros((n_mp * step_rows, width), BF)
    for step in range(n_mp):
        beside = swap(block, 1)
        pieces = []
        for j in range(n_chips):
            pieces += [block[:, j * rows : (j + 1) * rows], beside[:, j * rows : (j + 1) * rows]]
        normed = lax.dynamic_update_slice_in_dim(
            normed, jnp.concatenate(pieces, axis=1), level_at(step) * step_rows, 0
        )
        if step < n_mp - 1:
            block = ring_on(block)

    grads_mine = half(grad_heads, core).reshape(n_mp, 1, own, cols)
    grads_other = swap(half(grad_heads, 1 - core), 1).reshape(n_mp, 1, own, cols)
    grad_out = core_order(grads_mine, grads_other, 1)

    layout = (n_mp, 2, own, cols)
    queries = jnp.dot(normed, whole_query, preferred_element_type=F32).reshape(layout)
    key_proj = jnp.dot(normed, whole_key, preferred_element_type=F32).reshape(layout)
    gains = (q_gain, k_gain)
    (grad_value,) = attention_call(first_kernel, (queries, key_proj, grad_out), gains, 1)

    def weight_product(grad, j):
        chip_rows = normed[:, j * 2 * rows : (j + 1) * 2 * rows]
        return dot_tn(chip_rows, grad)

    def scatter_weight(grad):
        totals = {}
        for j in range(0, n_chips, 4):
            far = weight_product(grad, j ^ 3).astype(BF)
            from_x = swap(far[:rows], 2)
            from_y = swap(far[rows:], 4)
            next_x = weight_product(grad, j ^ 1)
            next_y = weight_product(grad, j ^ 2)
            mine = weight_product(grad, j)
            next_x = jnp.concatenate([next_x[:rows], next_x[rows:] + from_y.astype(F32)], axis=0)
            next_y = jnp.concatenate([next_y[:rows] + from_x.astype(F32), next_y[rows:]], axis=0)
            from_x = swap(next_x.astype(BF), 2)
            from_y = swap(next_y.astype(BF), 4)
            totals[j] = mine + from_x.astype(F32) + from_y.astype(F32)
        bit = n_dp // 2
        while bit >= 8:
            for j in [j for j in totals if j < bit // 2]:
                totals[j] = totals[j] + swap(totals.pop(j ^ (bit // 2)).astype(BF), bit).astype(F32)
            bit //= 2
        total = totals[0].astype(BF)
        return core_order(total[:rows], swap(total[rows:], 1), 1)

    flat = (n_mp * step_rows, cols)
    grad_value = grad_value.reshape(flat)
    out_value = scatter_weight(grad_value)

    values = jnp.dot(normed, whole_value, preferred_element_type=F32).astype(BF).reshape(layout)
    grad_query, grad_key = attention_call(
        rest_kernel, (queries, key_proj, values, grad_out), gains, 2
    )
    grad_query, grad_key = grad_query.reshape(flat), grad_key.reshape(flat)

    arrived = None
    for step in range(n_mp):
        start = level_at(step + 1) * step_rows
        partial = None
        for grad, weight in (
            (grad_query, whole_query),
            (grad_key, whole_key),
            (grad_value, whole_value),
        ):
            term = dot_nt(lax.dynamic_slice_in_dim(grad, start, step_rows, 0), weight)
            partial = term if partial is None else partial + term
        pieces = [partial[:, r * rows : (r + 1) * rows] for r in range(n_dp)]
        sent = jnp.concatenate(pieces[1::2], axis=1).astype(BF)
        kept = jnp.concatenate(pieces[0::2], axis=1)
        kept = kept + swap(sent, 1).astype(F32)
        if arrived is not None:
            kept = kept + arrived.astype(F32)
        if step < n_mp - 1:
            arrived = ring_on(kept.astype(BF))

    out_query = scatter_weight(grad_query)
    out_key = scatter_weight(grad_key)

    mine = lax.dynamic_slice_in_dim(kept, core * own, own, 0)
    other = swap(lax.dynamic_slice_in_dim(kept, (1 - core) * own, own, 0).astype(BF), 1).astype(F32)
    pieces = []
    for j in range(n_chips):
        pieces += [mine[:, j * rows : (j + 1) * rows], other[:, j * rows : (j + 1) * rows]]
    relative = jnp.concatenate(pieces, axis=1)
    grad_normed = jnp.concatenate([feature_block(relative, b) for b in range(n_dp)], axis=1)
    grad_tokens = normalize_back(grad_normed, unit_rows, row_spread, norm_gain).astype(BF)
    return (grad_tokens, out_query, out_key, out_value)


def solution(mesh):
    matrix = P("dp", "mp")
    token_rows = P(("dp", "mp"), None)
    return jax.shard_map(
        functools.partial(per_device, mesh.shape["dp"], mesh.shape["mp"]),
        mesh=mesh,
        in_specs=(token_rows, P(), P(), P(), matrix, matrix, matrix, matrix),
        out_specs=(token_rows, matrix, matrix, matrix),
        check_vma=False,
    )
```

```python
import functools

import jax
import jax.numpy as jnp
from jax import lax
from jax.experimental import pallas as pl
from jax.experimental.pallas import tpu as pltpu
from jax.sharding import PartitionSpec as P

PATCH = 256
BF = jnp.bfloat16
F32 = jnp.float32


def normalize(row_data, gain_vector):
    average = jnp.mean(row_data, axis=-1, keepdims=True)
    centred = row_data - average
    inv_spread = lax.rsqrt(jnp.mean(centred * centred, axis=-1, keepdims=True) + 1e-06)
    unit_data = centred * inv_spread
    return (unit_data * gain_vector, unit_data, inv_spread)


def normalize_back(grad_out, unit_data, inv_spread, gain_vector):
    scaled = grad_out * gain_vector
    inner_term = jnp.mean(scaled * unit_data, axis=-1, keepdims=True)
    return (scaled - jnp.mean(scaled, axis=-1, keepdims=True) - unit_data * inner_term) * inv_spread


def dot_nt(a, b):
    return lax.dot_general(a, b, (((1,), (1,)), ((), ())), preferred_element_type=F32)


def dot_tn(a, b):
    return lax.dot_general(a, b, (((0,), (0,)), ((), ())), preferred_element_type=F32)


def attention_of(query_bf, key_bf):
    scores = dot_nt(key_bf, query_bf) * query_bf.shape[-1] ** (-0.5)
    raised = jnp.exp(scores - jnp.max(scores, axis=0, keepdims=True))
    return raised * (1.0 / jnp.sum(raised, axis=0, keepdims=True))


def first_kernel(q_ref, k_ref, g_ref, q_gain_ref, k_gain_ref, grad_value_ref, turned_ref):
    query_bf = normalize(q_ref[...], q_gain_ref[...])[0].astype(BF)
    key_bf = normalize(k_ref[...], k_gain_ref[...])[0].astype(BF)
    attention = attention_of(query_bf, key_bf).astype(BF)
    grad_value = jnp.dot(attention, g_ref[...], preferred_element_type=F32)
    grad_value_ref[...] = grad_value.astype(BF)
    turned_ref[...] = grad_value.T.astype(BF)


def rest_kernel(
    q_ref, k_ref, v_ref, g_ref, q_gain_ref, k_gain_ref, grad_q_ref, turned_q_ref, grad_k_ref, turned_k_ref
):
    q_gain, k_gain = q_gain_ref[...], k_gain_ref[...]
    query_normed, query_unit, query_spread = normalize(q_ref[...], q_gain)
    key_normed, key_unit, key_spread = normalize(k_ref[...], k_gain)
    query_bf, key_bf = query_normed.astype(BF), key_normed.astype(BF)
    attention = attention_of(query_bf, key_bf)
    grad_probs = dot_nt(v_ref[...], g_ref[...])
    delta = jnp.sum(attention * grad_probs, axis=0, keepdims=True)
    factor = query_bf.shape[-1] ** (-0.5)
    grad_scores = (attention * (grad_probs - delta) * factor).astype(BF)
    grad_kn = jnp.dot(grad_scores, query_bf, preferred_element_type=F32)
    grad_qn = dot_tn(grad_scores, key_bf)
    grad_query = normalize_back(grad_qn, query_unit, query_spread, q_gain)
    grad_key = normalize_back(grad_kn, key_unit, key_spread, k_gain)
    grad_q_ref[...] = grad_query.astype(BF)
    turned_q_ref[...] = grad_query.T.astype(BF)
    grad_k_ref[...] = grad_key.astype(BF)
    turned_k_ref[...] = grad_key.T.astype(BF)


def attention_call(kernel, arrays, gains, n_out):
    tokens, columns = arrays[0].shape
    head = gains[0].shape[-1]
    block = pl.BlockSpec((PATCH, head), lambda i, h: (i, h))
    turned = pl.BlockSpec((head, PATCH), lambda i, h: (h, i))
    gain_block = pl.BlockSpec((1, head), lambda i, h: (0, 0))
    pairs = (tokens // PATCH) * (columns // head)
    return pl.pallas_call(
        kernel,
        grid=(tokens // PATCH, columns // head),
        in_specs=[block] * len(arrays) + [gain_block] * len(gains),
        out_specs=[block, turned] * n_out,
        out_shape=[
            jax.ShapeDtypeStruct((tokens, columns), BF),
            jax.ShapeDtypeStruct((columns, tokens), BF),
        ]
        * n_out,
        cost_estimate=pl.CostEstimate(
            flops=pairs * 8 * PATCH * PATCH * head,
            bytes_accessed=4 * len(arrays) * arrays[0].size,
            transcendentals=pairs * PATCH * PATCH,
        ),
    )(*arrays, *[gain.reshape(1, head) for gain in gains])


def per_device(n_dp, n_mp, tokens, norm_gain, q_gain, k_gain, w_query, w_key, w_value, grad_heads):
    own, width = tokens.shape
    rows, cols = w_query.shape[0], w_query.shape[1] // 2
    n_chips = n_dp // 2
    group = n_mp * own
    place = lax.axis_index("dp")
    core = place & 1

    def swap(array, bit):
        return lax.ppermute(array, "dp", [(i, i ^ bit) for i in range(n_dp)])

    def half(array, which):
        return lax.dynamic_slice_in_dim(array, which * cols, cols, 1)

    def after(arrays, *others):
        flat, tree = jax.tree.flatten(arrays)
        done = lax.optimization_barrier((*flat, *jax.tree.leaves(others)))
        return jax.tree.unflatten(tree, done[: len(flat)])

    def add(a, b):
        return a.astype(F32) + b.astype(F32)

    ring = list(range(0, n_mp, 2)) + list(range(n_mp - 1, 0, -2))
    level = lax.axis_index("mp")
    spot = jnp.where(level % 2 == 0, level // 2, n_mp - 1 - level // 2)
    ring_pairs = [(ring[i], ring[(i + 1) % n_mp]) for i in range(n_mp)]

    def level_at(back):
        at = (spot + 2 * n_mp - back) % n_mp
        return jnp.where(at < n_mp // 2, 2 * at, 2 * (n_mp - 1 - at) + 1)

    def ring_on(arrays):
        return [lax.ppermute(array, "mp", ring_pairs) for array in arrays]

    def feature_block(array, r):
        return lax.dynamic_slice_in_dim(array, (place ^ r) * rows, rows, 1)

    def pieces_of(weight):
        return {0: half(weight, core), 1: swap(half(weight, 1 - core), 1)}

    def gather_start(held):
        held = dict(held)
        bit = 8
        while bit < n_dp:
            held.update({r ^ bit: swap(part, bit) for r, part in list(held.items())})
            bit *= 2
        for r, part in list(held.items()):
            held[r ^ 2] = swap(part, 2)
            held[r ^ 4] = swap(part, 4)
        return held

    def gather_rest(held):
        held = dict(held)
        for r in range(0, n_dp, 8):
            held[r ^ 6] = swap(held[r ^ 2], 4)
            held[r ^ 7] = swap(held[r ^ 5], 2)
        return held

    def relayed(held):
        return [held[r ^ f] for r in range(0, n_dp, 8) for f in (6, 7)]

    def whole(held):
        return jnp.concatenate([held[r] for r in (*range(0, n_dp, 2), *range(1, n_dp, 2))], axis=0)

    held_query = gather_start(pieces_of(w_query))

    normed_own, unit_rows, row_spread = normalize(tokens.astype(F32), norm_gain)
    normed_own = normed_own.astype(BF)
    even = jnp.concatenate([feature_block(normed_own, r) for r in range(0, n_dp, 2)], axis=1)
    odd = jnp.concatenate([feature_block(normed_own, r) for r in range(1, n_dp, 2)], axis=1)
    blocks = [even, swap(odd, 1)]

    held_key = gather_start(after(pieces_of(w_key), even))
    value_pieces = pieces_of(w_value)
    grads_mine = half(grad_heads, core)
    grads_other = swap(half(grad_heads, 1 - core), 1)

    normed = jnp.zeros((2 * group, width), BF)

    def put(normed, blocks, step):
        start = level_at(step) * own
        mine, other = core * group + start, (1 - core) * group + start
        beside_other, beside_mine = (swap(block, 1) for block in blocks)
        for block, at, column in (
            (blocks[0], mine, 0),
            (blocks[1], other, 0),
            (beside_other, other, width // 2),
            (beside_mine, mine, width // 2),
        ):
            normed = lax.dynamic_update_slice(normed, block, (at, column))
        return normed

    grad_out = jnp.zeros((2 * group, cols), BF)
    grad_out = lax.dynamic_update_slice_in_dim(grad_out, grads_mine, core * group, 0)
    grad_out = lax.dynamic_update_slice_in_dim(grad_out, grads_other, (1 - core) * group, 0)

    normed = put(normed, blocks, 0)
    for step in range(1, n_mp):
        blocks = ring_on(blocks)
        if step == 1:
            held_query, blocks, normed = after((held_query, blocks, normed))
            held_query = gather_rest(held_query)
        elif step == 2:
            held_key, blocks = after((held_key, blocks))
            held_key = gather_rest(held_key)
            held_value = gather_start(after(value_pieces, relayed(held_query)))
        normed = put(normed, blocks, step)
    normed, held_query, held_key = after((normed, held_query, held_key))
    full_query, full_key = whole(held_query), whole(held_key)

    queries = jnp.dot(normed, full_query, preferred_element_type=F32)
    key_proj = jnp.dot(normed, full_key, preferred_element_type=F32)
    gains = (q_gain, k_gain)
    grad_value, turned_value = attention_call(first_kernel, (queries, key_proj, grad_out), gains, 1)

    def product(turned, r):
        unit = (r & 1) * n_chips + r // 2
        side = normed[:, unit * rows : (unit + 1) * rows]
        return jnp.dot(turned, side, preferred_element_type=F32)

    def scatter_start(turned):
        state = {}
        for r in range(0, n_dp, 8):
            far = [product(turned, r ^ f).astype(BF) for f in (6, 7)]
            state[r, "far"] = [swap(far[0], 2), swap(far[1], 4)]
            next_x, next_y = [product(turned, r ^ f).astype(BF) for f in (2, 5)]
            state[r, "sent"] = [swap(next_x, 2), swap(next_y, 4)]
            state[r, "next"] = [product(turned, r ^ f) for f in (3, 4)]
            state[r, "own"] = [product(turned, r ^ f) for f in (0, 1)]
        return state

    def scatter_rest(state):
        state = dict(state)
        for r in range(0, n_dp, 8):
            from_x, from_y = state[r, "far"]
            next_x, next_y = state[r, "next"]
            next_x, next_y = add(next_x, from_y).astype(BF), add(next_y, from_x).astype(BF)
            state[r, "late"] = [swap(next_x, 2), swap(next_y, 4)]
        return state

    def scatter_end(state):
        totals = {}
        for r in range(0, n_dp, 8):
            own_even, own_odd = state[r, "own"]
            even_x, odd_y = state[r, "sent"]
            odd_x, even_y = state[r, "late"]
            totals[r] = [add(own_even, even_x) + even_y, add(own_odd, odd_x) + odd_y]
        bit = n_dp // 2
        while bit >= 8:
            for r in [r for r in totals if r < bit]:
                passed = [swap(total.astype(BF), bit) for total in totals.pop(r ^ bit)]
                totals[r] = [add(a, b) for a, b in zip(totals[r], passed)]
            bit //= 2
        mine, other = [total.astype(BF) for total in totals[0]]
        result = jnp.zeros((2 * cols, rows), BF)
        result = lax.dynamic_update_slice_in_dim(result, mine, core * cols, 0)
        result = lax.dynamic_update_slice_in_dim(result, swap(other, 1), (1 - core) * cols, 0)
        return result.T

    def computed(state):
        return [state[key] for key in state if key[1] in ("next", "own")]

    held_value, turned_value = after((held_value, turned_value))
    held_value = gather_rest(held_value)
    state_value = scatter_start(turned_value)

    full_value = whole(after(held_value, computed(state_value)))
    values = jnp.dot(normed, full_value, preferred_element_type=F32).astype(BF)
    grad_query, turned_query, grad_key, turned_key = attention_call(
        rest_kernel, (queries, key_proj, values, grad_out), gains, 2
    )

    state_value, turned_query = after((state_value, turned_query), turned_key)
    state_value = scatter_rest(state_value)
    state_query = scatter_start(turned_query)

    grads = after([grad_query, grad_key, grad_value], computed(state_query))
    grads = [grad.reshape(2, n_mp, own, cols) for grad in grads]
    arrived = None
    for step in range(n_mp):
        at = level_at(step + 1)
        partial = None
        for grad, weight in zip(grads, (full_query, full_key, full_value)):
            chosen = lax.dynamic_slice_in_dim(grad, at, 1, 1).reshape(2 * own, cols)
            term = dot_nt(chosen, weight)
            partial = term if partial is None else partial + term
        sent = partial[:, width // 2 :].astype(BF)
        if step == 0:
            state_key = scatter_start(after(turned_key, sent))
            grads = after(grads, computed(state_key))
        elif step == 1:
            state_query = scatter_rest(after(state_query, sent))
        elif step == n_mp - 2:
            state_key = scatter_rest(after(state_key, sent))
        kept = add(partial[:, : width // 2], swap(sent, 1))
        if arrived is not None:
            kept = add(kept, arrived)
        if step < n_mp - 1:
            (arrived,) = ring_on([kept.astype(BF)])

    out_value, out_query, out_key = (
        scatter_end(state) for state in (state_value, state_query, state_key)
    )

    mine = lax.dynamic_slice_in_dim(kept, core * own, own, 0)
    other = swap(lax.dynamic_slice_in_dim(kept, (1 - core) * own, own, 0).astype(BF), 1).astype(F32)
    units = jnp.concatenate([mine, other], axis=1)
    ordered = []
    for b in range(n_dp):
        r = b ^ place
        unit = (r & 1) * n_chips + r // 2
        ordered.append(lax.dynamic_slice_in_dim(units, unit * rows, rows, 1))
    grad_normed = jnp.concatenate(ordered, axis=1)
    grad_tokens = normalize_back(grad_normed, unit_rows, row_spread, norm_gain).astype(BF)
    return (grad_tokens, out_query, out_key, out_value)


def solution(mesh):
    matrix = P("dp", "mp")
    token_rows = P(("dp", "mp"), None)
    return jax.shard_map(
        functools.partial(per_device, mesh.shape["dp"], mesh.shape["mp"]),
        mesh=mesh,
        in_specs=(token_rows, P(), P(), P(), matrix, matrix, matrix, matrix),
        out_specs=(token_rows, matrix, matrix, matrix),
        check_vma=False,
    )
```

```python
import functools

import jax
import jax.numpy as jnp
from jax import lax
from jax.experimental import pallas as pl
from jax.experimental.pallas import tpu as pltpu
from jax.sharding import PartitionSpec as P

PATCH = 256
BF = jnp.bfloat16
F32 = jnp.float32


def normalize(row_data, gain_vector):
    average = jnp.mean(row_data, axis=-1, keepdims=True)
    centred = row_data - average
    inv_spread = lax.rsqrt(jnp.mean(centred * centred, axis=-1, keepdims=True) + 1e-06)
    unit_data = centred * inv_spread
    return (unit_data * gain_vector, unit_data, inv_spread)


def normalize_back(grad_out, unit_data, inv_spread, gain_vector):
    scaled = grad_out * gain_vector
    inner_term = jnp.mean(scaled * unit_data, axis=-1, keepdims=True)
    return (scaled - jnp.mean(scaled, axis=-1, keepdims=True) - unit_data * inner_term) * inv_spread


def dot_nt(a, b):
    return lax.dot_general(a, b, (((1,), (1,)), ((), ())), preferred_element_type=F32)


def dot_tn(a, b):
    return lax.dot_general(a, b, (((0,), (0,)), ((), ())), preferred_element_type=F32)


def params(mib):
    return pltpu.CompilerParams(vmem_limit_bytes=mib * 2**20)


def blank(shape, dtype):
    return pl.pallas_call(
        lambda out_ref: None,
        out_shape=jax.ShapeDtypeStruct(shape, dtype),
        out_specs=pl.BlockSpec(memory_space=pl.ANY),
    )()


def attention_of(query_bf, key_bf):
    scores = dot_nt(key_bf, query_bf) * query_bf.shape[-1] ** (-0.5)
    raised = jnp.exp(scores - jnp.max(scores, axis=0, keepdims=True))
    return raised * (1.0 / jnp.sum(raised, axis=0, keepdims=True))


def first_kernel(qk_ref, g_ref, gains_ref, turned_ref):
    head, cols = gains_ref.shape[1], g_ref.shape[1]
    for h in range(cols // head):
        at, key_at = pl.ds(h * head, head), pl.ds(cols + h * head, head)
        query_bf = normalize(qk_ref[:, at], gains_ref[0:1])[0].astype(BF)
        key_bf = normalize(qk_ref[:, key_at], gains_ref[1:2])[0].astype(BF)
        attention = attention_of(query_bf, key_bf).astype(BF)
        grad_value = jnp.dot(attention, g_ref[:, at], preferred_element_type=F32)
        turned_ref[at, :] = grad_value.T.astype(BF)


def rest_kernel(qk_ref, g_ref, v_ref, gains_ref, turned_ref):
    head, cols = gains_ref.shape[1], g_ref.shape[1]
    factor = head ** (-0.5)
    q_gain, k_gain = gains_ref[0:1], gains_ref[1:2]
    for h in range(cols // head):
        at, key_at = pl.ds(h * head, head), pl.ds(cols + h * head, head)
        query_normed, query_unit, query_spread = normalize(qk_ref[:, at], q_gain)
        key_normed, key_unit, key_spread = normalize(qk_ref[:, key_at], k_gain)
        query_bf, key_bf = query_normed.astype(BF), key_normed.astype(BF)
        attention = attention_of(query_bf, key_bf)
        grad_probs = dot_nt(v_ref[:, at], g_ref[:, at])
        delta = jnp.sum(attention * grad_probs, axis=0, keepdims=True)
        grad_scores = (attention * (grad_probs - delta) * factor).astype(BF)
        grad_kn = jnp.dot(grad_scores, query_bf, preferred_element_type=F32)
        grad_qn = dot_tn(grad_scores, key_bf)
        grad_query = normalize_back(grad_qn, query_unit, query_spread, q_gain)
        grad_key = normalize_back(grad_kn, key_unit, key_spread, k_gain)
        turned_ref[at, :] = grad_query.T.astype(BF)
        turned_ref[key_at, :] = grad_key.T.astype(BF)


def attention_call(kernel, arrays, gains, out_rows):
    tokens, columns = arrays[1].shape
    head = gains.shape[-1]
    pairs = (tokens // PATCH) * (columns // head)
    return pl.pallas_call(
        kernel,
        grid=(tokens // PATCH,),
        in_specs=[pl.BlockSpec((PATCH, array.shape[1]), lambda i: (i, 0)) for array in arrays]
        + [pl.BlockSpec(gains.shape, lambda i: (0, 0))],
        out_specs=pl.BlockSpec((out_rows, PATCH), lambda i: (0, i)),
        out_shape=jax.ShapeDtypeStruct((out_rows, tokens), BF),
        compiler_params=params(32),
        cost_estimate=pl.CostEstimate(
            flops=pairs * 8 * PATCH * PATCH * head,
            bytes_accessed=4 * len(arrays) * arrays[0].size,
            transcendentals=pairs * PATCH * PATCH,
        ),
    )(*arrays, gains)


def product_kernel(n_add, turn, turned_ref, *refs):
    turned = turned_ref[...]
    outs = refs[-2:]
    for side in range(2):
        total = jnp.dot(turned, refs[side][...], preferred_element_type=F32)
        for ref in refs[2 + side * n_add : 2 + (side + 1) * n_add]:
            total = total + ref[...].astype(F32)
        outs[side][...] = (total.T if turn else total).astype(BF)


def product_call(turned, normed, rows, units, addends=((), ()), turn=False):
    columns, tokens = turned.shape
    tile = 256 if rows % 256 == 0 else 128
    n_add, steps = len(addends[0]), rows // tile
    wide = pl.BlockSpec((columns, tile), lambda i: (0, i))
    tall = pl.BlockSpec((tile, columns), lambda i: (i, 0))

    def side(unit):
        return pl.BlockSpec((tokens, tile), lambda i: (0, unit * steps + i))

    shape = (rows, columns) if turn else (columns, rows)
    return pl.pallas_call(
        functools.partial(product_kernel, n_add, turn),
        grid=(steps,),
        in_specs=[pl.BlockSpec((columns, tokens), lambda i: (0, 0)), side(units[0]), side(units[1])]
        + [wide] * (2 * n_add),
        out_specs=[tall if turn else wide] * 2,
        out_shape=[jax.ShapeDtypeStruct(shape, BF)] * 2,
        compiler_params=params(24),
        cost_estimate=pl.CostEstimate(
            flops=4 * columns * tokens * rows,
            bytes_accessed=2 * (columns * tokens + 2 * tokens * rows + (2 + 2 * n_add) * columns * rows),
            transcendentals=0,
        ),
    )(turned, normed, normed, *addends[0], *addends[1])


def back_kernel(pair_ref, value_ref, w_pair_ref, w_value_ref, *refs):
    total = jnp.dot(w_pair_ref[...], pair_ref[...], preferred_element_type=F32)
    total = total + jnp.dot(w_value_ref[...], value_ref[...], preferred_element_type=F32)
    for ref in refs[:-1]:
        total = total + ref[...].astype(F32)
    refs[-1][...] = total.astype(refs[-1].dtype)


def back_call(pair, value, w_pair, w_value, rows, odd, addends, dtype):
    level_tokens = pair.shape[1]
    units = w_pair.shape[0] // rows // 2
    first = units if odd else 0
    block = pl.BlockSpec((rows, level_tokens), lambda i: (i, 0))
    return pl.pallas_call(
        back_kernel,
        grid=(units,),
        in_specs=[
            pl.BlockSpec(pair.shape, lambda i: (0, 0)),
            pl.BlockSpec(value.shape, lambda i: (0, 0)),
            pl.BlockSpec((rows, w_pair.shape[1]), lambda i: (first + i, 0)),
            pl.BlockSpec((rows, w_value.shape[1]), lambda i: (first + i, 0)),
        ]
        + [block] * len(addends),
        out_specs=block,
        out_shape=jax.ShapeDtypeStruct((units * rows, level_tokens), dtype),
        compiler_params=params(24),
        cost_estimate=pl.CostEstimate(
            flops=2 * units * rows * level_tokens * (pair.shape[0] + value.shape[0]),
            bytes_accessed=2 * units * rows * (pair.shape[0] + value.shape[0] + 3 * level_tokens),
            transcendentals=0,
        ),
    )(pair, value, w_pair, w_value, *addends)


def place_kernel(core_ref, mine_ref, other_ref, out_ref):
    here = pl.program_id(0) == core_ref[0]

    @pl.when(here)
    def _():
        out_ref[...] = mine_ref[...]

    @pl.when(jnp.logical_not(here))
    def _():
        out_ref[...] = other_ref[...]


def place_call(core, mine, other, cols, part):
    rows = mine.shape[0]
    block = pl.BlockSpec((rows, cols), lambda i, core_ref: (0, part))
    return pl.pallas_call(
        place_kernel,
        grid_spec=pltpu.PrefetchScalarGridSpec(
            num_scalar_prefetch=1,
            grid=(2,),
            in_specs=[block, block],
            out_specs=pl.BlockSpec((rows, cols), lambda i, core_ref: (0, i)),
        ),
        out_shape=jax.ShapeDtypeStruct((rows, 2 * cols), BF),
        compiler_params=params(16),
    )(core.reshape(1), mine, other)


def per_device(n_dp, n_mp, tokens, norm_gain, q_gain, k_gain, w_query, w_key, w_value, grad_heads):
    own, width = tokens.shape
    rows, cols = w_query.shape[0], w_query.shape[1] // 2
    n_chips = n_dp // 2
    group = n_mp * own
    place = lax.axis_index("dp")
    core = place & 1

    def swap(array, bit):
        return lax.ppermute(array, "dp", [(i, i ^ bit) for i in range(n_dp)])

    def half(array, which):
        return lax.dynamic_slice_in_dim(array, which * cols, cols, 1)

    def after(arrays, *others):
        flat, tree = jax.tree.flatten(arrays)
        done = lax.optimization_barrier((*flat, *jax.tree.leaves(others)))
        return jax.tree.unflatten(tree, done[: len(flat)])

    ring = list(range(0, n_mp, 2)) + list(range(n_mp - 1, 0, -2))
    level = lax.axis_index("mp")
    spot = jnp.where(level & 1 == 0, level >> 1, n_mp - 1 - (level >> 1))
    ring_pairs = [(ring[i], ring[(i + 1) % n_mp]) for i in range(n_mp)]

    def level_at(back):
        at = lax.rem(spot + 2 * n_mp - back, n_mp)
        return jnp.where(at < n_mp // 2, 2 * at, 2 * (n_mp - 1 - at) + 1)

    def ring_on(array):
        return lax.ppermute(array, "mp", ring_pairs)

    def unit_of(r):
        return (r & 1) * n_chips + (r >> 1)

    def feature_block(array, r):
        return lax.dynamic_slice_in_dim(array, (place ^ r) * rows, rows, 1)

    weights = (w_query, w_key, w_value)
    other_rows = swap(jnp.concatenate([half(w, 1 - core) for w in weights], axis=1), 1)
    own_rows = jnp.concatenate([half(w, core) for w in weights], axis=1)
    shard_pair, shard_value = (
        jnp.concatenate([own_rows[:, at], other_rows[:, at]], axis=0)
        for at in (slice(0, 2 * cols), slice(2 * cols, None))
    )

    def gather_start(shard):
        held = {0: shard}
        bit = 8
        while bit < n_dp:
            held.update({r ^ bit: swap(part, bit) for r, part in list(held.items())})
            bit *= 2
        for r, part in list(held.items()):
            held[r ^ 2] = swap(part, 2)
            held[r ^ 4] = swap(part, 4)
        return held

    def gather_rest(held):
        relays = {}
        for r in range(0, n_dp, 8):
            relays[r ^ 6] = swap(held[r ^ 2][:rows], 4)
            relays[r ^ 7] = swap(held[r ^ 4][rows:], 2)
        return relays

    def whole(held, relays):
        pieces = dict(relays)
        for r, part in held.items():
            pieces[r], pieces[r ^ 1] = part[:rows], part[rows:]
        return jnp.concatenate([pieces[r] for r in (*range(0, n_dp, 2), *range(1, n_dp, 2))], axis=0)

    held_pair = gather_start(shard_pair)

    normed_own, unit_rows, row_spread = normalize(tokens.astype(F32), norm_gain)
    normed_own = normed_own.astype(BF)
    even = jnp.concatenate([feature_block(normed_own, r) for r in range(0, n_dp, 2)], axis=1)
    odd = jnp.concatenate([feature_block(normed_own, r) for r in range(1, n_dp, 2)], axis=1)
    block = jnp.concatenate([even, swap(odd, 1)], axis=0)

    normed = blank((2 * group, width), BF)

    def put(normed, block, step):
        beside = swap(block, 1)
        start = level_at(step) * own
        mine, other = core * group + start, (1 - core) * group + start
        for piece, at, column in (
            (block[:own], mine, 0),
            (block[own:], other, 0),
            (beside[:own], other, width // 2),
            (beside[own:], mine, width // 2),
        ):
            normed = lax.dynamic_update_slice(normed, piece, (at, column))
        return normed

    normed = put(normed, block, 0)
    relays_pair = None
    for step in range(1, n_mp):
        block = ring_on(block)
        normed = put(normed, block, step)
        if step == 1:
            held_pair, normed = after((held_pair, normed))
            relays_pair = gather_rest(held_pair)
    held_value = gather_start(after(shard_value, relays_pair))

    grads_other = swap(half(grad_heads, 1 - core), 1)
    grad_out = blank((2 * group, cols), BF)
    grad_out = lax.dynamic_update_slice_in_dim(grad_out, half(grad_heads, core), core * group, 0)
    grad_out = lax.dynamic_update_slice_in_dim(grad_out, grads_other, (1 - core) * group, 0)
    gains = jnp.stack([q_gain, k_gain])

    full_pair = whole(held_pair, relays_pair)
    pair = jnp.dot(normed, full_pair, preferred_element_type=F32)
    turned_value = attention_call(first_kernel, (pair, grad_out), gains, cols)

    def products(turned, r, offsets, addends=((), ()), turn=False):
        return product_call(
            turned, normed, rows, [unit_of(r ^ f) for f in offsets], addends, turn
        )

    def scatter_far(turned):
        sent = {}
        for r in range(0, n_dp, 8):
            far_even, far_odd = products(turned, r, (6, 7))
            sent[r] = [swap(far_even, 2), swap(far_odd, 4)]
        return sent

    def scatter_early(turned):
        sent = {}
        for r in range(0, n_dp, 8):
            even_x, odd_y = products(turned, r, (2, 5))
            sent[r] = [swap(even_x, 2), swap(odd_y, 4)]
        return sent

    def scatter_late(turned, far):
        sent = {}
        for r in range(0, n_dp, 8):
            from_x, from_y = far[r]
            odd_x, even_y = products(turned, r, (3, 4), ((from_y,), (from_x,)))
            sent[r] = [swap(odd_x, 2), swap(even_y, 4)]
        return sent

    def scatter_end(turned, early, late):
        if n_dp == 8:
            (even_x, odd_y), (odd_x, even_y) = early[0], late[0]
            return products(turned, 0, (0, 1), ((even_x, even_y), (odd_x, odd_y)), True)
        totals = {}
        for r in range(0, n_dp, 8):
            (even_x, odd_y), (odd_x, even_y) = early[r], late[r]
            totals[r] = products(turned, r, (0, 1), ((even_x, even_y), (odd_x, odd_y)))
        bit = n_dp // 2
        while bit >= 8:
            for r in [r for r in totals if r < bit]:
                passed = [swap(total, bit) for total in totals.pop(r ^ bit)]
                totals[r] = [
                    (a.astype(F32) + b.astype(F32)).astype(BF) for a, b in zip(totals[r], passed)
                ]
            bit //= 2
        return [total.T for total in totals[0]]

    held_value, turned_value = after((held_value, turned_value))
    relays_value = gather_rest(held_value)
    far_value = scatter_far(turned_value)
    early_value = scatter_early(turned_value)
    full_value = whole(held_value, relays_value)
    values = jnp.dot(normed, full_value, preferred_element_type=F32).astype(BF)
    turned_pair = attention_call(rest_kernel, (pair, grad_out, values), gains, 2 * cols)

    turned_pair, turned_value, far_value = after((turned_pair, turned_value, far_value))
    late_value = scatter_late(turned_value, far_value)

    def back_odd(step):
        at = level_at(step + 1) * own
        chosen = [
            jnp.concatenate(
                [lax.dynamic_slice_in_dim(turned, g * group + at, own, 1) for g in range(2)], axis=1
            )
            for turned in (turned_pair, turned_value)
        ]
        sent = back_call(*chosen, full_pair, full_value, rows, True, (), BF)
        return chosen, swap(sent, 1)

    def back_even(chosen, passed, arrived, dtype):
        addends = (passed,) if arrived is None else (passed, arrived)
        return back_call(*chosen, full_pair, full_value, rows, False, addends, dtype)

    arrived = None
    for step in range(n_mp):
        last = step == n_mp - 1
        chosen, passed = back_odd(step)
        total = back_even(chosen, passed, arrived, F32 if last else BF)
        if not last:
            arrived = ring_on(total)
        if step == 0:
            far_pair = scatter_far(after(turned_pair, total))
            early_pair = scatter_early(turned_pair)
        elif step == 1:
            turned_late, far_pair = after((turned_pair, far_pair), total)
            late_pair = scatter_late(turned_late, far_pair)

    mine = lax.dynamic_slice_in_dim(total, core * own, own, 1)
    other = swap(lax.dynamic_slice_in_dim(total, (1 - core) * own, own, 1).astype(BF), 1).astype(F32)
    units = jnp.concatenate([mine, other], axis=0).T
    ordered = [
        lax.dynamic_slice_in_dim(units, unit_of(b ^ place) * rows, rows, 1) for b in range(n_dp)
    ]
    grad_normed = jnp.concatenate(ordered, axis=1)
    grad_tokens = normalize_back(grad_normed, unit_rows, row_spread, norm_gain).astype(BF)

    mine, other = scatter_end(turned_value, early_value, late_value)
    out_value = place_call(core, mine, swap(other, 1), cols, 0)
    mine, other = scatter_end(turned_pair, early_pair, late_pair)
    other = swap(other, 1)
    out_query, out_key = (place_call(core, mine, other, cols, part) for part in range(2))
    return (grad_tokens, out_query, out_key, out_value)


def solution(mesh):
    matrix = P("dp", "mp")
    token_rows = P(("dp", "mp"), None)
    return jax.shard_map(
        functools.partial(per_device, mesh.shape["dp"], mesh.shape["mp"]),
        mesh=mesh,
        in_specs=(token_rows, P(), P(), P(), matrix, matrix, matrix, matrix),
        out_specs=(token_rows, matrix, matrix, matrix),
        check_vma=False,
    )
```

```python
import functools

import jax
import jax.numpy as jnp
from jax import lax
from jax.experimental import pallas as pl
from jax.experimental.pallas import tpu as pltpu
from jax.sharding import PartitionSpec as P

PATCH = 256
BF = jnp.bfloat16
F32 = jnp.float32


def normalize(row_data, gain_vector):
    average = jnp.mean(row_data, axis=-1, keepdims=True)
    centred = row_data - average
    inv_spread = lax.rsqrt(jnp.mean(centred * centred, axis=-1, keepdims=True) + 1e-06)
    unit_data = centred * inv_spread
    return (unit_data * gain_vector, unit_data, inv_spread)


def normalize_back(grad_out, unit_data, inv_spread, gain_vector):
    scaled = grad_out * gain_vector
    inner_term = jnp.mean(scaled * unit_data, axis=-1, keepdims=True)
    return (scaled - jnp.mean(scaled, axis=-1, keepdims=True) - unit_data * inner_term) * inv_spread


def dot_nt(a, b):
    return lax.dot_general(a, b, (((1,), (1,)), ((), ())), preferred_element_type=F32)


def dot_tn(a, b):
    return lax.dot_general(a, b, (((0,), (0,)), ((), ())), preferred_element_type=F32)


def params(mib):
    return pltpu.CompilerParams(vmem_limit_bytes=mib * 2**20)


def blank(shape, dtype):
    return pl.pallas_call(
        lambda out_ref: None,
        out_shape=jax.ShapeDtypeStruct(shape, dtype),
        out_specs=pl.BlockSpec(memory_space=pl.ANY),
    )()


def attention_of(query_bf, key_bf):
    scores = dot_nt(key_bf, query_bf) * query_bf.shape[-1] ** (-0.5)
    raised = jnp.exp(scores - jnp.max(scores, axis=0, keepdims=True))
    return raised * (1.0 / jnp.sum(raised, axis=0, keepdims=True))


def first_kernel(qk_ref, g_ref, gains_ref, turned_ref):
    head, cols = gains_ref.shape[1], g_ref.shape[1]
    for h in range(cols // head):
        at, key_at = pl.ds(h * head, head), pl.ds(cols + h * head, head)
        query_bf = normalize(qk_ref[:, at], gains_ref[0:1])[0].astype(BF)
        key_bf = normalize(qk_ref[:, key_at], gains_ref[1:2])[0].astype(BF)
        attention = attention_of(query_bf, key_bf).astype(BF)
        grad_value = jnp.dot(attention, g_ref[:, at], preferred_element_type=F32)
        turned_ref[at, :] = grad_value.T.astype(BF)


def rest_kernel(qk_ref, g_ref, v_ref, gains_ref, turned_ref):
    head, cols = gains_ref.shape[1], g_ref.shape[1]
    factor = head ** (-0.5)
    q_gain, k_gain = gains_ref[0:1], gains_ref[1:2]
    for h in range(cols // head):
        at, key_at = pl.ds(h * head, head), pl.ds(cols + h * head, head)
        query_normed, query_unit, query_spread = normalize(qk_ref[:, at], q_gain)
        key_normed, key_unit, key_spread = normalize(qk_ref[:, key_at], k_gain)
        query_bf, key_bf = query_normed.astype(BF), key_normed.astype(BF)
        attention = attention_of(query_bf, key_bf)
        grad_probs = dot_nt(v_ref[:, at], g_ref[:, at])
        delta = jnp.sum(attention * grad_probs, axis=0, keepdims=True)
        grad_scores = (attention * (grad_probs - delta) * factor).astype(BF)
        grad_kn = jnp.dot(grad_scores, query_bf, preferred_element_type=F32)
        grad_qn = dot_tn(grad_scores, key_bf)
        grad_query = normalize_back(grad_qn, query_unit, query_spread, q_gain)
        grad_key = normalize_back(grad_kn, key_unit, key_spread, k_gain)
        turned_ref[at, :] = grad_query.T.astype(BF)
        turned_ref[key_at, :] = grad_key.T.astype(BF)


def attention_call(kernel, arrays, gains, out_rows):
    tokens, columns = arrays[1].shape
    head = gains.shape[-1]
    pairs = (tokens // PATCH) * (columns // head)
    return pl.pallas_call(
        kernel,
        grid=(tokens // PATCH,),
        in_specs=[pl.BlockSpec((PATCH, array.shape[1]), lambda i: (i, 0)) for array in arrays]
        + [pl.BlockSpec(gains.shape, lambda i: (0, 0))],
        out_specs=pl.BlockSpec((out_rows, PATCH), lambda i: (0, i)),
        out_shape=jax.ShapeDtypeStruct((out_rows, tokens), BF),
        compiler_params=params(32),
        cost_estimate=pl.CostEstimate(
            flops=pairs * 8 * PATCH * PATCH * head,
            bytes_accessed=4 * len(arrays) * arrays[0].size,
            transcendentals=pairs * PATCH * PATCH,
        ),
    )(*arrays, gains)


def product_kernel(n_add, turn, turned_ref, *refs):
    turned = turned_ref[...]
    outs = refs[-2:]
    for side in range(2):
        total = jnp.dot(turned, refs[side][...], preferred_element_type=F32)
        for ref in refs[2 + side * n_add : 2 + (side + 1) * n_add]:
            total = total + ref[...].astype(F32)
        outs[side][...] = (total.T if turn else total).astype(BF)


def product_call(turned, normed, rows, units, addends=((), ()), turn=False):
    columns, tokens = turned.shape
    tile = 256 if rows % 256 == 0 else 128
    n_add, steps = len(addends[0]), rows // tile
    wide = pl.BlockSpec((columns, tile), lambda i: (0, i))
    tall = pl.BlockSpec((tile, columns), lambda i: (i, 0))

    def side(unit):
        return pl.BlockSpec((tokens, tile), lambda i: (0, unit * steps + i))

    shape = (rows, columns) if turn else (columns, rows)
    return pl.pallas_call(
        functools.partial(product_kernel, n_add, turn),
        grid=(steps,),
        in_specs=[pl.BlockSpec((columns, tokens), lambda i: (0, 0)), side(units[0]), side(units[1])]
        + [wide] * (2 * n_add),
        out_specs=[tall if turn else wide] * 2,
        out_shape=[jax.ShapeDtypeStruct(shape, BF)] * 2,
        compiler_params=params(24),
        cost_estimate=pl.CostEstimate(
            flops=4 * columns * tokens * rows,
            bytes_accessed=2 * (columns * tokens + 2 * tokens * rows + (2 + 2 * n_add) * columns * rows),
            transcendentals=0,
        ),
    )(turned, normed, normed, *addends[0], *addends[1])


def back_kernel(pair_ref, value_ref, w_pair_ref, w_value_ref, *refs):
    total = jnp.dot(w_pair_ref[...], pair_ref[...], preferred_element_type=F32)
    total = total + jnp.dot(w_value_ref[...], value_ref[...], preferred_element_type=F32)
    for ref in refs[:-1]:
        total = total + ref[...].astype(F32)
    refs[-1][...] = total.astype(refs[-1].dtype)


def back_call(pair, value, w_pair, w_value, rows, odd, addends, dtype):
    level_tokens = pair.shape[1]
    units = w_pair.shape[0] // rows // 2
    first = units if odd else 0
    block = pl.BlockSpec((rows, level_tokens), lambda i: (i, 0))
    return pl.pallas_call(
        back_kernel,
        grid=(units,),
        in_specs=[
            pl.BlockSpec(pair.shape, lambda i: (0, 0)),
            pl.BlockSpec(value.shape, lambda i: (0, 0)),
            pl.BlockSpec((rows, w_pair.shape[1]), lambda i: (first + i, 0)),
            pl.BlockSpec((rows, w_value.shape[1]), lambda i: (first + i, 0)),
        ]
        + [block] * len(addends),
        out_specs=block,
        out_shape=jax.ShapeDtypeStruct((units * rows, level_tokens), dtype),
        compiler_params=params(24),
        cost_estimate=pl.CostEstimate(
            flops=2 * units * rows * level_tokens * (pair.shape[0] + value.shape[0]),
            bytes_accessed=2 * units * rows * (pair.shape[0] + value.shape[0] + 3 * level_tokens),
            transcendentals=0,
        ),
    )(pair, value, w_pair, w_value, *addends)


def place_kernel(core_ref, mine_ref, other_ref, out_ref):
    here = pl.program_id(0) == core_ref[0]

    @pl.when(here)
    def _():
        out_ref[...] = mine_ref[...]

    @pl.when(jnp.logical_not(here))
    def _():
        out_ref[...] = other_ref[...]


def place_call(core, mine, other, cols, part):
    rows = mine.shape[0]
    block = pl.BlockSpec((rows, cols), lambda i, core_ref: (0, part))
    return pl.pallas_call(
        place_kernel,
        grid_spec=pltpu.PrefetchScalarGridSpec(
            num_scalar_prefetch=1,
            grid=(2,),
            in_specs=[block, block],
            out_specs=pl.BlockSpec((rows, cols), lambda i, core_ref: (0, i)),
        ),
        out_shape=jax.ShapeDtypeStruct((rows, 2 * cols), BF),
        compiler_params=params(16),
    )(core.reshape(1), mine, other)


def finish_kernel(rows, n_dp, place_ref, mine_ref, other_ref, unit_ref, spread_ref, gain_ref, out_ref, held):
    n_chips = n_dp // 2
    held[: n_chips * rows] = mine_ref[...]
    held[n_chips * rows :] = other_ref[...].astype(F32)
    place = place_ref[0]
    columns = []
    total, inner = 0.0, 0.0
    for b in range(n_dp):
        r = b ^ place
        unit = (r & 1) * n_chips + (r >> 1)
        at = pl.ds(b * rows, rows)
        grad = held[pl.ds(pl.multiple_of(unit * rows, rows), rows), :].T
        scaled = grad * gain_ref[:, at]
        total = total + jnp.sum(scaled, axis=-1, keepdims=True)
        inner = inner + jnp.sum(scaled * unit_ref[:, at], axis=-1, keepdims=True)
        columns.append(scaled)
    average, inner = total * (1.0 / (n_dp * rows)), inner * (1.0 / (n_dp * rows))
    for b in range(n_dp):
        at = pl.ds(b * rows, rows)
        result = (columns[b] - average - unit_ref[:, at] * inner) * spread_ref[...]
        out_ref[:, at] = result.astype(BF)


def finish_call(place, mine, other, unit_rows, row_spread, norm_gain, rows):
    own, width = unit_rows.shape
    vmem = pl.BlockSpec(memory_space=pltpu.VMEM)
    return pl.pallas_call(
        functools.partial(finish_kernel, rows, width // rows),
        in_specs=[pl.BlockSpec(memory_space=pltpu.SMEM)] + [vmem] * 5,
        out_specs=vmem,
        out_shape=jax.ShapeDtypeStruct((own, width), BF),
        scratch_shapes=[pltpu.VMEM((width, own), F32)],
        compiler_params=params(32),
    )(place.reshape(1), mine, other, unit_rows, row_spread, norm_gain.reshape(1, width))


def per_device(n_dp, n_mp, tokens, norm_gain, q_gain, k_gain, w_query, w_key, w_value, grad_heads):
    own, width = tokens.shape
    rows, cols = w_query.shape[0], w_query.shape[1] // 2
    n_chips = n_dp // 2
    group = n_mp * own
    place = lax.axis_index("dp")
    core = place & 1

    def swap(array, bit):
        return lax.ppermute(array, "dp", [(i, i ^ bit) for i in range(n_dp)])

    def half(array, which):
        return lax.dynamic_slice_in_dim(array, which * cols, cols, 1)

    def after(arrays, *others):
        flat, tree = jax.tree.flatten(arrays)
        done = lax.optimization_barrier((*flat, *jax.tree.leaves(others)))
        return jax.tree.unflatten(tree, done[: len(flat)])

    ring = list(range(0, n_mp, 2)) + list(range(n_mp - 1, 0, -2))
    level = lax.axis_index("mp")
    spot = jnp.where(level & 1 == 0, level >> 1, n_mp - 1 - (level >> 1))
    ring_pairs = [(ring[i], ring[(i + 1) % n_mp]) for i in range(n_mp)]

    def level_at(back):
        at = lax.rem(spot + 2 * n_mp - back, n_mp)
        return jnp.where(at < n_mp // 2, 2 * at, 2 * (n_mp - 1 - at) + 1)

    def ring_on(array):
        return lax.ppermute(array, "mp", ring_pairs)

    def unit_of(r):
        return (r & 1) * n_chips + (r >> 1)

    def feature_block(array, r):
        return lax.dynamic_slice_in_dim(array, (place ^ r) * rows, rows, 1)

    def columns_of(weights, which):
        return jnp.concatenate([half(w, which) for w in weights], axis=1)

    def gather_start(held):
        held = dict(held)
        bit = 8
        while bit < n_dp:
            held.update({r ^ bit: swap(part, bit) for r, part in list(held.items())})
            bit *= 2
        for r, part in list(held.items()):
            held[r ^ 2] = swap(part, 2)
            held[r ^ 4] = swap(part, 4)
        return held

    def gather_rest(held):
        held = dict(held)
        for r in range(0, n_dp, 8):
            held[r ^ 6] = swap(held[r ^ 2], 4)
            held[r ^ 7] = swap(held[r ^ 5], 2)
        return held

    def whole(held):
        return jnp.concatenate([held[r] for r in (*range(0, n_dp, 2), *range(1, n_dp, 2))], axis=0)

    pair_weights = (w_query, w_key)
    own_pair, sent_pair = columns_of(pair_weights, core), columns_of(pair_weights, 1 - core)
    held_pair = gather_start({0: own_pair})
    other_pair = swap(sent_pair, 1)

    tokens = after(tokens, own_pair, sent_pair)
    normed_own, unit_rows, row_spread = normalize(tokens.astype(F32), norm_gain)
    normed_own = normed_own.astype(BF)
    even = jnp.concatenate([feature_block(normed_own, r) for r in range(0, n_dp, 2)], axis=1)
    odd = jnp.concatenate([feature_block(normed_own, r) for r in range(1, n_dp, 2)], axis=1)
    block = jnp.concatenate([even, swap(odd, 1)], axis=0)
    held_pair.update(gather_start({1: other_pair}))

    normed = blank((2 * group, width), BF)

    def put(normed, block, step):
        beside = swap(block, 1)
        start = level_at(step) * own
        mine, other = core * group + start, (1 - core) * group + start
        for piece, at, column in (
            (block[:own], mine, 0),
            (block[own:], other, 0),
            (beside[:own], other, width // 2),
            (beside[own:], mine, width // 2),
        ):
            normed = lax.dynamic_update_slice(normed, piece, (at, column))
        return normed

    normed = put(normed, block, 0)
    for step in range(1, n_mp):
        block = ring_on(block)
        normed = put(normed, block, step)
        if step == 1:
            held_pair, normed, w_value, grad_heads = after((held_pair, normed, w_value, grad_heads))
            held_pair = gather_rest(held_pair)
            shard_value = [half(w_value, core), swap(half(w_value, 1 - core), 1)]
            shard_value = jnp.concatenate(shard_value, axis=0)
            grads_mine, grads_other = half(grad_heads, core), swap(half(grad_heads, 1 - core), 1)
        elif step == 2:
            shard_value, normed = after((shard_value, normed))
            held_value = gather_start({0: shard_value})

    grad_out = blank((2 * group, cols), BF)
    grad_out = lax.dynamic_update_slice_in_dim(grad_out, grads_mine, core * group, 0)
    grad_out = lax.dynamic_update_slice_in_dim(grad_out, grads_other, (1 - core) * group, 0)
    gains = jnp.stack([q_gain, k_gain])

    full_pair = whole(held_pair)
    pair = jnp.dot(normed, full_pair, preferred_element_type=F32)
    turned_value = attention_call(first_kernel, (pair, grad_out), gains, cols)

    def products(turned, r, offsets, addends=((), ()), turn=False):
        return product_call(
            turned, normed, rows, [unit_of(r ^ f) for f in offsets], addends, turn
        )

    blocks_of_four = range(0, n_dp, 8)

    def far_messages(turned):
        return [products(turned, r, (6, 7)) for r in blocks_of_four]

    def early_messages(turned):
        return [products(turned, r, (2, 5)) for r in blocks_of_four]

    def late_messages(turned, far):
        return [
            products(turned, r, (3, 4), ((from_y,), (from_x,)))
            for r, (from_x, from_y) in zip(blocks_of_four, far)
        ]

    def send(messages):
        return [[swap(to_x, 2), swap(to_y, 4)] for to_x, to_y in messages]

    def scatter_end(turned, early, late):
        if n_dp == 8:
            (even_x, odd_y), (odd_x, even_y) = early[0], late[0]
            return products(turned, 0, (0, 1), ((even_x, even_y), (odd_x, odd_y)), True)
        totals = {}
        for r in range(0, n_dp, 8):
            (even_x, odd_y), (odd_x, even_y) = early[r // 8], late[r // 8]
            totals[r] = products(turned, r, (0, 1), ((even_x, even_y), (odd_x, odd_y)))
        bit = n_dp // 2
        while bit >= 8:
            for r in [r for r in totals if r < bit]:
                passed = [swap(total, bit) for total in totals.pop(r ^ bit)]
                totals[r] = [
                    (a.astype(F32) + b.astype(F32)).astype(BF) for a, b in zip(totals[r], passed)
                ]
            bit //= 2
        return [total.T for total in totals[0]]

    far_value, early_value = far_messages(turned_value), early_messages(turned_value)
    held_value, far_value, early_value = after((held_value, far_value, early_value))
    held_value = {r ^ f: held_value[r][f * rows : (f + 1) * rows] for r in held_value for f in (0, 1)}
    held_value, far_value = after((held_value, far_value))
    held_value = gather_rest(held_value)
    far_value = send(far_value)
    held_value, early_value = after((held_value, early_value))
    early_value = send(early_value)
    full_value = whole(held_value)
    values = jnp.dot(normed, full_value, preferred_element_type=F32).astype(BF)
    turned_pair = attention_call(rest_kernel, (pair, grad_out, values), gains, 2 * cols)

    turned_value, turned_pair, far_value = after((turned_value, turned_pair, far_value))
    late_value = late_messages(turned_value, far_value)
    turned_value, turned_pair, late_value = after((turned_value, turned_pair, late_value))
    late_value = send(late_value)

    def back_odd(step, gate):
        at = level_at(step + 1) * own
        chosen = [
            jnp.concatenate(
                [lax.dynamic_slice_in_dim(turned, g * group + at, own, 1) for g in range(2)], axis=1
            )
            for turned in after((turned_pair, turned_value), gate)
        ]
        sent = back_call(*chosen, full_pair, full_value, rows, True, (), BF)
        return chosen, sent, swap(sent, 1)

    gate, arrived = [], None
    for step in range(n_mp):
        last = step == n_mp - 1
        if last:
            early_pair, gate = after((early_pair, gate))
        chosen, sent, passed = back_odd(step, gate)
        if step == 0:
            far_pair = far_messages(after(turned_pair, sent))
            chosen, far_pair, early_value = after((chosen, far_pair, early_value))
        elif step == 1:
            turned_early, late_value = after((turned_pair, late_value), sent)
            early_pair = early_messages(turned_early)
            chosen, early_pair = after((chosen, early_pair))
        elif step == 2:
            late_pair = late_messages(after(turned_pair, sent), far_pair)
            chosen, late_pair = after((chosen, late_pair))
            late_pair = send(late_pair)
            chosen, ends_value = after((chosen, scatter_end(turned_value, early_value, late_value)))
            passed_value = swap(ends_value[1], 1)
        total = back_call(
            *chosen, full_pair, full_value, rows, False, (passed,), F32 if last else BF
        )
        if last:
            ends_pair = scatter_end(after(turned_pair, total), early_pair, late_pair)
            total, ends_pair = after((total, ends_pair))
        if arrived is not None:
            total = total.astype(F32) + arrived.astype(F32)
        if not last:
            total = total.astype(BF)
            arrived = ring_on(total)
        gate = total
        if step == 0:
            far_pair, gate = after((far_pair, total))
            far_pair = send(far_pair)
        elif step == 1:
            early_pair, gate = after((early_pair, total))
            early_pair = send(early_pair)

    passed_pair = swap(ends_pair[1], 1)
    mine = lax.dynamic_slice_in_dim(total, core * own, own, 1)
    other = swap(lax.dynamic_slice_in_dim(total, (1 - core) * own, own, 1).astype(BF), 1)
    out_value = place_call(core, ends_value[0], passed_value, cols, 0)
    out_query, out_key = (
        place_call(core, ends_pair[0], passed_pair, cols, part) for part in range(2)
    )
    grad_tokens = finish_call(place, mine, other, unit_rows, row_spread, norm_gain, rows)
    return (grad_tokens, out_query, out_key, out_value)


def solution(mesh):
    matrix = P("dp", "mp")
    token_rows = P(("dp", "mp"), None)
    return jax.shard_map(
        functools.partial(per_device, mesh.shape["dp"], mesh.shape["mp"]),
        mesh=mesh,
        in_specs=(token_rows, P(), P(), P(), matrix, matrix, matrix, matrix),
        out_specs=(token_rows, matrix, matrix, matrix),
        check_vma=False,
    )
```

```python
import functools

import jax
import jax.numpy as jnp
from jax import lax
from jax.experimental import pallas as pl
from jax.experimental.pallas import tpu as pltpu
from jax.sharding import PartitionSpec as P

PATCH = 256
BF = jnp.bfloat16
F32 = jnp.float32


def normalize(row_data, gain_vector):
    average = jnp.mean(row_data, axis=-1, keepdims=True)
    centred = row_data - average
    inv_spread = lax.rsqrt(jnp.mean(centred * centred, axis=-1, keepdims=True) + 1e-06)
    unit_data = centred * inv_spread
    return (unit_data * gain_vector, unit_data, inv_spread)


def normalize_back(grad_out, unit_data, inv_spread, gain_vector):
    scaled = grad_out * gain_vector
    inner_term = jnp.mean(scaled * unit_data, axis=-1, keepdims=True)
    return (scaled - jnp.mean(scaled, axis=-1, keepdims=True) - unit_data * inner_term) * inv_spread


def dot_nt(a, b):
    return lax.dot_general(a, b, (((1,), (1,)), ((), ())), preferred_element_type=F32)


def dot_tn(a, b):
    return lax.dot_general(a, b, (((0,), (0,)), ((), ())), preferred_element_type=F32)


def params(mib):
    return pltpu.CompilerParams(vmem_limit_bytes=mib * 2**20)


def cost(flops, bytes_accessed):
    return pl.CostEstimate(flops=flops, bytes_accessed=bytes_accessed, transcendentals=0)


def blank(shape, dtype):
    return pl.pallas_call(
        lambda out_ref: None,
        out_shape=jax.ShapeDtypeStruct(shape, dtype),
        out_specs=pl.BlockSpec(memory_space=pl.ANY),
    )()


def attention_of(query_bf, key_bf):
    scores = dot_nt(key_bf, query_bf) * query_bf.shape[-1] ** (-0.5)
    raised = jnp.exp(scores - jnp.max(scores, axis=0, keepdims=True))
    return raised * (1.0 / jnp.sum(raised, axis=0, keepdims=True))


def first_kernel(qk_ref, g_ref, gains_ref, turned_ref):
    head, cols = gains_ref.shape[1], g_ref.shape[1]
    for h in range(cols // head):
        at, key_at = pl.ds(h * head, head), pl.ds(cols + h * head, head)
        query_bf = normalize(qk_ref[:, at], gains_ref[0:1])[0].astype(BF)
        key_bf = normalize(qk_ref[:, key_at], gains_ref[1:2])[0].astype(BF)
        attention = attention_of(query_bf, key_bf).astype(BF)
        grad_value = jnp.dot(attention, g_ref[:, at], preferred_element_type=F32)
        turned_ref[at, :] = grad_value.T.astype(BF)


def rest_kernel(qk_ref, g_ref, v_ref, gains_ref, turned_ref):
    head, cols = gains_ref.shape[1], g_ref.shape[1]
    factor = head ** (-0.5)
    q_gain, k_gain = gains_ref[0:1], gains_ref[1:2]
    for h in range(cols // head):
        at, key_at = pl.ds(h * head, head), pl.ds(cols + h * head, head)
        query_normed, query_unit, query_spread = normalize(qk_ref[:, at], q_gain)
        key_normed, key_unit, key_spread = normalize(qk_ref[:, key_at], k_gain)
        query_bf, key_bf = query_normed.astype(BF), key_normed.astype(BF)
        attention = attention_of(query_bf, key_bf)
        grad_probs = dot_nt(v_ref[:, at], g_ref[:, at])
        delta = jnp.sum(attention * grad_probs, axis=0, keepdims=True)
        grad_scores = (attention * (grad_probs - delta) * factor).astype(BF)
        grad_kn = jnp.dot(grad_scores, query_bf, preferred_element_type=F32)
        grad_qn = dot_tn(grad_scores, key_bf)
        grad_query = normalize_back(grad_qn, query_unit, query_spread, q_gain)
        grad_key = normalize_back(grad_kn, key_unit, key_spread, k_gain)
        turned_ref[at, :] = grad_query.T.astype(BF)
        turned_ref[key_at, :] = grad_key.T.astype(BF)


def attention_call(kernel, arrays, gains, out_rows):
    tokens, columns = arrays[1].shape
    head = gains.shape[-1]
    pairs = (tokens // PATCH) * (columns // head)
    return pl.pallas_call(
        kernel,
        grid=(tokens // PATCH,),
        in_specs=[pl.BlockSpec((PATCH, array.shape[1]), lambda i: (i, 0)) for array in arrays]
        + [pl.BlockSpec(gains.shape, lambda i: (0, 0))],
        out_specs=pl.BlockSpec((out_rows, PATCH), lambda i: (0, i)),
        out_shape=jax.ShapeDtypeStruct((out_rows, tokens), BF),
        compiler_params=params(32),
        cost_estimate=cost(pairs * 8 * PATCH * PATCH * head, 4 * len(arrays) * arrays[0].size),
    )(*arrays, gains)


def product_kernel(n_add, turn, turned_ref, *refs):
    turned = turned_ref[...]
    outs = refs[-2:]
    for side in range(2):
        total = jnp.dot(turned, refs[side][...], preferred_element_type=F32)
        for ref in refs[2 + side * n_add : 2 + (side + 1) * n_add]:
            total = total + ref[...].astype(F32)
        outs[side][...] = (total.T if turn else total).astype(BF)


def product_call(turned, normed, rows, units, addends=((), ()), turn=False):
    columns, tokens = turned.shape
    tile = 256 if rows % 256 == 0 else 128
    count, n_add, steps = len(units[0]), len(addends[0]), rows // tile

    def side(first, last):
        return pl.BlockSpec((tokens, tile), lambda u, i: (0, (first + u * (last - first)) * steps + i))

    def added(which):
        return pl.BlockSpec((columns, tile), lambda u, i: (which, i))

    if turn:
        shape, out = (rows, columns), pl.BlockSpec((tile, columns), lambda u, i: (i, 0))
    else:
        shape, out = (count * columns, rows), pl.BlockSpec((columns, tile), lambda u, i: (u, i))
    addends = [*addends[0], *addends[1]]
    return pl.pallas_call(
        functools.partial(product_kernel, n_add, turn),
        grid=(count, steps),
        in_specs=[
            pl.BlockSpec((columns, tokens), lambda u, i: (0, 0)),
            *[side(chosen[0], chosen[-1]) for chosen in units],
            *[added(which) for _, which in addends],
        ],
        out_specs=[out] * 2,
        out_shape=[jax.ShapeDtypeStruct(shape, BF)] * 2,
        compiler_params=params(24),
        cost_estimate=cost(
            4 * count * columns * tokens * rows,
            2 * columns * tokens + 4 * count * tokens * rows + (4 + 4 * n_add) * columns * rows,
        ),
    )(turned, normed, normed, *[array for array, _ in addends])


def back_kernel(pair_ref, value_ref, w_pair_ref, w_value_ref, *refs):
    total = jnp.dot(w_pair_ref[...], pair_ref[...], preferred_element_type=F32)
    total = total + jnp.dot(w_value_ref[...], value_ref[...], preferred_element_type=F32)
    for ref in refs[:-1]:
        total = total + ref[...].astype(F32)
    refs[-1][...] = total.astype(refs[-1].dtype)


def back_call(pair, value, w_pair, w_value, rows, odd, addends, dtype):
    level_tokens = pair.shape[1]
    units = w_pair.shape[0] // rows // 2
    first = units if odd else 0
    block = pl.BlockSpec((rows, level_tokens), lambda i: (i, 0))
    return pl.pallas_call(
        back_kernel,
        grid=(units,),
        in_specs=[
            pl.BlockSpec(pair.shape, lambda i: (0, 0)),
            pl.BlockSpec(value.shape, lambda i: (0, 0)),
            pl.BlockSpec((rows, w_pair.shape[1]), lambda i: (first + i, 0)),
            pl.BlockSpec((rows, w_value.shape[1]), lambda i: (first + i, 0)),
        ]
        + [block] * len(addends),
        out_specs=block,
        out_shape=jax.ShapeDtypeStruct((units * rows, level_tokens), dtype),
        compiler_params=params(24),
        cost_estimate=cost(
            2 * units * rows * level_tokens * (pair.shape[0] + value.shape[0]),
            2 * units * rows * (pair.shape[0] + value.shape[0] + 3 * level_tokens),
        ),
    )(pair, value, w_pair, w_value, *addends)


def place_kernel(core_ref, mine_ref, other_ref, out_ref):
    here = pl.program_id(0) == core_ref[0]

    @pl.when(here)
    def _():
        out_ref[...] = mine_ref[...]

    @pl.when(jnp.logical_not(here))
    def _():
        out_ref[...] = other_ref[...]


def place_call(core, mine, other, cols, part):
    rows = mine.shape[0]
    block = pl.BlockSpec((rows, cols), lambda i, core_ref: (0, part))
    return pl.pallas_call(
        place_kernel,
        grid_spec=pltpu.PrefetchScalarGridSpec(
            num_scalar_prefetch=1,
            grid=(2,),
            in_specs=[block, block],
            out_specs=pl.BlockSpec((rows, cols), lambda i, core_ref: (0, i)),
        ),
        out_shape=jax.ShapeDtypeStruct((rows, 2 * cols), BF),
        compiler_params=params(16),
    )(core.reshape(1), mine, other)


def finish_kernel(rows, n_dp, place_ref, mine_ref, other_ref, unit_ref, spread_ref, gain_ref, out_ref, held):
    n_chips = n_dp // 2
    held[: n_chips * rows] = mine_ref[...]
    held[n_chips * rows :] = other_ref[...].astype(F32)
    place = place_ref[0]
    columns = []
    total, inner = 0.0, 0.0
    for b in range(n_dp):
        r = b ^ place
        unit = (r & 1) * n_chips + (r >> 1)
        at = pl.ds(b * rows, rows)
        grad = held[pl.ds(pl.multiple_of(unit * rows, rows), rows), :].T
        scaled = grad * gain_ref[:, at]
        total = total + jnp.sum(scaled, axis=-1, keepdims=True)
        inner = inner + jnp.sum(scaled * unit_ref[:, at], axis=-1, keepdims=True)
        columns.append(scaled)
    average, inner = total * (1.0 / (n_dp * rows)), inner * (1.0 / (n_dp * rows))
    for b in range(n_dp):
        at = pl.ds(b * rows, rows)
        result = (columns[b] - average - unit_ref[:, at] * inner) * spread_ref[...]
        out_ref[:, at] = result.astype(BF)


def finish_call(place, mine, other, unit_rows, row_spread, norm_gain, rows):
    own, width = unit_rows.shape
    vmem = pl.BlockSpec(memory_space=pltpu.VMEM)
    return pl.pallas_call(
        functools.partial(finish_kernel, rows, width // rows),
        in_specs=[pl.BlockSpec(memory_space=pltpu.SMEM)] + [vmem] * 5,
        out_specs=vmem,
        out_shape=jax.ShapeDtypeStruct((own, width), BF),
        scratch_shapes=[pltpu.VMEM((width, own), F32)],
        compiler_params=params(32),
    )(place.reshape(1), mine, other, unit_rows, row_spread, norm_gain.reshape(1, width))


def per_device(n_dp, n_mp, tokens, norm_gain, q_gain, k_gain, w_query, w_key, w_value, grad_heads):
    own, width = tokens.shape
    rows, cols = w_query.shape[0], w_query.shape[1] // 2
    n_chips = n_dp // 2
    group = n_mp * own
    place = lax.axis_index("dp")
    core = place & 1

    def swap(array, bit):
        return lax.ppermute(array, "dp", [(i, i ^ bit) for i in range(n_dp)])

    def half(array, which):
        return lax.dynamic_slice_in_dim(array, which * cols, cols, 1)

    def together(*arrays):
        return lax.optimization_barrier(arrays)

    ring = list(range(0, n_mp, 2)) + list(range(n_mp - 1, 0, -2))
    level = lax.axis_index("mp")
    spot = jnp.where(level & 1 == 0, level >> 1, n_mp - 1 - (level >> 1))
    ring_pairs = [(ring[i], ring[(i + 1) % n_mp]) for i in range(n_mp)]

    def level_at(back):
        at = lax.rem(spot + 2 * n_mp - back, n_mp)
        return jnp.where(at < n_mp // 2, 2 * at, 2 * (n_mp - 1 - at) + 1)

    def ring_on(array):
        return lax.ppermute(array, "mp", ring_pairs)

    def unit_of(r):
        return (r & 1) * n_chips + (r >> 1)

    def feature_block(array, r):
        return lax.dynamic_slice_in_dim(array, (place ^ r) * rows, rows, 1)

    def columns_of(weights, which):
        return jnp.concatenate([half(w, which) for w in weights], axis=1)

    def gather_start(held):
        held = dict(held)
        bit = 8
        while bit < n_dp:
            held.update({r ^ bit: swap(part, bit) for r, part in list(held.items())})
            bit *= 2
        for r, part in list(held.items()):
            held[r ^ 2] = swap(part, 2)
            held[r ^ 4] = swap(part, 4)
        return held

    def gather_rest(held):
        held = dict(held)
        for r in range(0, n_dp, 8):
            held[r ^ 6] = swap(held[r ^ 2], 4)
            held[r ^ 7] = swap(held[r ^ 5], 2)
        return held

    def whole(held):
        return jnp.concatenate([held[r] for r in (*range(0, n_dp, 2), *range(1, n_dp, 2))], axis=0)

    pair_weights = (w_query, w_key)
    own_pair, sent_pair = columns_of(pair_weights, core), columns_of(pair_weights, 1 - core)
    tokens, own_pair, sent_pair = together(tokens, own_pair, sent_pair)
    held_pair = gather_start({0: own_pair})
    other_pair = swap(sent_pair, 1)

    normed_own, unit_rows, row_spread = normalize(tokens.astype(F32), norm_gain)
    normed_own = normed_own.astype(BF)
    even = jnp.concatenate([feature_block(normed_own, r) for r in range(0, n_dp, 2)], axis=1)
    odd = jnp.concatenate([feature_block(normed_own, r) for r in range(1, n_dp, 2)], axis=1)
    block = jnp.concatenate([even, swap(odd, 1)], axis=0)

    normed = blank((2 * group, width), BF)

    def put(normed, block, step):
        beside = swap(block, 1)
        start = level_at(step) * own
        mine, other = core * group + start, (1 - core) * group + start
        for piece, at, column in (
            (block[:own], mine, 0),
            (block[own:], other, 0),
            (beside[:own], other, width // 2),
            (beside[own:], mine, width // 2),
        ):
            normed = lax.dynamic_update_slice(normed, piece, (at, column))
        return normed

    held_pair, normed = together(held_pair, normed)
    held_pair.update(gather_start({1: other_pair}))
    normed = put(normed, block, 0)
    for step in range(1, n_mp):
        block = ring_on(block)
        normed = put(normed, block, step)
        if step == 1:
            held_pair, normed, w_value, grad_heads = together(held_pair, normed, w_value, grad_heads)
            held_pair = gather_rest(held_pair)
            shard_value = [half(w_value, core), swap(half(w_value, 1 - core), 1)]
            shard_value = jnp.concatenate(shard_value, axis=0)
            grads_mine, grads_other = half(grad_heads, core), swap(half(grad_heads, 1 - core), 1)
        elif step == 2:
            shard_value, normed = together(shard_value, normed)
            held_value = gather_start({0: shard_value})

    grad_out = blank((2 * group, cols), BF)
    grad_out = lax.dynamic_update_slice_in_dim(grad_out, grads_mine, core * group, 0)
    grad_out = lax.dynamic_update_slice_in_dim(grad_out, grads_other, (1 - core) * group, 0)
    gains = jnp.stack([q_gain, k_gain])

    full_pair = whole(held_pair)
    pair = jnp.dot(normed, full_pair, preferred_element_type=F32)
    turned_value = attention_call(first_kernel, (pair, grad_out), gains, cols)

    def products(turned, r, offsets, addends=((), ()), turn=False):
        units = [[unit_of(r ^ f) for f in side] for side in offsets]
        return product_call(turned, normed, rows, units, addends, turn)

    blocks_of_four = range(0, n_dp, 8)

    def messages(turned, to_x, to_y):
        return [products(turned, r, (to_x, to_y)) for r in blocks_of_four]

    def late_messages(turned, far):
        return [
            products(turned, r, ((3,), (4,)), (((from_y, 0),), ((from_x, 0),)))
            for r, (from_x, from_y) in zip(blocks_of_four, far)
        ]

    def send(messages):
        return [[swap(to_x, 2), swap(to_y, 4)] for to_x, to_y in messages]

    def scatter_end(turned, early, unit, late):
        def own(r, turn):
            (early_x, early_y), (late_x, late_y) = early[r // 8], late[r // 8]
            addends = (((early_x, unit), (late_y, 0)), ((early_y, unit), (late_x, 0)))
            return products(turned, r, ((0,), (1,)), addends, turn)

        if n_dp == 8:
            return own(0, True)
        totals = {r: own(r, False) for r in blocks_of_four}
        bit = n_dp // 2
        while bit >= 8:
            for r in [r for r in totals if r < bit]:
                passed = [swap(total, bit) for total in totals.pop(r ^ bit)]
                totals[r] = [
                    (a.astype(F32) + b.astype(F32)).astype(BF) for a, b in zip(totals[r], passed)
                ]
            bit //= 2
        return [total.T for total in totals[0]]

    held_value, turned_value = together(held_value, turned_value)
    pieces = {r ^ f: part[f * rows : (f + 1) * rows] for r, part in held_value.items() for f in (0, 1)}
    relayed = [r ^ f for r in blocks_of_four for f in (2, 5)]
    pieces.update(zip(relayed, together(*[pieces[r] for r in relayed])))
    held_value = gather_rest(pieces)
    first_value = send(messages(turned_value, (6, 2), (7, 5)))
    full_value = whole(held_value)
    values = jnp.dot(normed, full_value, preferred_element_type=F32).astype(BF)
    turned_pair = attention_call(rest_kernel, (pair, grad_out, values), gains, 2 * cols)

    def back_odd(step, turned_pair, turned_value):
        at = level_at(step + 1) * own
        chosen = [
            jnp.concatenate(
                [lax.dynamic_slice_in_dim(turned, g * group + at, own, 1) for g in range(2)], axis=1
            )
            for turned in (turned_pair, turned_value)
        ]
        return chosen, back_call(*chosen, full_pair, full_value, rows, True, (), BF)

    def back_even(chosen, passed, dtype):
        return back_call(*chosen, full_pair, full_value, rows, False, (passed,), dtype)

    chosen, sent, partial = {}, {}, {}
    chosen[0], sent[0] = back_odd(0, turned_pair, turned_value)
    chosen[1], sent[1] = back_odd(1, turned_pair, turned_value)
    late_value = late_messages(turned_value, first_value)
    late_value, sent = together(late_value, sent)
    late_value = send(late_value)
    passed = {step: swap(sent[step], 1) for step in range(2)}
    far_pair = messages(turned_pair, (6,), (7,))
    far_pair, passed = together(far_pair, passed)
    message = back_even(chosen[0], passed[0], BF)
    message, far_pair, turned_pair, turned_value = together(message, far_pair, turned_pair, turned_value)
    arrived, far_pair = ring_on(message), send(far_pair)

    turned_pair, turned_value, late_value = together(turned_pair, turned_value, late_value)
    for step in range(2, 4):
        chosen[step], sent[step] = back_odd(step, turned_pair, turned_value)
    ends_value = scatter_end(turned_value, first_value, 1, late_value)
    partial[1] = back_even(chosen[1], passed[1], BF)
    early_pair = messages(turned_pair, (2,), (5,))
    for step in range(1, n_mp - 1):
        if step == 1:
            partial[1], early_pair, sent, far_pair, ends_value = together(
                partial[1], early_pair, sent, far_pair, ends_value
            )
        elif step == 2:
            partial[2], late_pair, early_pair = together(partial[2], late_pair, early_pair)
        message = (partial[step].astype(F32) + arrived.astype(F32)).astype(BF)
        if step == 1:
            message, early_pair, sent, turned_pair, turned_value = together(
                message, early_pair, sent, turned_pair, turned_value
            )
            early_pair = send(early_pair)
        elif step == 2:
            message, late_pair, ends_value = together(message, late_pair, ends_value)
            late_pair, passed_value = send(late_pair), swap(ends_value[1], 1)
        arrived = ring_on(message)
        if step + 2 < n_mp:
            near = [step + 1, step + 2] if step + 3 == n_mp else [step + 1]
            for level_step in near:
                passed[level_step] = swap(sent[level_step], 1)
            here = [passed[level_step] for level_step in near]
            turned_pair, turned_value, here = together(turned_pair, turned_value, here)
            passed.update(zip(near, here))
            for level_step in near:
                dtype = F32 if level_step == n_mp - 1 else BF
                partial[level_step] = back_even(chosen[level_step], passed[level_step], dtype)
            if step + 3 == n_mp:
                partial[n_mp - 2], partial[n_mp - 1] = together(partial[n_mp - 2], partial[n_mp - 1])
            else:
                chosen[step + 3], sent[step + 3] = back_odd(step + 3, turned_pair, turned_value)
            if step == 1:
                late_pair = late_messages(turned_pair, far_pair)
    total = partial[n_mp - 1] + arrived.astype(F32)

    mine = lax.dynamic_slice_in_dim(total, core * own, own, 1)
    other = lax.dynamic_slice_in_dim(total, (1 - core) * own, own, 1).astype(BF)
    mine, other, turned_pair = together(mine, other, turned_pair)
    other = swap(other, 1)
    ends_pair = scatter_end(turned_pair, early_pair, 0, late_pair)
    passed_pair = swap(ends_pair[1], 1)
    out_value = place_call(core, ends_value[0], passed_value, cols, 0)
    out_query, out_key = (
        place_call(core, ends_pair[0], passed_pair, cols, part) for part in range(2)
    )
    grad_tokens = finish_call(place, mine, other, unit_rows, row_spread, norm_gain, rows)
    return (grad_tokens, out_query, out_key, out_value)


def solution(mesh):
    matrix = P("dp", "mp")
    token_rows = P(("dp", "mp"), None)
    return jax.shard_map(
        functools.partial(per_device, mesh.shape["dp"], mesh.shape["mp"]),
        mesh=mesh,
        in_specs=(token_rows, P(), P(), P(), matrix, matrix, matrix, matrix),
        out_specs=(token_rows, matrix, matrix, matrix),
        check_vma=False,
    )
```

```python
import functools

import jax
import jax.numpy as jnp
from jax import lax
from jax.experimental import pallas as pl
from jax.experimental.pallas import tpu as pltpu
from jax.sharding import PartitionSpec as P

PATCH = 256
BF = jnp.bfloat16
F32 = jnp.float32


def normalize(row_data, gain_vector):
    average = jnp.mean(row_data, axis=-1, keepdims=True)
    centred = row_data - average
    inv_spread = lax.rsqrt(jnp.mean(centred * centred, axis=-1, keepdims=True) + 1e-06)
    unit_data = centred * inv_spread
    return (unit_data * gain_vector, unit_data, inv_spread)


def normalize_back(grad_out, unit_data, inv_spread, gain_vector):
    scaled = grad_out * gain_vector
    inner_term = jnp.mean(scaled * unit_data, axis=-1, keepdims=True)
    return (scaled - jnp.mean(scaled, axis=-1, keepdims=True) - unit_data * inner_term) * inv_spread


def dot_nt(a, b):
    return lax.dot_general(a, b, (((1,), (1,)), ((), ())), preferred_element_type=F32)


def dot_tn(a, b):
    return lax.dot_general(a, b, (((0,), (0,)), ((), ())), preferred_element_type=F32)


def params(mib):
    return pltpu.CompilerParams(vmem_limit_bytes=mib * 2**20)


def cost(flops, bytes_accessed):
    return pl.CostEstimate(flops=flops, bytes_accessed=bytes_accessed, transcendentals=0)


def blank(shape, dtype):
    return pl.pallas_call(
        lambda out_ref: None,
        out_shape=jax.ShapeDtypeStruct(shape, dtype),
        out_specs=pl.BlockSpec(memory_space=pl.ANY),
    )()


def attention_of(query_bf, key_bf):
    scores = dot_nt(key_bf, query_bf) * query_bf.shape[-1] ** (-0.5)
    raised = jnp.exp(scores - jnp.max(scores, axis=0, keepdims=True))
    return raised * (1.0 / jnp.sum(raised, axis=0, keepdims=True))


def first_kernel(qk_ref, g_ref, gains_ref, turned_ref):
    head, cols = gains_ref.shape[1], g_ref.shape[1]
    for h in range(cols // head):
        at, key_at = pl.ds(h * head, head), pl.ds(cols + h * head, head)
        query_bf = normalize(qk_ref[:, at], gains_ref[0:1])[0].astype(BF)
        key_bf = normalize(qk_ref[:, key_at], gains_ref[1:2])[0].astype(BF)
        attention = attention_of(query_bf, key_bf).astype(BF)
        grad_value = jnp.dot(attention, g_ref[:, at], preferred_element_type=F32)
        turned_ref[at, :] = grad_value.T.astype(BF)


def rest_kernel(qk_ref, g_ref, v_ref, gains_ref, turned_ref):
    head, cols = gains_ref.shape[1], g_ref.shape[1]
    factor = head ** (-0.5)
    q_gain, k_gain = gains_ref[0:1], gains_ref[1:2]
    for h in range(cols // head):
        at, key_at = pl.ds(h * head, head), pl.ds(cols + h * head, head)
        query_normed, query_unit, query_spread = normalize(qk_ref[:, at], q_gain)
        key_normed, key_unit, key_spread = normalize(qk_ref[:, key_at], k_gain)
        query_bf, key_bf = query_normed.astype(BF), key_normed.astype(BF)
        attention = attention_of(query_bf, key_bf)
        grad_probs = dot_nt(v_ref[:, at], g_ref[:, at])
        delta = jnp.sum(attention * grad_probs, axis=0, keepdims=True)
        grad_scores = (attention * (grad_probs - delta) * factor).astype(BF)
        grad_kn = jnp.dot(grad_scores, query_bf, preferred_element_type=F32)
        grad_qn = dot_tn(grad_scores, key_bf)
        grad_query = normalize_back(grad_qn, query_unit, query_spread, q_gain)
        grad_key = normalize_back(grad_kn, key_unit, key_spread, k_gain)
        turned_ref[at, :] = grad_query.T.astype(BF)
        turned_ref[key_at, :] = grad_key.T.astype(BF)


def attention_call(kernel, arrays, gains, out_rows):
    tokens, columns = arrays[1].shape
    head = gains.shape[-1]
    pairs = (tokens // PATCH) * (columns // head)
    return pl.pallas_call(
        kernel,
        grid=(tokens // PATCH,),
        in_specs=[pl.BlockSpec((PATCH, array.shape[1]), lambda i: (i, 0)) for array in arrays]
        + [pl.BlockSpec(gains.shape, lambda i: (0, 0))],
        out_specs=pl.BlockSpec((out_rows, PATCH), lambda i: (0, i)),
        out_shape=jax.ShapeDtypeStruct((out_rows, tokens), BF),
        compiler_params=params(16),
        cost_estimate=cost(pairs * 8 * PATCH * PATCH * head, 4 * len(arrays) * arrays[0].size),
    )(*arrays, gains)


def product_kernel(specs, grid, n_add, turn, turned_ref, normed_ref, *refs):
    def body(*blocks):
        turned = turned_ref[...]
        for side in range(2):
            total = jnp.dot(turned, blocks[side][...], preferred_element_type=F32)
            for block in blocks[2 + side * n_add : 2 + (side + 1) * n_add]:
                total = total + block[...].astype(F32)
            blocks[side - 2][...] = (total.T if turn else total).astype(BF)

    pltpu.emit_pipeline(body, grid=grid, in_specs=specs[:-2], out_specs=specs[-2:])(
        normed_ref, normed_ref, *refs
    )


def product_call(turned, normed, rows, units, addends=((), ()), turn=False):
    columns, tokens = turned.shape
    tile = 256 if rows % 256 == 0 else 128
    count, n_add, steps = len(units[0]), len(addends[0]), rows // tile

    def side(first, last):
        return pl.BlockSpec((tokens, tile), lambda u, i: (0, (first + u * (last - first)) * steps + i))

    def added(which):
        return pl.BlockSpec((columns, tile), lambda u, i: (which, i))

    if turn:
        shape, out = (rows, columns), pl.BlockSpec((tile, columns), lambda u, i: (i, 0))
    else:
        shape, out = (count * columns, rows), pl.BlockSpec((columns, tile), lambda u, i: (u, i))
    addends = [*addends[0], *addends[1]]
    specs = [side(chosen[0], chosen[-1]) for chosen in units] + [added(which) for _, which in addends]
    return pl.pallas_call(
        functools.partial(product_kernel, specs + [out] * 2, (count, steps), n_add, turn),
        in_specs=[pl.BlockSpec(memory_space=pltpu.VMEM), pl.BlockSpec(memory_space=pltpu.HBM)]
        + [pl.BlockSpec(memory_space=pl.ANY)] * len(addends),
        out_specs=[pl.BlockSpec(memory_space=pl.ANY)] * 2,
        out_shape=[jax.ShapeDtypeStruct(shape, BF)] * 2,
        compiler_params=params(10),
        cost_estimate=cost(
            4 * count * columns * tokens * rows,
            2 * columns * tokens + 4 * count * tokens * rows + (4 + 4 * n_add) * columns * rows,
        ),
    )(turned, normed, *[array for array, _ in addends])


def back_kernel(specs, grid, pair_ref, value_ref, *refs):
    def body(w_pair_ref, w_value_ref, *blocks):
        total = jnp.dot(w_pair_ref[...], pair_ref[...], preferred_element_type=F32)
        total = total + jnp.dot(w_value_ref[...], value_ref[...], preferred_element_type=F32)
        for block in blocks[:-1]:
            total = total + block[...].astype(F32)
        blocks[-1][...] = total.astype(blocks[-1].dtype)

    pltpu.emit_pipeline(body, grid=grid, in_specs=specs[:-1], out_specs=specs[-1:])(*refs)


def back_call(pair, value, w_pair, w_value, rows, odd, addends, dtype):
    level_tokens = pair.shape[1]
    tile = rows // 2 if rows % 256 == 0 else rows
    steps = w_pair.shape[0] // tile // 2
    first = steps if odd else 0
    block = pl.BlockSpec((tile, level_tokens), lambda i: (i, 0))
    specs = [pl.BlockSpec((tile, w.shape[1]), lambda i: (first + i, 0)) for w in (w_pair, w_value)]
    vmem, hbm = (pl.BlockSpec(memory_space=space) for space in (pltpu.VMEM, pltpu.HBM))
    anywhere = pl.BlockSpec(memory_space=pl.ANY)
    return pl.pallas_call(
        functools.partial(back_kernel, specs + [block] * (len(addends) + 1), (steps,)),
        in_specs=[vmem, vmem, hbm, hbm] + [anywhere] * len(addends),
        out_specs=anywhere,
        out_shape=jax.ShapeDtypeStruct((steps * tile, level_tokens), dtype),
        compiler_params=params(8),
        cost_estimate=cost(
            2 * steps * tile * level_tokens * (pair.shape[0] + value.shape[0]),
            2 * steps * tile * (pair.shape[0] + value.shape[0] + 3 * level_tokens),
        ),
    )(pair, value, w_pair, w_value, *addends)


def gather_kernel(cols, n_parts, core_ref, *refs):
    parts, outs = refs[: 2 * n_parts], refs[2 * n_parts :]
    here = pl.program_id(0) == core_ref[0]

    def store(blocks):
        total = blocks[0][...].astype(F32)
        for block in blocks[1:]:
            total = total + block[...].astype(F32)
        for k, out in enumerate(outs):
            out[...] = total[k * cols : (k + 1) * cols].T.astype(BF)

    @pl.when(here)
    def _():
        store(parts[:n_parts])

    @pl.when(jnp.logical_not(here))
    def _():
        store(parts[n_parts:])


def gather_call(core, mine, other, cols):
    columns, rows = mine[0].shape
    tile = 256 if rows % 256 == 0 else 128
    here = pl.BlockSpec(
        (columns, tile), lambda h, i, core_ref: (0, jnp.where(h == core_ref[0], i, rows // tile * h - h))
    )
    there = pl.BlockSpec(
        (columns, tile), lambda h, i, core_ref: (0, jnp.where(h != core_ref[0], i, rows // tile * h - h))
    )
    return pl.pallas_call(
        functools.partial(gather_kernel, cols, len(mine)),
        grid_spec=pltpu.PrefetchScalarGridSpec(
            num_scalar_prefetch=1,
            grid=(2, rows // tile),
            in_specs=[here] * len(mine) + [there] * len(other),
            out_specs=[pl.BlockSpec((tile, cols), lambda h, i, core_ref: (i, h))] * (columns // cols),
        ),
        out_shape=[jax.ShapeDtypeStruct((rows, 2 * cols), BF)] * (columns // cols),
        compiler_params=params(12),
    )(core.reshape(1), *mine, *other)


def place_kernel(core_ref, mine_ref, other_ref, out_ref):
    here = pl.program_id(0) == core_ref[0]

    @pl.when(here)
    def _():
        out_ref[...] = mine_ref[...]

    @pl.when(jnp.logical_not(here))
    def _():
        out_ref[...] = other_ref[...]


def place_call(core, mine, other, cols, part):
    rows = mine.shape[0]
    block = pl.BlockSpec((rows, cols), lambda i, core_ref: (0, part))
    return pl.pallas_call(
        place_kernel,
        grid_spec=pltpu.PrefetchScalarGridSpec(
            num_scalar_prefetch=1,
            grid=(2,),
            in_specs=[block, block],
            out_specs=pl.BlockSpec((rows, cols), lambda i, core_ref: (0, i)),
        ),
        out_shape=jax.ShapeDtypeStruct((rows, 2 * cols), BF),
        compiler_params=params(16),
    )(core.reshape(1), mine, other)


def finish_kernel(rows, n_dp, place_ref, mine_ref, other_ref, unit_ref, spread_ref, gain_ref, out_ref, held):
    n_chips = n_dp // 2
    held[: n_chips * rows] = mine_ref[...]
    held[n_chips * rows :] = other_ref[...].astype(F32)
    place = place_ref[0]
    columns = []
    total, inner = 0.0, 0.0
    for b in range(n_dp):
        r = b ^ place
        unit = (r & 1) * n_chips + (r >> 1)
        at = pl.ds(b * rows, rows)
        grad = held[pl.ds(pl.multiple_of(unit * rows, rows), rows), :].T
        scaled = grad * gain_ref[:, at]
        total = total + jnp.sum(scaled, axis=-1, keepdims=True)
        inner = inner + jnp.sum(scaled * unit_ref[:, at], axis=-1, keepdims=True)
        columns.append(scaled)
    average, inner = total * (1.0 / (n_dp * rows)), inner * (1.0 / (n_dp * rows))
    for b in range(n_dp):
        at = pl.ds(b * rows, rows)
        result = (columns[b] - average - unit_ref[:, at] * inner) * spread_ref[...]
        out_ref[:, at] = result.astype(BF)


def finish_call(place, mine, other, unit_rows, row_spread, norm_gain, rows):
    own, width = unit_rows.shape
    vmem = pl.BlockSpec(memory_space=pltpu.VMEM)
    return pl.pallas_call(
        functools.partial(finish_kernel, rows, width // rows),
        in_specs=[pl.BlockSpec(memory_space=pltpu.SMEM)] + [vmem] * 5,
        out_specs=vmem,
        out_shape=jax.ShapeDtypeStruct((own, width), BF),
        scratch_shapes=[pltpu.VMEM((width, own), F32)],
        compiler_params=params(20),
    )(place.reshape(1), mine, other, unit_rows, row_spread, norm_gain.reshape(1, width))


def per_device(n_dp, n_mp, tokens, norm_gain, q_gain, k_gain, w_query, w_key, w_value, grad_heads):
    own, width = tokens.shape
    rows, cols = w_query.shape[0], w_query.shape[1] // 2
    n_chips = n_dp // 2
    group = n_mp * own
    place = lax.axis_index("dp")
    core = place & 1

    def swap(array, bit):
        return lax.ppermute(array, "dp", [(i, i ^ bit) for i in range(n_dp)])

    def half(array, which):
        return lax.dynamic_slice_in_dim(array, which * cols, cols, 1)

    def together(*arrays):
        return lax.optimization_barrier(arrays)

    ring = list(range(0, n_mp, 2)) + list(range(n_mp - 1, 0, -2))
    level = lax.axis_index("mp")
    spot = jnp.where(level & 1 == 0, level >> 1, n_mp - 1 - (level >> 1))
    ring_pairs = [(ring[i], ring[(i + 1) % n_mp]) for i in range(n_mp)]

    def level_at(back):
        at = lax.rem(spot + 2 * n_mp - back, n_mp)
        return jnp.where(at < n_mp // 2, 2 * at, 2 * (n_mp - 1 - at) + 1)

    def ring_on(array):
        return lax.ppermute(array, "mp", ring_pairs)

    def unit_of(r):
        return (r & 1) * n_chips + (r >> 1)

    def feature_block(array, r):
        return lax.dynamic_slice_in_dim(array, (place ^ r) * rows, rows, 1)

    def columns_of(weights, which):
        return jnp.concatenate([half(w, which) for w in weights], axis=1)

    def gather_start(held):
        held = dict(held)
        bit = 8
        while bit < n_dp:
            held.update({r ^ bit: swap(part, bit) for r, part in list(held.items())})
            bit *= 2
        for r, part in list(held.items()):
            held[r ^ 2] = swap(part, 2)
            held[r ^ 4] = swap(part, 4)
        return held

    def gather_rest(held):
        held = dict(held)
        for r in range(0, n_dp, 8):
            held[r ^ 6] = swap(held[r ^ 2], 4)
            held[r ^ 7] = swap(held[r ^ 5], 2)
        return held

    def whole(held):
        return jnp.concatenate([held[r] for r in (*range(0, n_dp, 2), *range(1, n_dp, 2))], axis=0)

    pair_weights = (w_query, w_key)
    own_pair, sent_pair = columns_of(pair_weights, core), columns_of(pair_weights, 1 - core)
    tokens, own_pair, sent_pair = together(tokens, own_pair, sent_pair)
    held_pair = gather_start({0: own_pair})
    other_pair = swap(sent_pair, 1)

    normed_own, unit_rows, row_spread = normalize(tokens.astype(F32), norm_gain)
    normed_own = normed_own.astype(BF)
    even = jnp.concatenate([feature_block(normed_own, r) for r in range(0, n_dp, 2)], axis=1)
    odd = jnp.concatenate([feature_block(normed_own, r) for r in range(1, n_dp, 2)], axis=1)
    block = jnp.concatenate([even, swap(odd, 1)], axis=0)

    normed = blank((2 * group, width), BF)

    def put(normed, block, step):
        beside = swap(block, 1)
        start = level_at(step) * own
        mine, other = core * group + start, (1 - core) * group + start
        for piece, at, column in (
            (block[:own], mine, 0),
            (block[own:], other, 0),
            (beside[:own], other, width // 2),
            (beside[own:], mine, width // 2),
        ):
            normed = lax.dynamic_update_slice(normed, piece, (at, column))
        return normed

    held_pair, normed = together(held_pair, normed)
    held_pair.update(gather_start({1: other_pair}))
    normed = put(normed, block, 0)
    for step in range(1, n_mp):
        block = ring_on(block)
        normed = put(normed, block, step)
        if step == 1:
            held_pair, normed, w_value, grad_heads = together(held_pair, normed, w_value, grad_heads)
            held_pair = gather_rest(held_pair)
            shard_value = [half(w_value, core), swap(half(w_value, 1 - core), 1)]
            shard_value = jnp.concatenate(shard_value, axis=0)
            grads_mine, grads_other = half(grad_heads, core), swap(half(grad_heads, 1 - core), 1)
        elif step == 2:
            shard_value, normed = together(shard_value, normed)
            held_value = gather_start({0: shard_value})

    grad_out = blank((2 * group, cols), BF)
    grad_out = lax.dynamic_update_slice_in_dim(grad_out, grads_mine, core * group, 0)
    grad_out = lax.dynamic_update_slice_in_dim(grad_out, grads_other, (1 - core) * group, 0)
    gains = jnp.stack([q_gain, k_gain])

    full_pair = whole(held_pair)
    pair = jnp.dot(normed, full_pair, preferred_element_type=F32)
    turned_value = attention_call(first_kernel, (pair, grad_out), gains, cols)

    def products(turned, r, offsets, addends=((), ()), turn=False):
        units = [[unit_of(r ^ f) for f in side] for side in offsets]
        return product_call(turned, normed, rows, units, addends, turn)

    blocks_of_four = range(0, n_dp, 8)

    def messages(turned, to_x, to_y):
        return [products(turned, r, (to_x, to_y)) for r in blocks_of_four]

    def late_messages(turned, far):
        return [
            products(turned, r, ((3,), (4,)), (((from_y, 0),), ((from_x, 0),)))
            for r, (from_x, from_y) in zip(blocks_of_four, far)
        ]

    def send(messages, x=2, y=4):
        return [[swap(to_x, x), swap(to_y, y)] for to_x, to_y in messages]

    def scatter_end(turned, early, unit, late):
        def own(r, turn):
            (early_x, early_y), (late_x, late_y) = early[r // 8], late[r // 8]
            addends = (((early_x, unit), (late_y, 0)), ((early_y, unit), (late_x, 0)))
            return products(turned, r, ((0,), (1,)), addends, turn)

        if n_dp == 8:
            return own(0, True)
        totals = {r: own(r, False) for r in blocks_of_four}
        bit = n_dp // 2
        while bit >= 8:
            for r in [r for r in totals if r < bit]:
                passed = [swap(total, bit) for total in totals.pop(r ^ bit)]
                totals[r] = [
                    (a.astype(F32) + b.astype(F32)).astype(BF) for a, b in zip(totals[r], passed)
                ]
            bit //= 2
        return [total.T for total in totals[0]]

    held_value, turned_value = together(held_value, turned_value)
    pieces = {r ^ f: part[f * rows : (f + 1) * rows] for r, part in held_value.items() for f in (0, 1)}
    relayed = [r ^ f for r in blocks_of_four for f in (2, 5)]
    pieces.update(zip(relayed, together(*[pieces[r] for r in relayed])))
    held_value = gather_rest(pieces)
    first_value = send(messages(turned_value, (6, 2), (7, 5)))
    full_value = whole(held_value)
    values = jnp.dot(normed, full_value, preferred_element_type=F32).astype(BF)
    turned_pair = attention_call(rest_kernel, (pair, grad_out, values), gains, 2 * cols)

    def back_odd(step, turned_pair, turned_value):
        at = level_at(step + 1) * own
        chosen = [
            jnp.concatenate(
                [lax.dynamic_slice_in_dim(turned, g * group + at, own, 1) for g in range(2)], axis=1
            )
            for turned in (turned_pair, turned_value)
        ]
        return chosen, back_call(*chosen, full_pair, full_value, rows, True, (), BF)

    def back_even(chosen, passed, dtype):
        return back_call(*chosen, full_pair, full_value, rows, False, (passed,), dtype)

    chosen, sent, partial = {}, {}, {}
    chosen[0], sent[0] = back_odd(0, turned_pair, turned_value)
    chosen[1], sent[1] = back_odd(1, turned_pair, turned_value)
    late_value = late_messages(turned_value, first_value)
    late_value, sent = together(late_value, sent)
    late_value = send(late_value)
    passed = {step: swap(sent[step], 1) for step in range(2)}
    far_pair = messages(turned_pair, (6,), (7,))
    far_pair, passed = together(far_pair, passed)
    message = back_even(chosen[0], passed[0], BF)
    message, far_pair, turned_pair, turned_value = together(message, far_pair, turned_pair, turned_value)
    arrived, far_pair = ring_on(message), send(far_pair)

    turned_pair, turned_value, late_value = together(turned_pair, turned_value, late_value)
    for step in range(2, 4):
        chosen[step], sent[step] = back_odd(step, turned_pair, turned_value)
    ends_value = scatter_end(turned_value, first_value, 1, late_value)
    partial[1] = back_even(chosen[1], passed[1], BF)
    early_pair = messages(turned_pair, (2,), (5,))
    for step in range(1, n_mp - 1):
        if step == 1:
            partial[1], early_pair, sent, far_pair, ends_value = together(
                partial[1], early_pair, sent, far_pair, ends_value
            )
        elif step == 2:
            partial[2], late_pair, early_pair, own_pair = together(
                partial[2], late_pair, early_pair, own_pair
            )
        message = (partial[step].astype(F32) + arrived.astype(F32)).astype(BF)
        if step == 1:
            message, early_pair, sent, turned_pair, turned_value = together(
                message, early_pair, sent, turned_pair, turned_value
            )
            early_pair = send(early_pair, y=5)
        elif step == 2:
            message, late_pair, own_pair, ends_value = together(
                message, late_pair, own_pair, ends_value
            )
            late_pair = send(late_pair, x=3)
            own_pair = [[even, swap(odd, 1)] for even, odd in own_pair]
            passed_value = swap(ends_value[1], 1)
        arrived = ring_on(message)
        if step + 2 < n_mp:
            near = [step + 1, step + 2] if step + 3 == n_mp else [step + 1]
            for level_step in near:
                passed[level_step] = swap(sent[level_step], 1)
            here = [passed[level_step] for level_step in near]
            turned_pair, turned_value, here = together(turned_pair, turned_value, here)
            passed.update(zip(near, here))
            for level_step in near:
                dtype = F32 if level_step == n_mp - 1 else BF
                partial[level_step] = back_even(chosen[level_step], passed[level_step], dtype)
            if step + 3 == n_mp:
                partial[n_mp - 2], partial[n_mp - 1] = together(partial[n_mp - 2], partial[n_mp - 1])
            else:
                chosen[step + 3], sent[step + 3] = back_odd(step + 3, turned_pair, turned_value)
            if step == 1:
                late_pair = late_messages(turned_pair, far_pair)
                own_pair = messages(turned_pair, (0,), (1,))
    total = partial[n_mp - 1] + arrived.astype(F32)

    mine = lax.dynamic_slice_in_dim(total, core * own, own, 1)
    other = lax.dynamic_slice_in_dim(total, (1 - core) * own, own, 1).astype(BF)
    other = swap(other, 1)
    grad_tokens = finish_call(place, mine, other, unit_rows, row_spread, norm_gain, rows)
    grad_tokens, late_pair = together(grad_tokens, late_pair)

    here, there = {}, {}
    for r, (own_even, own_odd), early, late in zip(blocks_of_four, own_pair, early_pair, late_pair):
        here[r] = [own_even, early[0], late[1]]
        there[r] = [own_odd, early[1], late[0]]
    bit = n_dp // 2
    while bit >= 8:
        for parts in (here, there):
            for r in [r for r in parts if r >= bit]:
                parts[r ^ bit].append(swap(sum(p.astype(F32) for p in parts.pop(r)).astype(BF), bit))
        bit //= 2
    out_query, out_key = gather_call(core, here[0], there[0], cols)
    out_value = place_call(core, ends_value[0], passed_value, cols, 0)
    return (grad_tokens, out_query, out_key, out_value)


def solution(mesh):
    matrix = P("dp", "mp")
    token_rows = P(("dp", "mp"), None)
    return jax.shard_map(
        functools.partial(per_device, mesh.shape["dp"], mesh.shape["mp"]),
        mesh=mesh,
        in_specs=(token_rows, P(), P(), P(), matrix, matrix, matrix, matrix),
        out_specs=(token_rows, matrix, matrix, matrix),
        check_vma=False,
    )
```

```python
import functools

import jax
import jax.numpy as jnp
from jax import lax
from jax.experimental import pallas as pl
from jax.experimental.pallas import tpu as pltpu
from jax.sharding import PartitionSpec as P

PATCH = 256
BF = jnp.bfloat16
F32 = jnp.float32


def normalize(row_data, gain_vector):
    average = jnp.mean(row_data, axis=-1, keepdims=True)
    centred = row_data - average
    inv_spread = lax.rsqrt(jnp.mean(centred * centred, axis=-1, keepdims=True) + 1e-06)
    unit_data = centred * inv_spread
    return (unit_data * gain_vector, unit_data, inv_spread)


def normalize_back(grad_out, unit_data, inv_spread, gain_vector):
    scaled = grad_out * gain_vector
    inner_term = jnp.mean(scaled * unit_data, axis=-1, keepdims=True)
    return (scaled - jnp.mean(scaled, axis=-1, keepdims=True) - unit_data * inner_term) * inv_spread


def dot_nt(a, b):
    return lax.dot_general(a, b, (((1,), (1,)), ((), ())), preferred_element_type=F32)


def dot_tn(a, b):
    return lax.dot_general(a, b, (((0,), (0,)), ((), ())), preferred_element_type=F32)


def params(mib):
    return pltpu.CompilerParams(vmem_limit_bytes=mib * 2**20)


def cost(flops, bytes_accessed):
    return pl.CostEstimate(flops=flops // 6, bytes_accessed=bytes_accessed // 6, transcendentals=0)


def blank(shape, dtype):
    return pl.pallas_call(
        lambda out_ref: None,
        out_shape=jax.ShapeDtypeStruct(shape, dtype),
        out_specs=pl.BlockSpec(memory_space=pl.ANY),
    )()


def attention_of(query_bf, key_bf):
    scores = dot_nt(key_bf, query_bf) * query_bf.shape[-1] ** (-0.5)
    raised = jnp.exp(scores - jnp.max(scores, axis=0, keepdims=True))
    return raised * (1.0 / jnp.sum(raised, axis=0, keepdims=True))


def first_kernel(qk_ref, g_ref, gains_ref, turned_ref):
    head, cols = gains_ref.shape[1], g_ref.shape[1]
    for h in range(cols // head):
        at, key_at = pl.ds(h * head, head), pl.ds(cols + h * head, head)
        query_bf = normalize(qk_ref[:, at], gains_ref[0:1])[0].astype(BF)
        key_bf = normalize(qk_ref[:, key_at], gains_ref[1:2])[0].astype(BF)
        attention = attention_of(query_bf, key_bf).astype(BF)
        grad_value = jnp.dot(attention, g_ref[:, at], preferred_element_type=F32)
        turned_ref[at, :] = grad_value.T.astype(BF)


def rest_kernel(qk_ref, g_ref, v_ref, gains_ref, turned_ref):
    head, cols = gains_ref.shape[1], g_ref.shape[1]
    factor = head ** (-0.5)
    q_gain, k_gain = gains_ref[0:1], gains_ref[1:2]
    for h in range(cols // head):
        at, key_at = pl.ds(h * head, head), pl.ds(cols + h * head, head)
        query_normed, query_unit, query_spread = normalize(qk_ref[:, at], q_gain)
        key_normed, key_unit, key_spread = normalize(qk_ref[:, key_at], k_gain)
        query_bf, key_bf = query_normed.astype(BF), key_normed.astype(BF)
        attention = attention_of(query_bf, key_bf)
        grad_probs = dot_nt(v_ref[:, at], g_ref[:, at])
        delta = jnp.sum(attention * grad_probs, axis=0, keepdims=True)
        grad_scores = (attention * (grad_probs - delta) * factor).astype(BF)
        grad_kn = jnp.dot(grad_scores, query_bf, preferred_element_type=F32)
        grad_qn = dot_tn(grad_scores, key_bf)
        grad_query = normalize_back(grad_qn, query_unit, query_spread, q_gain)
        grad_key = normalize_back(grad_kn, key_unit, key_spread, k_gain)
        turned_ref[at, :] = grad_query.T.astype(BF)
        turned_ref[key_at, :] = grad_key.T.astype(BF)


def attention_call(kernel, arrays, gains, out_rows):
    tokens, columns = arrays[1].shape
    head = gains.shape[-1]
    pairs = (tokens // PATCH) * (columns // head)
    return pl.pallas_call(
        kernel,
        grid=(tokens // PATCH,),
        in_specs=[pl.BlockSpec((PATCH, array.shape[1]), lambda i: (i, 0)) for array in arrays]
        + [pl.BlockSpec(gains.shape, lambda i: (0, 0))],
        out_specs=pl.BlockSpec((out_rows, PATCH), lambda i: (0, i)),
        out_shape=jax.ShapeDtypeStruct((out_rows, tokens), BF),
        compiler_params=params(12),
        cost_estimate=cost(pairs * 8 * PATCH * PATCH * head, 4 * len(arrays) * arrays[0].size),
    )(*arrays, gains)


def product_kernel(specs, grid, n_add, turn, turned_ref, normed_ref, *refs):
    def body(*blocks):
        turned = turned_ref[...]
        for side in range(2):
            total = jnp.dot(turned, blocks[side][...], preferred_element_type=F32)
            for block in blocks[2 + side * n_add : 2 + (side + 1) * n_add]:
                total = total + block[...].astype(F32)
            blocks[side - 2][...] = (total.T if turn else total).astype(BF)

    pltpu.emit_pipeline(body, grid=grid, in_specs=specs[:-2], out_specs=specs[-2:])(
        normed_ref, normed_ref, *refs
    )


def product_call(turned, normed, rows, units, addends=((), ()), turn=False):
    columns, tokens = turned.shape
    tile = 256 if rows % 256 == 0 else 128
    count, n_add, steps = len(units[0]), len(addends[0]), rows // tile

    def side(first, last):
        return pl.BlockSpec((tokens, tile), lambda u, i: (0, (first + u * (last - first)) * steps + i))

    def added(which):
        return pl.BlockSpec((columns, tile), lambda u, i: (which, i))

    if turn:
        shape, out = (rows, columns), pl.BlockSpec((tile, columns), lambda u, i: (i, 0))
    else:
        shape, out = (count * columns, rows), pl.BlockSpec((columns, tile), lambda u, i: (u, i))
    addends = [*addends[0], *addends[1]]
    specs = [side(chosen[0], chosen[-1]) for chosen in units] + [added(which) for _, which in addends]
    return pl.pallas_call(
        functools.partial(product_kernel, specs + [out] * 2, (count, steps), n_add, turn),
        in_specs=[pl.BlockSpec(memory_space=pltpu.VMEM), pl.BlockSpec(memory_space=pltpu.HBM)]
        + [pl.BlockSpec(memory_space=pl.ANY)] * len(addends),
        out_specs=[pl.BlockSpec(memory_space=pl.ANY)] * 2,
        out_shape=[jax.ShapeDtypeStruct(shape, BF)] * 2,
        compiler_params=params(10),
        cost_estimate=cost(
            4 * count * columns * tokens * rows,
            2 * columns * tokens + 4 * count * tokens * rows + (4 + 4 * n_add) * columns * rows,
        ),
    )(turned, normed, *[array for array, _ in addends])


def back_kernel(pair_ref, value_ref, w_pair_ref, w_value_ref, *refs):
    total = jnp.dot(w_pair_ref[...], pair_ref[...], preferred_element_type=F32)
    total = total + jnp.dot(w_value_ref[...], value_ref[...], preferred_element_type=F32)
    for ref in refs[:-1]:
        total = total + ref[...].astype(F32)
    refs[-1][...] = total.astype(refs[-1].dtype)


def back_call(pair, value, w_pair, w_value, rows, odd, addends, dtype):
    level_tokens = pair.shape[1]
    units = w_pair.shape[0] // rows // 2
    first = units if odd else 0
    block = pl.BlockSpec((rows, level_tokens), lambda i: (i, 0))
    return pl.pallas_call(
        back_kernel,
        grid=(units,),
        in_specs=[
            pl.BlockSpec(pair.shape, lambda i: (0, 0)),
            pl.BlockSpec(value.shape, lambda i: (0, 0)),
            pl.BlockSpec((rows, w_pair.shape[1]), lambda i: (first + i, 0)),
            pl.BlockSpec((rows, w_value.shape[1]), lambda i: (first + i, 0)),
        ]
        + [block] * len(addends),
        out_specs=block,
        out_shape=jax.ShapeDtypeStruct((units * rows, level_tokens), dtype),
        compiler_params=params(11),
        cost_estimate=cost(
            2 * units * rows * level_tokens * (pair.shape[0] + value.shape[0]),
            2 * units * rows * (pair.shape[0] + value.shape[0] + 3 * level_tokens),
        ),
    )(pair, value, w_pair, w_value, *addends)


def gather_kernel(cols, n_parts, core_ref, *refs):
    parts, outs = refs[: 2 * n_parts], refs[2 * n_parts :]
    here = pl.program_id(0) == core_ref[0]

    def store(blocks):
        total = blocks[0][...].astype(F32)
        for block in blocks[1:]:
            total = total + block[...].astype(F32)
        for k, out in enumerate(outs):
            out[...] = total[k * cols : (k + 1) * cols].T.astype(BF)

    @pl.when(here)
    def _():
        store(parts[:n_parts])

    @pl.when(jnp.logical_not(here))
    def _():
        store(parts[n_parts:])


def gather_call(core, mine, other, cols):
    columns, rows = mine[0].shape
    tile = 256 if rows % 256 == 0 else 128
    here = pl.BlockSpec(
        (columns, tile), lambda h, i, core_ref: (0, jnp.where(h == core_ref[0], i, rows // tile * h - h))
    )
    there = pl.BlockSpec(
        (columns, tile), lambda h, i, core_ref: (0, jnp.where(h != core_ref[0], i, rows // tile * h - h))
    )
    return pl.pallas_call(
        functools.partial(gather_kernel, cols, len(mine)),
        grid_spec=pltpu.PrefetchScalarGridSpec(
            num_scalar_prefetch=1,
            grid=(2, rows // tile),
            in_specs=[here] * len(mine) + [there] * len(other),
            out_specs=[pl.BlockSpec((tile, cols), lambda h, i, core_ref: (i, h))] * (columns // cols),
        ),
        out_shape=[jax.ShapeDtypeStruct((rows, 2 * cols), BF)] * (columns // cols),
        compiler_params=params(12),
    )(core.reshape(1), *mine, *other)


def place_kernel(core_ref, mine_ref, other_ref, out_ref):
    here = pl.program_id(0) == core_ref[0]

    @pl.when(here)
    def _():
        out_ref[...] = mine_ref[...]

    @pl.when(jnp.logical_not(here))
    def _():
        out_ref[...] = other_ref[...]


def place_call(core, mine, other, cols, part):
    rows = mine.shape[0]
    block = pl.BlockSpec((rows, cols), lambda i, core_ref: (0, part))
    return pl.pallas_call(
        place_kernel,
        grid_spec=pltpu.PrefetchScalarGridSpec(
            num_scalar_prefetch=1,
            grid=(2,),
            in_specs=[block, block],
            out_specs=pl.BlockSpec((rows, cols), lambda i, core_ref: (0, i)),
        ),
        out_shape=jax.ShapeDtypeStruct((rows, 2 * cols), BF),
        compiler_params=params(12),
    )(core.reshape(1), mine, other)


def finish_kernel(rows, n_dp, place_ref, mine_ref, other_ref, unit_ref, spread_ref, gain_ref, out_ref, held):
    n_chips = n_dp // 2
    held[: n_chips * rows] = mine_ref[...]
    held[n_chips * rows :] = other_ref[...].astype(F32)
    place = place_ref[0]
    columns = []
    total, inner = 0.0, 0.0
    for b in range(n_dp):
        r = b ^ place
        unit = (r & 1) * n_chips + (r >> 1)
        at = pl.ds(b * rows, rows)
        grad = held[pl.ds(pl.multiple_of(unit * rows, rows), rows), :].T
        scaled = grad * gain_ref[:, at]
        total = total + jnp.sum(scaled, axis=-1, keepdims=True)
        inner = inner + jnp.sum(scaled * unit_ref[:, at], axis=-1, keepdims=True)
        columns.append(scaled)
    average, inner = total * (1.0 / (n_dp * rows)), inner * (1.0 / (n_dp * rows))
    for b in range(n_dp):
        at = pl.ds(b * rows, rows)
        result = (columns[b] - average - unit_ref[:, at] * inner) * spread_ref[...]
        out_ref[:, at] = result.astype(BF)


def finish_call(place, mine, other, unit_rows, row_spread, norm_gain, rows):
    own, width = unit_rows.shape
    vmem = pl.BlockSpec(memory_space=pltpu.VMEM)
    return pl.pallas_call(
        functools.partial(finish_kernel, rows, width // rows),
        in_specs=[pl.BlockSpec(memory_space=pltpu.SMEM)] + [vmem] * 5,
        out_specs=vmem,
        out_shape=jax.ShapeDtypeStruct((own, width), BF),
        scratch_shapes=[pltpu.VMEM((width, own), F32)],
        compiler_params=params(20),
    )(place.reshape(1), mine, other, unit_rows, row_spread, norm_gain.reshape(1, width))


def per_device(n_dp, n_mp, tokens, norm_gain, q_gain, k_gain, w_query, w_key, w_value, grad_heads):
    own, width = tokens.shape
    rows, cols = w_query.shape[0], w_query.shape[1] // 2
    n_chips = n_dp // 2
    group = n_mp * own
    place = lax.axis_index("dp")
    core = place & 1

    def swap(array, bit):
        return lax.ppermute(array, "dp", [(i, i ^ bit) for i in range(n_dp)])

    def half(array, which):
        return lax.dynamic_slice_in_dim(array, which * cols, cols, 1)

    def together(*arrays):
        return lax.optimization_barrier(arrays)

    ring = list(range(0, n_mp, 2)) + list(range(n_mp - 1, 0, -2))
    level = lax.axis_index("mp")
    spot = jnp.where(level & 1 == 0, level >> 1, n_mp - 1 - (level >> 1))
    ring_pairs = [(ring[i], ring[(i + 1) % n_mp]) for i in range(n_mp)]

    def level_at(back):
        at = lax.rem(spot + 2 * n_mp - back, n_mp)
        return jnp.where(at < n_mp // 2, 2 * at, 2 * (n_mp - 1 - at) + 1)

    def ring_on(array):
        return lax.ppermute(array, "mp", ring_pairs)

    def unit_of(r):
        return (r & 1) * n_chips + (r >> 1)

    def feature_block(array, r):
        return lax.dynamic_slice_in_dim(array, (place ^ r) * rows, rows, 1)

    def columns_of(weights, which):
        return jnp.concatenate([half(w, which) for w in weights], axis=1)

    def gather_start(held):
        held = dict(held)
        bit = 8
        while bit < n_dp:
            held.update({r ^ bit: swap(part, bit) for r, part in list(held.items())})
            bit *= 2
        for r, part in list(held.items()):
            held[r ^ 2] = swap(part, 2)
            held[r ^ 4] = swap(part, 4)
        return held

    def gather_rest(held):
        held = dict(held)
        for r in range(0, n_dp, 8):
            held[r ^ 6] = swap(held[r ^ 2], 4)
            held[r ^ 7] = swap(held[r ^ 5], 2)
        return held

    def whole(held):
        return jnp.concatenate([held[r] for r in (*range(0, n_dp, 2), *range(1, n_dp, 2))], axis=0)

    pair_weights = (w_query, w_key)
    own_pair, sent_pair = columns_of(pair_weights, core), columns_of(pair_weights, 1 - core)
    tokens, own_pair, sent_pair = together(tokens, own_pair, sent_pair)
    held_pair = gather_start({0: own_pair})
    other_pair = swap(sent_pair, 1)

    normed_own, unit_rows, row_spread = normalize(tokens.astype(F32), norm_gain)
    normed_own = normed_own.astype(BF)
    even = jnp.concatenate([feature_block(normed_own, r) for r in range(0, n_dp, 2)], axis=1)
    odd = jnp.concatenate([feature_block(normed_own, r) for r in range(1, n_dp, 2)], axis=1)
    block = jnp.concatenate([even, swap(odd, 1)], axis=0)

    normed = blank((2 * group, width), BF)

    def put(normed, block, step):
        beside = swap(block, 1)
        start = level_at(step) * own
        mine, other = core * group + start, (1 - core) * group + start
        for piece, at, column in (
            (block[:own], mine, 0),
            (block[own:], other, 0),
            (beside[:own], other, width // 2),
            (beside[own:], mine, width // 2),
        ):
            normed = lax.dynamic_update_slice(normed, piece, (at, column))
        return normed

    held_pair, normed = together(held_pair, normed)
    held_pair.update(gather_start({1: other_pair}))
    normed = put(normed, block, 0)
    for step in range(1, n_mp):
        block = ring_on(block)
        normed = put(normed, block, step)
        if step == 1:
            held_pair, normed, w_value, grad_heads = together(held_pair, normed, w_value, grad_heads)
            held_pair = gather_rest(held_pair)
            shard_value = [half(w_value, core), swap(half(w_value, 1 - core), 1)]
            shard_value = jnp.concatenate(shard_value, axis=0)
            grads_mine, grads_other = half(grad_heads, core), swap(half(grad_heads, 1 - core), 1)
        elif step == 2:
            shard_value, normed = together(shard_value, normed)
            held_value = gather_start({0: shard_value})

    grad_out = blank((2 * group, cols), BF)
    grad_out = lax.dynamic_update_slice_in_dim(grad_out, grads_mine, core * group, 0)
    grad_out = lax.dynamic_update_slice_in_dim(grad_out, grads_other, (1 - core) * group, 0)
    gains = jnp.stack([q_gain, k_gain])

    full_pair = whole(held_pair)
    pair = jnp.dot(normed, full_pair, preferred_element_type=F32)
    turned_value = attention_call(first_kernel, (pair, grad_out), gains, cols)

    def products(turned, r, offsets, addends=((), ()), turn=False):
        units = [[unit_of(r ^ f) for f in side] for side in offsets]
        return product_call(turned, normed, rows, units, addends, turn)

    blocks_of_four = range(0, n_dp, 8)

    def messages(turned, to_x, to_y):
        return [products(turned, r, (to_x, to_y)) for r in blocks_of_four]

    def late_messages(turned, far):
        return [
            products(turned, r, ((3,), (4,)), (((from_y, 0),), ((from_x, 0),)))
            for r, (from_x, from_y) in zip(blocks_of_four, far)
        ]

    def send(messages, x=2, y=4):
        return [[swap(to_x, x), swap(to_y, y)] for to_x, to_y in messages]

    def scatter_end(turned, early, unit, late):
        def own(r, turn):
            (early_x, early_y), (late_x, late_y) = early[r // 8], late[r // 8]
            addends = (((early_x, unit), (late_y, 0)), ((early_y, unit), (late_x, 0)))
            return products(turned, r, ((0,), (1,)), addends, turn)

        if n_dp == 8:
            return own(0, True)
        totals = {r: own(r, False) for r in blocks_of_four}
        bit = n_dp // 2
        while bit >= 8:
            for r in [r for r in totals if r < bit]:
                passed = [swap(total, bit) for total in totals.pop(r ^ bit)]
                totals[r] = [
                    (a.astype(F32) + b.astype(F32)).astype(BF) for a, b in zip(totals[r], passed)
                ]
            bit //= 2
        return [total.T for total in totals[0]]

    held_value, turned_value = together(held_value, turned_value)
    pieces = {r ^ f: part[f * rows : (f + 1) * rows] for r, part in held_value.items() for f in (0, 1)}
    relayed = [r ^ f for r in blocks_of_four for f in (2, 5)]
    pieces.update(zip(relayed, together(*[pieces[r] for r in relayed])))
    held_value = gather_rest(pieces)
    first_value = send(messages(turned_value, (6, 2), (7, 5)))
    full_value = whole(held_value)
    values = jnp.dot(normed, full_value, preferred_element_type=F32).astype(BF)
    turned_pair = attention_call(rest_kernel, (pair, grad_out, values), gains, 2 * cols)

    def back_odd(step, turned_pair, turned_value):
        at = level_at(step + 1) * own
        chosen = [
            jnp.concatenate(
                [lax.dynamic_slice_in_dim(turned, g * group + at, own, 1) for g in range(2)], axis=1
            )
            for turned in (turned_pair, turned_value)
        ]
        return chosen, back_call(*chosen, full_pair, full_value, rows, True, (), BF)

    def back_even(chosen, passed, dtype):
        return back_call(*chosen, full_pair, full_value, rows, False, (passed,), dtype)

    chosen, sent, partial = {}, {}, {}
    chosen[0], sent[0] = back_odd(0, turned_pair, turned_value)
    chosen[1], sent[1] = back_odd(1, turned_pair, turned_value)
    late_value = late_messages(turned_value, first_value)
    late_value, sent = together(late_value, sent)
    late_value = send(late_value)
    passed = {step: swap(sent[step], 1) for step in range(2)}
    far_pair = messages(turned_pair, (6,), (7,))
    far_pair, passed = together(far_pair, passed)
    message = back_even(chosen[0], passed[0], BF)
    message, far_pair, turned_pair, turned_value = together(message, far_pair, turned_pair, turned_value)
    arrived, far_pair = ring_on(message), send(far_pair)

    turned_pair, turned_value, late_value = together(turned_pair, turned_value, late_value)
    for step in range(2, 4):
        chosen[step], sent[step] = back_odd(step, turned_pair, turned_value)
    ends_value = scatter_end(turned_value, first_value, 1, late_value)
    partial[1] = back_even(chosen[1], passed[1], BF)
    early_pair = messages(turned_pair, (2,), (5,))
    for step in range(1, n_mp - 1):
        if step == 1:
            partial[1], early_pair, sent, far_pair, ends_value = together(
                partial[1], early_pair, sent, far_pair, ends_value
            )
        elif step == 2:
            partial[2], late_pair, early_pair, own_pair = together(
                partial[2], late_pair, early_pair, own_pair
            )
        message = (partial[step].astype(F32) + arrived.astype(F32)).astype(BF)
        if step == 1:
            message, early_pair, sent, turned_pair, turned_value = together(
                message, early_pair, sent, turned_pair, turned_value
            )
            early_pair = send(early_pair, y=5)
        elif step == 2:
            message, late_pair, own_pair, ends_value = together(
                message, late_pair, own_pair, ends_value
            )
            late_pair = send(late_pair, x=3)
            own_pair = [[even, swap(odd, 1)] for even, odd in own_pair]
            passed_value = swap(ends_value[1], 1)
        arrived = ring_on(message)
        if step + 2 < n_mp:
            near = [step + 1, step + 2] if step + 3 == n_mp else [step + 1]
            for level_step in near:
                passed[level_step] = swap(sent[level_step], 1)
            here = [passed[level_step] for level_step in near]
            turned_pair, turned_value, here = together(turned_pair, turned_value, here)
            passed.update(zip(near, here))
            for level_step in near:
                dtype = F32 if level_step == n_mp - 1 else BF
                partial[level_step] = back_even(chosen[level_step], passed[level_step], dtype)
            if step + 3 == n_mp:
                partial[n_mp - 2], partial[n_mp - 1] = together(partial[n_mp - 2], partial[n_mp - 1])
            else:
                chosen[step + 3], sent[step + 3] = back_odd(step + 3, turned_pair, turned_value)
            if step == 1:
                late_pair = late_messages(turned_pair, far_pair)
                own_pair = messages(turned_pair, (0,), (1,))
    out_value = place_call(core, ends_value[0], passed_value, cols, 0)
    arrived, out_value = together(arrived, out_value)
    total = partial[n_mp - 1] + arrived.astype(F32)

    mine = lax.dynamic_slice_in_dim(total, core * own, own, 1)
    other = lax.dynamic_slice_in_dim(total, (1 - core) * own, own, 1).astype(BF)
    other = swap(other, 1)

    here, there = {}, {}
    for r, (own_even, own_odd), early, late in zip(blocks_of_four, own_pair, early_pair, late_pair):
        here[r] = [own_even, early[0], late[1]]
        there[r] = [own_odd, early[1], late[0]]
    bit = n_dp // 2
    while bit >= 8:
        for parts in (here, there):
            for r in [r for r in parts if r >= bit]:
                parts[r ^ bit].append(swap(sum(p.astype(F32) for p in parts.pop(r)).astype(BF), bit))
        bit //= 2
    out_query, out_key = gather_call(core, here[0], there[0], cols)
    other, out_query, out_key = together(other, out_query, out_key)
    grad_tokens = finish_call(place, mine, other, unit_rows, row_spread, norm_gain, rows)
    return (grad_tokens, out_query, out_key, out_value)


def solution(mesh):
    matrix = P("dp", "mp")
    token_rows = P(("dp", "mp"), None)
    return jax.shard_map(
        functools.partial(per_device, mesh.shape["dp"], mesh.shape["mp"]),
        mesh=mesh,
        in_specs=(token_rows, P(), P(), P(), matrix, matrix, matrix, matrix),
        out_specs=(token_rows, matrix, matrix, matrix),
        check_vma=False,
    )
```

```python
import functools

import jax
import jax.numpy as jnp
from jax import lax
from jax.experimental import pallas as pl
from jax.experimental.pallas import tpu as pltpu
from jax.sharding import PartitionSpec as P

PATCH = 256
BF = jnp.bfloat16
F32 = jnp.float32


def normalize(row_data, gain_vector):
    average = jnp.mean(row_data, axis=-1, keepdims=True)
    centred = row_data - average
    inv_spread = lax.rsqrt(jnp.mean(centred * centred, axis=-1, keepdims=True) + 1e-06)
    unit_data = centred * inv_spread
    return (unit_data * gain_vector, unit_data, inv_spread)


def normalize_back(grad_out, unit_data, inv_spread, gain_vector):
    scaled = grad_out * gain_vector
    inner_term = jnp.mean(scaled * unit_data, axis=-1, keepdims=True)
    return (scaled - jnp.mean(scaled, axis=-1, keepdims=True) - unit_data * inner_term) * inv_spread


def dot_nt(a, b):
    return lax.dot_general(a, b, (((1,), (1,)), ((), ())), preferred_element_type=F32)


def dot_tn(a, b):
    return lax.dot_general(a, b, (((0,), (0,)), ((), ())), preferred_element_type=F32)


def params(mib):
    return pltpu.CompilerParams(vmem_limit_bytes=mib * 2**20)


def cost(flops, bytes_accessed):
    return pl.CostEstimate(flops=flops // 6, bytes_accessed=bytes_accessed // 6, transcendentals=0)


def blank(shape, dtype):
    return pl.pallas_call(
        lambda out_ref: None,
        out_shape=jax.ShapeDtypeStruct(shape, dtype),
        out_specs=pl.BlockSpec(memory_space=pl.ANY),
    )()


def attention_of(query_bf, key_bf):
    scores = dot_nt(key_bf, query_bf) * query_bf.shape[-1] ** (-0.5)
    raised = jnp.exp(scores - jnp.max(scores, axis=0, keepdims=True))
    return raised * (1.0 / jnp.sum(raised, axis=0, keepdims=True))


def first_kernel(qk_ref, g_ref, gains_ref, turned_ref):
    head, cols = gains_ref.shape[1], g_ref.shape[1]
    for h in range(cols // head):
        at, key_at = pl.ds(h * head, head), pl.ds(cols + h * head, head)
        query_bf = normalize(qk_ref[:, at], gains_ref[0:1])[0].astype(BF)
        key_bf = normalize(qk_ref[:, key_at], gains_ref[1:2])[0].astype(BF)
        attention = attention_of(query_bf, key_bf).astype(BF)
        grad_value = jnp.dot(attention, g_ref[:, at], preferred_element_type=F32)
        turned_ref[at, :] = grad_value.T.astype(BF)


def rest_kernel(qk_ref, g_ref, v_ref, gains_ref, turned_ref):
    head, cols = gains_ref.shape[1], g_ref.shape[1]
    factor = head ** (-0.5)
    q_gain, k_gain = gains_ref[0:1], gains_ref[1:2]
    for h in range(cols // head):
        at, key_at = pl.ds(h * head, head), pl.ds(cols + h * head, head)
        query_normed, query_unit, query_spread = normalize(qk_ref[:, at], q_gain)
        key_normed, key_unit, key_spread = normalize(qk_ref[:, key_at], k_gain)
        query_bf, key_bf = query_normed.astype(BF), key_normed.astype(BF)
        attention = attention_of(query_bf, key_bf)
        grad_probs = dot_nt(v_ref[:, at], g_ref[:, at])
        delta = jnp.sum(attention * grad_probs, axis=0, keepdims=True)
        grad_scores = (attention * (grad_probs - delta) * factor).astype(BF)
        grad_kn = jnp.dot(grad_scores, query_bf, preferred_element_type=F32)
        grad_qn = dot_tn(grad_scores, key_bf)
        grad_query = normalize_back(grad_qn, query_unit, query_spread, q_gain)
        grad_key = normalize_back(grad_kn, key_unit, key_spread, k_gain)
        turned_ref[at, :] = grad_query.T.astype(BF)
        turned_ref[key_at, :] = grad_key.T.astype(BF)


def attention_call(kernel, arrays, gains, out_rows):
    tokens, columns = arrays[1].shape
    head = gains.shape[-1]
    pairs = (tokens // PATCH) * (columns // head)
    return pl.pallas_call(
        kernel,
        grid=(tokens // PATCH,),
        in_specs=[pl.BlockSpec((PATCH, array.shape[1]), lambda i: (i, 0)) for array in arrays]
        + [pl.BlockSpec(gains.shape, lambda i: (0, 0))],
        out_specs=pl.BlockSpec((out_rows, PATCH), lambda i: (0, i)),
        out_shape=jax.ShapeDtypeStruct((out_rows, tokens), BF),
        compiler_params=params(12),
        cost_estimate=cost(pairs * 8 * PATCH * PATCH * head, 4 * len(arrays) * arrays[0].size),
    )(*arrays, gains)


def product_kernel(n_add, turn, turned_ref, *refs):
    turned = turned_ref[...]
    outs = refs[-2:]
    for side in range(2):
        total = jnp.dot(turned, refs[side][...], preferred_element_type=F32)
        for ref in refs[2 + side * n_add : 2 + (side + 1) * n_add]:
            total = total + ref[...].astype(F32)
        outs[side][...] = (total.T if turn else total).astype(BF)


def product_call(turned, normed, rows, units, addends=((), ()), turn=False):
    columns, tokens = turned.shape
    tile = 256 if rows % 256 == 0 else 128
    count, n_add, steps = len(units[0]), len(addends[0]), rows // tile

    def side(first, last):
        return pl.BlockSpec((tokens, tile), lambda u, i: (0, (first + u * (last - first)) * steps + i))

    def added(which):
        return pl.BlockSpec((columns, tile), lambda u, i: (which, i))

    if turn:
        shape, out = (rows, columns), pl.BlockSpec((tile, columns), lambda u, i: (i, 0))
    else:
        shape, out = (count * columns, rows), pl.BlockSpec((columns, tile), lambda u, i: (u, i))
    addends = [*addends[0], *addends[1]]
    return pl.pallas_call(
        functools.partial(product_kernel, n_add, turn),
        grid=(count, steps),
        in_specs=[
            pl.BlockSpec((columns, tokens), lambda u, i: (0, 0)),
            *[side(chosen[0], chosen[-1]) for chosen in units],
            *[added(which) for _, which in addends],
        ],
        out_specs=[out] * 2,
        out_shape=[jax.ShapeDtypeStruct(shape, BF)] * 2,
        compiler_params=params(14),
        cost_estimate=cost(
            4 * count * columns * tokens * rows,
            2 * columns * tokens + 4 * count * tokens * rows + (4 + 4 * n_add) * columns * rows,
        ),
    )(turned, normed, normed, *[array for array, _ in addends])


def back_kernel(pair_ref, value_ref, w_pair_ref, w_value_ref, *refs):
    total = jnp.dot(w_pair_ref[...], pair_ref[...], preferred_element_type=F32)
    total = total + jnp.dot(w_value_ref[...], value_ref[...], preferred_element_type=F32)
    for ref in refs[:-1]:
        total = total + ref[...].astype(F32)
    refs[-1][...] = total.astype(refs[-1].dtype)


def back_call(pair, value, w_pair, w_value, rows, odd, addends, dtype):
    level_tokens = pair.shape[1]
    units = w_pair.shape[0] // rows // 2
    first = units if odd else 0
    block = pl.BlockSpec((rows, level_tokens), lambda i: (i, 0))
    return pl.pallas_call(
        back_kernel,
        grid=(units,),
        in_specs=[
            pl.BlockSpec(pair.shape, lambda i: (0, 0)),
            pl.BlockSpec(value.shape, lambda i: (0, 0)),
            pl.BlockSpec((rows, w_pair.shape[1]), lambda i: (first + i, 0)),
            pl.BlockSpec((rows, w_value.shape[1]), lambda i: (first + i, 0)),
        ]
        + [block] * len(addends),
        out_specs=block,
        out_shape=jax.ShapeDtypeStruct((units * rows, level_tokens), dtype),
        compiler_params=params(11),
        cost_estimate=cost(
            2 * units * rows * level_tokens * (pair.shape[0] + value.shape[0]),
            2 * units * rows * (pair.shape[0] + value.shape[0] + 3 * level_tokens),
        ),
    )(pair, value, w_pair, w_value, *addends)


def gather_kernel(cols, n_parts, core_ref, *refs):
    parts, outs = refs[: 2 * n_parts], refs[2 * n_parts :]
    here = pl.program_id(0) == core_ref[0]

    def store(blocks):
        total = blocks[0][...].astype(F32)
        for block in blocks[1:]:
            total = total + block[...].astype(F32)
        for k, out in enumerate(outs):
            out[...] = total[k * cols : (k + 1) * cols].T.astype(BF)

    @pl.when(here)
    def _():
        store(parts[:n_parts])

    @pl.when(jnp.logical_not(here))
    def _():
        store(parts[n_parts:])


def gather_call(core, mine, other, cols):
    columns, rows = mine[0].shape
    tile = 256 if rows % 256 == 0 else 128
    here = pl.BlockSpec(
        (columns, tile), lambda h, i, core_ref: (0, jnp.where(h == core_ref[0], i, rows // tile * h - h))
    )
    there = pl.BlockSpec(
        (columns, tile), lambda h, i, core_ref: (0, jnp.where(h != core_ref[0], i, rows // tile * h - h))
    )
    return pl.pallas_call(
        functools.partial(gather_kernel, cols, len(mine)),
        grid_spec=pltpu.PrefetchScalarGridSpec(
            num_scalar_prefetch=1,
            grid=(2, rows // tile),
            in_specs=[here] * len(mine) + [there] * len(other),
            out_specs=[pl.BlockSpec((tile, cols), lambda h, i, core_ref: (i, h))] * (columns // cols),
        ),
        out_shape=[jax.ShapeDtypeStruct((rows, 2 * cols), BF)] * (columns // cols),
        compiler_params=params(40),
    )(core.reshape(1), *mine, *other)


def place_kernel(core_ref, mine_ref, other_ref, out_ref):
    here = pl.program_id(0) == core_ref[0]

    @pl.when(here)
    def _():
        out_ref[...] = mine_ref[...]

    @pl.when(jnp.logical_not(here))
    def _():
        out_ref[...] = other_ref[...]


def place_call(core, mine, other, cols, part):
    rows = mine.shape[0]
    block = pl.BlockSpec((rows, cols), lambda i, core_ref: (0, part))
    return pl.pallas_call(
        place_kernel,
        grid_spec=pltpu.PrefetchScalarGridSpec(
            num_scalar_prefetch=1,
            grid=(2,),
            in_specs=[block, block],
            out_specs=pl.BlockSpec((rows, cols), lambda i, core_ref: (0, i)),
        ),
        out_shape=jax.ShapeDtypeStruct((rows, 2 * cols), BF),
        compiler_params=params(12),
    )(core.reshape(1), mine, other)


def finish_kernel(rows, n_dp, place_ref, mine_ref, other_ref, unit_ref, spread_ref, gain_ref, out_ref, held):
    n_chips = n_dp // 2
    held[: n_chips * rows] = mine_ref[...]
    held[n_chips * rows :] = other_ref[...].astype(F32)
    place = place_ref[0]
    columns = []
    total, inner = 0.0, 0.0
    for b in range(n_dp):
        r = b ^ place
        unit = (r & 1) * n_chips + (r >> 1)
        at = pl.ds(b * rows, rows)
        grad = held[pl.ds(pl.multiple_of(unit * rows, rows), rows), :].T
        scaled = grad * gain_ref[:, at]
        total = total + jnp.sum(scaled, axis=-1, keepdims=True)
        inner = inner + jnp.sum(scaled * unit_ref[:, at], axis=-1, keepdims=True)
        columns.append(scaled)
    average, inner = total * (1.0 / (n_dp * rows)), inner * (1.0 / (n_dp * rows))
    for b in range(n_dp):
        at = pl.ds(b * rows, rows)
        result = (columns[b] - average - unit_ref[:, at] * inner) * spread_ref[...]
        out_ref[:, at] = result.astype(BF)


def finish_call(place, mine, other, unit_rows, row_spread, norm_gain, rows):
    own, width = unit_rows.shape
    vmem = pl.BlockSpec(memory_space=pltpu.VMEM)
    return pl.pallas_call(
        functools.partial(finish_kernel, rows, width // rows),
        in_specs=[pl.BlockSpec(memory_space=pltpu.SMEM)] + [vmem] * 5,
        out_specs=vmem,
        out_shape=jax.ShapeDtypeStruct((own, width), BF),
        scratch_shapes=[pltpu.VMEM((width, own), F32)],
        compiler_params=params(20),
    )(place.reshape(1), mine, other, unit_rows, row_spread, norm_gain.reshape(1, width))


def per_device(n_dp, n_mp, tokens, norm_gain, q_gain, k_gain, w_query, w_key, w_value, grad_heads):
    own, width = tokens.shape
    rows, cols = w_query.shape[0], w_query.shape[1] // 2
    n_chips = n_dp // 2
    group = n_mp * own
    place = lax.axis_index("dp")
    core = place & 1

    def swap(array, bit):
        return lax.ppermute(array, "dp", [(i, i ^ bit) for i in range(n_dp)])

    def half(array, which):
        return lax.dynamic_slice_in_dim(array, which * cols, cols, 1)

    def together(*arrays):
        return lax.optimization_barrier(arrays)

    ring = list(range(0, n_mp, 2)) + list(range(n_mp - 1, 0, -2))
    level = lax.axis_index("mp")
    spot = jnp.where(level & 1 == 0, level >> 1, n_mp - 1 - (level >> 1))
    ring_pairs = [(ring[i], ring[(i + 1) % n_mp]) for i in range(n_mp)]

    def level_at(back):
        at = lax.rem(spot + 2 * n_mp - back, n_mp)
        return jnp.where(at < n_mp // 2, 2 * at, 2 * (n_mp - 1 - at) + 1)

    def ring_on(array):
        return lax.ppermute(array, "mp", ring_pairs)

    def unit_of(r):
        return (r & 1) * n_chips + (r >> 1)

    def feature_block(array, r):
        return lax.dynamic_slice_in_dim(array, (place ^ r) * rows, rows, 1)

    def columns_of(weights, which):
        return jnp.concatenate([half(w, which) for w in weights], axis=1)

    def gather_start(held):
        held = dict(held)
        bit = 8
        while bit < n_dp:
            held.update({r ^ bit: swap(part, bit) for r, part in list(held.items())})
            bit *= 2
        for r, part in list(held.items()):
            held[r ^ 2] = swap(part, 2)
            held[r ^ 4] = swap(part, 4)
        return held

    def gather_rest(held):
        held = dict(held)
        for r in range(0, n_dp, 8):
            held[r ^ 6] = swap(held[r ^ 2], 4)
            held[r ^ 7] = swap(held[r ^ 5], 2)
        return held

    def whole(held):
        return jnp.concatenate([held[r] for r in (*range(0, n_dp, 2), *range(1, n_dp, 2))], axis=0)

    pair_weights = (w_query, w_key)
    own_pair, sent_pair = columns_of(pair_weights, core), columns_of(pair_weights, 1 - core)
    tokens, own_pair, sent_pair = together(tokens, own_pair, sent_pair)
    held_pair = gather_start({0: own_pair})
    other_pair = swap(sent_pair, 1)

    normed_own, unit_rows, row_spread = normalize(tokens.astype(F32), norm_gain)
    normed_own = normed_own.astype(BF)
    even = jnp.concatenate([feature_block(normed_own, r) for r in range(0, n_dp, 2)], axis=1)
    odd = jnp.concatenate([feature_block(normed_own, r) for r in range(1, n_dp, 2)], axis=1)
    block = jnp.concatenate([even, swap(odd, 1)], axis=0)

    normed = blank((2 * group, width), BF)

    def put(normed, block, step):
        beside = swap(block, 1)
        start = level_at(step) * own
        mine, other = core * group + start, (1 - core) * group + start
        for piece, at, column in (
            (block[:own], mine, 0),
            (block[own:], other, 0),
            (beside[:own], other, width // 2),
            (beside[own:], mine, width // 2),
        ):
            normed = lax.dynamic_update_slice(normed, piece, (at, column))
        return normed

    held_pair, normed = together(held_pair, normed)
    held_pair.update(gather_start({1: other_pair}))
    normed = put(normed, block, 0)
    for step in range(1, n_mp):
        block = ring_on(block)
        normed = put(normed, block, step)
        if step == 1:
            held_pair, normed, w_value, grad_heads = together(held_pair, normed, w_value, grad_heads)
            held_pair = gather_rest(held_pair)
            shard_value = [half(w_value, core), swap(half(w_value, 1 - core), 1)]
            shard_value = jnp.concatenate(shard_value, axis=0)
            grads_mine, grads_other = half(grad_heads, core), swap(half(grad_heads, 1 - core), 1)
        elif step == 2:
            shard_value, normed = together(shard_value, normed)
            held_value = gather_start({0: shard_value})

    grad_out = blank((2 * group, cols), BF)
    grad_out = lax.dynamic_update_slice_in_dim(grad_out, grads_mine, core * group, 0)
    grad_out = lax.dynamic_update_slice_in_dim(grad_out, grads_other, (1 - core) * group, 0)
    gains = jnp.stack([q_gain, k_gain])

    full_pair = whole(held_pair)
    pair = jnp.dot(normed, full_pair, preferred_element_type=F32)
    turned_value = attention_call(first_kernel, (pair, grad_out), gains, cols)

    def products(turned, r, offsets, addends=((), ()), turn=False):
        units = [[unit_of(r ^ f) for f in side] for side in offsets]
        return product_call(turned, normed, rows, units, addends, turn)

    blocks_of_four = range(0, n_dp, 8)

    def messages(turned, to_x, to_y):
        return [products(turned, r, (to_x, to_y)) for r in blocks_of_four]

    def late_messages(turned, far):
        return [
            products(turned, r, ((3,), (4,)), (((from_y, 0),), ((from_x, 0),)))
            for r, (from_x, from_y) in zip(blocks_of_four, far)
        ]

    def send(messages, x=2, y=4):
        return [[swap(to_x, x), swap(to_y, y)] for to_x, to_y in messages]

    def scatter_end(turned, early, unit, late):
        def own(r, turn):
            (early_x, early_y), (late_x, late_y) = early[r // 8], late[r // 8]
            addends = (((early_x, unit), (late_y, 0)), ((early_y, unit), (late_x, 0)))
            return products(turned, r, ((0,), (1,)), addends, turn)

        if n_dp == 8:
            return own(0, True)
        totals = {r: own(r, False) for r in blocks_of_four}
        bit = n_dp // 2
        while bit >= 8:
            for r in [r for r in totals if r < bit]:
                passed = [swap(total, bit) for total in totals.pop(r ^ bit)]
                totals[r] = [
                    (a.astype(F32) + b.astype(F32)).astype(BF) for a, b in zip(totals[r], passed)
                ]
            bit //= 2
        return [total.T for total in totals[0]]

    held_value, turned_value = together(held_value, turned_value)
    pieces = {r ^ f: part[f * rows : (f + 1) * rows] for r, part in held_value.items() for f in (0, 1)}
    relayed = [r ^ f for r in blocks_of_four for f in (2, 5)]
    pieces.update(zip(relayed, together(*[pieces[r] for r in relayed])))
    held_value = gather_rest(pieces)
    first_value = send(messages(turned_value, (6, 2), (7, 5)))
    full_value = whole(held_value)
    values = jnp.dot(normed, full_value, preferred_element_type=F32).astype(BF)
    turned_pair = attention_call(rest_kernel, (pair, grad_out, values), gains, 2 * cols)

    def back_odd(step, turned_pair, turned_value):
        at = level_at(step + 1) * own
        chosen = [
            jnp.concatenate(
                [lax.dynamic_slice_in_dim(turned, g * group + at, own, 1) for g in range(2)], axis=1
            )
            for turned in (turned_pair, turned_value)
        ]
        return chosen, back_call(*chosen, full_pair, full_value, rows, True, (), BF)

    def back_even(chosen, passed, dtype):
        return back_call(*chosen, full_pair, full_value, rows, False, (passed,), dtype)

    chosen, sent, partial = {}, {}, {}
    chosen[0], sent[0] = back_odd(0, turned_pair, turned_value)
    chosen[1], sent[1] = back_odd(1, turned_pair, turned_value)
    late_value = late_messages(turned_value, first_value)
    late_value, sent = together(late_value, sent)
    late_value = send(late_value)
    passed = {step: swap(sent[step], 1) for step in range(2)}
    far_pair = messages(turned_pair, (6,), (7,))
    far_pair, passed = together(far_pair, passed)
    message = back_even(chosen[0], passed[0], BF)
    message, far_pair, turned_pair, turned_value = together(message, far_pair, turned_pair, turned_value)
    arrived, far_pair = ring_on(message), send(far_pair)

    turned_pair, turned_value, late_value = together(turned_pair, turned_value, late_value)
    for step in range(2, 4):
        chosen[step], sent[step] = back_odd(step, turned_pair, turned_value)
    ends_value = scatter_end(turned_value, first_value, 1, late_value)
    partial[1] = back_even(chosen[1], passed[1], BF)
    early_pair = messages(turned_pair, (2,), (5,))
    for step in range(1, n_mp - 1):
        if step == 1:
            partial[1], early_pair, sent, far_pair, ends_value = together(
                partial[1], early_pair, sent, far_pair, ends_value
            )
        elif step == 2:
            partial[2], late_pair, early_pair, own_pair = together(
                partial[2], late_pair, early_pair, own_pair
            )
        message = (partial[step].astype(F32) + arrived.astype(F32)).astype(BF)
        if step == 1:
            message, early_pair, sent, turned_pair, turned_value = together(
                message, early_pair, sent, turned_pair, turned_value
            )
            early_pair = send(early_pair, y=5)
        elif step == 2:
            message, late_pair, own_pair, ends_value = together(
                message, late_pair, own_pair, ends_value
            )
            late_pair = send(late_pair, x=3)
            own_pair = [[even, swap(odd, 1)] for even, odd in own_pair]
            passed_value = swap(ends_value[1], 1)
        arrived = ring_on(message)
        if step + 2 < n_mp:
            near = [step + 1, step + 2] if step + 3 == n_mp else [step + 1]
            for level_step in near:
                passed[level_step] = swap(sent[level_step], 1)
            here = [passed[level_step] for level_step in near]
            turned_pair, turned_value, here = together(turned_pair, turned_value, here)
            passed.update(zip(near, here))
            for level_step in near:
                dtype = F32 if level_step == n_mp - 1 else BF
                partial[level_step] = back_even(chosen[level_step], passed[level_step], dtype)
            if step + 3 == n_mp:
                partial[n_mp - 2], partial[n_mp - 1] = together(partial[n_mp - 2], partial[n_mp - 1])
            else:
                chosen[step + 3], sent[step + 3] = back_odd(step + 3, turned_pair, turned_value)
            if step == 1:
                late_pair = late_messages(turned_pair, far_pair)
                own_pair = messages(turned_pair, (0,), (1,))
    out_value = place_call(core, ends_value[0], passed_value, cols, 0)
    here, there = {}, {}
    for r, (own_even, own_odd), (even_x, odd_y) in zip(blocks_of_four, own_pair, early_pair):
        here[r] = (own_even.astype(F32) + even_x.astype(F32)).astype(BF)
        there[r] = (own_odd.astype(F32) + odd_y.astype(F32)).astype(BF)
    arrived, out_value, here, there = together(arrived, out_value, here, there)
    total = partial[n_mp - 1] + arrived.astype(F32)

    mine = lax.dynamic_slice_in_dim(total, core * own, own, 1)
    other = lax.dynamic_slice_in_dim(total, (1 - core) * own, own, 1).astype(BF)
    other = swap(other, 1)

    for r, (odd_x, even_y) in zip(blocks_of_four, late_pair):
        here[r], there[r] = [here[r], even_y], [there[r], odd_x]
    bit = n_dp // 2
    while bit >= 8:
        for parts in (here, there):
            for r in [r for r in parts if r >= bit]:
                parts[r ^ bit].append(swap(sum(p.astype(F32) for p in parts.pop(r)).astype(BF), bit))
        bit //= 2
    out_query, out_key = gather_call(core, here[0], there[0], cols)
    other, out_query, out_key = together(other, out_query, out_key)
    grad_tokens = finish_call(place, mine, other, unit_rows, row_spread, norm_gain, rows)
    return (grad_tokens, out_query, out_key, out_value)


def solution(mesh):
    matrix = P("dp", "mp")
    token_rows = P(("dp", "mp"), None)
    return jax.shard_map(
        functools.partial(per_device, mesh.shape["dp"], mesh.shape["mp"]),
        mesh=mesh,
        in_specs=(token_rows, P(), P(), P(), matrix, matrix, matrix, matrix),
        out_specs=(token_rows, matrix, matrix, matrix),
        check_vma=False,
    )
```

```python
import functools

import jax
import jax.numpy as jnp
from jax import lax
from jax.experimental import pallas as pl
from jax.experimental.pallas import tpu as pltpu
from jax.sharding import PartitionSpec as P

PATCH = 256
BF = jnp.bfloat16
F32 = jnp.float32


def normalize(row_data, gain_vector):
    average = jnp.mean(row_data, axis=-1, keepdims=True)
    centred = row_data - average
    inv_spread = lax.rsqrt(jnp.mean(centred * centred, axis=-1, keepdims=True) + 1e-06)
    unit_data = centred * inv_spread
    return (unit_data * gain_vector, unit_data, inv_spread)


def normalize_back(grad_out, unit_data, inv_spread, gain_vector):
    scaled = grad_out * gain_vector
    inner_term = jnp.mean(scaled * unit_data, axis=-1, keepdims=True)
    return (scaled - jnp.mean(scaled, axis=-1, keepdims=True) - unit_data * inner_term) * inv_spread


def dot_nt(a, b):
    return lax.dot_general(a, b, (((1,), (1,)), ((), ())), preferred_element_type=F32)


def dot_tn(a, b):
    return lax.dot_general(a, b, (((0,), (0,)), ((), ())), preferred_element_type=F32)


def params(mib):
    return pltpu.CompilerParams(vmem_limit_bytes=mib * 2**20)


def cost(flops, bytes_accessed):
    return pl.CostEstimate(flops=flops // 6, bytes_accessed=bytes_accessed // 6, transcendentals=0)


def blank(shape, dtype):
    return pl.pallas_call(
        lambda out_ref: None,
        out_shape=jax.ShapeDtypeStruct(shape, dtype),
        out_specs=pl.BlockSpec(memory_space=pl.ANY),
    )()


def attention_of(query_bf, key_bf):
    scores = dot_nt(key_bf, query_bf) * query_bf.shape[-1] ** (-0.5)
    raised = jnp.exp(scores - jnp.max(scores, axis=0, keepdims=True))
    return raised * (1.0 / jnp.sum(raised, axis=0, keepdims=True))


def first_kernel(qk_ref, g_ref, gains_ref, turned_ref):
    head, cols = gains_ref.shape[1], g_ref.shape[1]
    for h in range(cols // head):
        at, key_at = pl.ds(h * head, head), pl.ds(cols + h * head, head)
        query_bf = normalize(qk_ref[:, at], gains_ref[0:1])[0].astype(BF)
        key_bf = normalize(qk_ref[:, key_at], gains_ref[1:2])[0].astype(BF)
        attention = attention_of(query_bf, key_bf).astype(BF)
        grad_value = jnp.dot(attention, g_ref[:, at], preferred_element_type=F32)
        turned_ref[at, :] = grad_value.T.astype(BF)


def rest_kernel(qk_ref, g_ref, v_ref, gains_ref, turned_ref):
    head, cols = gains_ref.shape[1], g_ref.shape[1]
    factor = head ** (-0.5)
    q_gain, k_gain = gains_ref[0:1], gains_ref[1:2]
    for h in range(cols // head):
        at, key_at = pl.ds(h * head, head), pl.ds(cols + h * head, head)
        query_normed, query_unit, query_spread = normalize(qk_ref[:, at], q_gain)
        key_normed, key_unit, key_spread = normalize(qk_ref[:, key_at], k_gain)
        query_bf, key_bf = query_normed.astype(BF), key_normed.astype(BF)
        attention = attention_of(query_bf, key_bf)
        grad_probs = dot_nt(v_ref[:, at], g_ref[:, at])
        delta = jnp.sum(attention * grad_probs, axis=0, keepdims=True)
        grad_scores = (attention * (grad_probs - delta) * factor).astype(BF)
        grad_kn = jnp.dot(grad_scores, query_bf, preferred_element_type=F32)
        grad_qn = dot_tn(grad_scores, key_bf)
        grad_query = normalize_back(grad_qn, query_unit, query_spread, q_gain)
        grad_key = normalize_back(grad_kn, key_unit, key_spread, k_gain)
        turned_ref[at, :] = grad_query.T.astype(BF)
        turned_ref[key_at, :] = grad_key.T.astype(BF)


def attention_call(kernel, arrays, gains, out_rows):
    tokens, columns = arrays[1].shape
    head = gains.shape[-1]
    pairs = (tokens // PATCH) * (columns // head)
    return pl.pallas_call(
        kernel,
        grid=(tokens // PATCH,),
        in_specs=[pl.BlockSpec((PATCH, array.shape[1]), lambda i: (i, 0)) for array in arrays]
        + [pl.BlockSpec(gains.shape, lambda i: (0, 0))],
        out_specs=pl.BlockSpec((out_rows, PATCH), lambda i: (0, i)),
        out_shape=jax.ShapeDtypeStruct((out_rows, tokens), BF),
        compiler_params=params(12),
        cost_estimate=cost(pairs * 8 * PATCH * PATCH * head, 4 * len(arrays) * arrays[0].size),
    )(*arrays, gains)


def product_kernel(n_add, turn, turned_ref, *refs):
    turned = turned_ref[...]
    outs = refs[-2:]
    for side in range(2):
        total = jnp.dot(turned, refs[side][...], preferred_element_type=F32)
        for ref in refs[2 + side * n_add : 2 + (side + 1) * n_add]:
            total = total + ref[...].astype(F32)
        outs[side][...] = (total.T if turn else total).astype(BF)


def product_call(turned, normed, rows, units, addends=((), ()), turn=False):
    columns, tokens = turned.shape
    tile = 256 if rows % 256 == 0 else 128
    count, n_add, steps = len(units[0]), len(addends[0]), rows // tile

    def side(first, last):
        return pl.BlockSpec((tokens, tile), lambda u, i: (0, (first + u * (last - first)) * steps + i))

    def added(which):
        return pl.BlockSpec((columns, tile), lambda u, i: (which, i))

    if turn:
        shape, out = (rows, columns), pl.BlockSpec((tile, columns), lambda u, i: (i, 0))
    else:
        shape, out = (count * columns, rows), pl.BlockSpec((columns, tile), lambda u, i: (u, i))
    addends = [*addends[0], *addends[1]]
    return pl.pallas_call(
        functools.partial(product_kernel, n_add, turn),
        grid=(count, steps),
        in_specs=[
            pl.BlockSpec((columns, tokens), lambda u, i: (0, 0)),
            *[side(chosen[0], chosen[-1]) for chosen in units],
            *[added(which) for _, which in addends],
        ],
        out_specs=[out] * 2,
        out_shape=[jax.ShapeDtypeStruct(shape, BF)] * 2,
        compiler_params=params(14),
        cost_estimate=cost(
            4 * count * columns * tokens * rows,
            2 * columns * tokens + 4 * count * tokens * rows + (4 + 4 * n_add) * columns * rows,
        ),
    )(turned, normed, normed, *[array for array, _ in addends])


def back_kernel(pair_ref, value_ref, w_pair_ref, w_value_ref, *refs):
    total = jnp.dot(w_pair_ref[...], pair_ref[...], preferred_element_type=F32)
    total = total + jnp.dot(w_value_ref[...], value_ref[...], preferred_element_type=F32)
    for ref in refs[:-1]:
        total = total + ref[...].astype(F32)
    refs[-1][...] = total.astype(refs[-1].dtype)


def back_call(pair, value, w_pair, w_value, rows, odd, addends, dtype):
    level_tokens = pair.shape[1]
    units = w_pair.shape[0] // rows // 2
    first = units if odd else 0
    block = pl.BlockSpec((rows, level_tokens), lambda i: (i, 0))
    return pl.pallas_call(
        back_kernel,
        grid=(units,),
        in_specs=[
            pl.BlockSpec(pair.shape, lambda i: (0, 0)),
            pl.BlockSpec(value.shape, lambda i: (0, 0)),
            pl.BlockSpec((rows, w_pair.shape[1]), lambda i: (first + i, 0)),
            pl.BlockSpec((rows, w_value.shape[1]), lambda i: (first + i, 0)),
        ]
        + [block] * len(addends),
        out_specs=block,
        out_shape=jax.ShapeDtypeStruct((units * rows, level_tokens), dtype),
        compiler_params=params(11),
        cost_estimate=cost(
            2 * units * rows * level_tokens * (pair.shape[0] + value.shape[0]),
            2 * units * rows * (pair.shape[0] + value.shape[0] + 3 * level_tokens),
        ),
    )(pair, value, w_pair, w_value, *addends)


def gather_kernel(cols, n_parts, core_ref, *refs):
    parts, outs = refs[: 2 * n_parts], refs[2 * n_parts :]
    here = pl.program_id(0) == core_ref[0]

    def store(blocks):
        total = blocks[0][...].astype(F32)
        for block in blocks[1:]:
            total = total + block[...].astype(F32)
        for k, out in enumerate(outs):
            out[...] = total[:, k * cols : (k + 1) * cols].astype(BF)

    @pl.when(here)
    def _():
        store(parts[:n_parts])

    @pl.when(jnp.logical_not(here))
    def _():
        store(parts[n_parts:])


def gather_call(core, mine, other, cols):
    rows, columns = mine[0].shape
    tile = 256 if rows % 256 == 0 else 128
    steps = rows // tile
    here = pl.BlockSpec(
        (tile, columns), lambda h, i, core_ref: (jnp.where(h == core_ref[0], i, steps * h - h), 0)
    )
    there = pl.BlockSpec(
        (tile, columns), lambda h, i, core_ref: (jnp.where(h != core_ref[0], i, steps * h - h), 0)
    )
    return pl.pallas_call(
        functools.partial(gather_kernel, cols, len(mine)),
        grid_spec=pltpu.PrefetchScalarGridSpec(
            num_scalar_prefetch=1,
            grid=(2, steps),
            in_specs=[here] * len(mine) + [there] * len(other),
            out_specs=[pl.BlockSpec((tile, cols), lambda h, i, core_ref: (i, h))] * (columns // cols),
        ),
        out_shape=[jax.ShapeDtypeStruct((rows, 2 * cols), BF)] * (columns // cols),
        compiler_params=params(60),
    )(core.reshape(1), *mine, *other)


def place_kernel(core_ref, mine_ref, other_ref, out_ref):
    here = pl.program_id(0) == core_ref[0]

    @pl.when(here)
    def _():
        out_ref[...] = mine_ref[...]

    @pl.when(jnp.logical_not(here))
    def _():
        out_ref[...] = other_ref[...]


def place_call(core, mine, other, cols, part):
    rows = mine.shape[0]
    block = pl.BlockSpec((rows, cols), lambda i, core_ref: (0, part))
    return pl.pallas_call(
        place_kernel,
        grid_spec=pltpu.PrefetchScalarGridSpec(
            num_scalar_prefetch=1,
            grid=(2,),
            in_specs=[block, block],
            out_specs=pl.BlockSpec((rows, cols), lambda i, core_ref: (0, i)),
        ),
        out_shape=jax.ShapeDtypeStruct((rows, 2 * cols), BF),
        compiler_params=params(12),
    )(core.reshape(1), mine, other)


def finish_kernel(rows, n_dp, place_ref, mine_ref, other_ref, unit_ref, spread_ref, gain_ref, out_ref, held):
    n_chips = n_dp // 2
    held[: n_chips * rows] = mine_ref[...]
    held[n_chips * rows :] = other_ref[...].astype(F32)
    place = place_ref[0]
    columns = []
    total, inner = 0.0, 0.0
    for b in range(n_dp):
        r = b ^ place
        unit = (r & 1) * n_chips + (r >> 1)
        at = pl.ds(b * rows, rows)
        grad = held[pl.ds(pl.multiple_of(unit * rows, rows), rows), :].T
        scaled = grad * gain_ref[:, at]
        total = total + jnp.sum(scaled, axis=-1, keepdims=True)
        inner = inner + jnp.sum(scaled * unit_ref[:, at], axis=-1, keepdims=True)
        columns.append(scaled)
    average, inner = total * (1.0 / (n_dp * rows)), inner * (1.0 / (n_dp * rows))
    for b in range(n_dp):
        at = pl.ds(b * rows, rows)
        result = (columns[b] - average - unit_ref[:, at] * inner) * spread_ref[...]
        out_ref[:, at] = result.astype(BF)


def finish_call(place, mine, other, unit_rows, row_spread, norm_gain, rows):
    own, width = unit_rows.shape
    vmem = pl.BlockSpec(memory_space=pltpu.VMEM)
    return pl.pallas_call(
        functools.partial(finish_kernel, rows, width // rows),
        in_specs=[pl.BlockSpec(memory_space=pltpu.SMEM)] + [vmem] * 5,
        out_specs=vmem,
        out_shape=jax.ShapeDtypeStruct((own, width), BF),
        scratch_shapes=[pltpu.VMEM((width, own), F32)],
        compiler_params=params(20),
    )(place.reshape(1), mine, other, unit_rows, row_spread, norm_gain.reshape(1, width))


def per_device(n_dp, n_mp, tokens, norm_gain, q_gain, k_gain, w_query, w_key, w_value, grad_heads):
    own, width = tokens.shape
    rows, cols = w_query.shape[0], w_query.shape[1] // 2
    n_chips = n_dp // 2
    group = n_mp * own
    place = lax.axis_index("dp")
    core = place & 1

    def swap(array, bit):
        return lax.ppermute(array, "dp", [(i, i ^ bit) for i in range(n_dp)])

    def half(array, which):
        return lax.dynamic_slice_in_dim(array, which * cols, cols, 1)

    def together(*arrays):
        return lax.optimization_barrier(arrays)

    ring = list(range(0, n_mp, 2)) + list(range(n_mp - 1, 0, -2))
    level = lax.axis_index("mp")
    spot = jnp.where(level & 1 == 0, level >> 1, n_mp - 1 - (level >> 1))
    ring_pairs = [(ring[i], ring[(i + 1) % n_mp]) for i in range(n_mp)]

    def level_at(back):
        at = lax.rem(spot + 2 * n_mp - back, n_mp)
        return jnp.where(at < n_mp // 2, 2 * at, 2 * (n_mp - 1 - at) + 1)

    def ring_on(array):
        return lax.ppermute(array, "mp", ring_pairs)

    def unit_of(r):
        return (r & 1) * n_chips + (r >> 1)

    def feature_block(array, r):
        return lax.dynamic_slice_in_dim(array, (place ^ r) * rows, rows, 1)

    def columns_of(weights, which):
        return jnp.concatenate([half(w, which) for w in weights], axis=1)

    def gather_start(held):
        held = dict(held)
        bit = 8
        while bit < n_dp:
            held.update({r ^ bit: swap(part, bit) for r, part in list(held.items())})
            bit *= 2
        for r, part in list(held.items()):
            held[r ^ 2] = swap(part, 2)
            held[r ^ 4] = swap(part, 4)
        return held

    def gather_rest(held):
        held = dict(held)
        for r in range(0, n_dp, 8):
            held[r ^ 6] = swap(held[r ^ 2], 4)
            held[r ^ 7] = swap(held[r ^ 5], 2)
        return held

    def whole(held):
        return jnp.concatenate([held[r] for r in (*range(0, n_dp, 2), *range(1, n_dp, 2))], axis=0)

    pair_weights = (w_query, w_key)
    own_pair, sent_pair = columns_of(pair_weights, core), columns_of(pair_weights, 1 - core)
    tokens, own_pair, sent_pair = together(tokens, own_pair, sent_pair)
    held_pair = gather_start({0: own_pair})
    other_pair = swap(sent_pair, 1)

    normed_own, unit_rows, row_spread = normalize(tokens.astype(F32), norm_gain)
    normed_own = normed_own.astype(BF)
    even = jnp.concatenate([feature_block(normed_own, r) for r in range(0, n_dp, 2)], axis=1)
    odd = jnp.concatenate([feature_block(normed_own, r) for r in range(1, n_dp, 2)], axis=1)
    block = jnp.concatenate([even, swap(odd, 1)], axis=0)

    normed = blank((2 * group, width), BF)

    def put(normed, block, step):
        beside = swap(block, 1)
        start = level_at(step) * own
        mine, other = core * group + start, (1 - core) * group + start
        for piece, at, column in (
            (block[:own], mine, 0),
            (block[own:], other, 0),
            (beside[:own], other, width // 2),
            (beside[own:], mine, width // 2),
        ):
            normed = lax.dynamic_update_slice(normed, piece, (at, column))
        return normed

    held_pair, normed = together(held_pair, normed)
    held_pair.update(gather_start({1: other_pair}))
    normed = put(normed, block, 0)
    for step in range(1, n_mp):
        block = ring_on(block)
        normed = put(normed, block, step)
        if step == 1:
            held_pair, normed, w_value, grad_heads = together(held_pair, normed, w_value, grad_heads)
            held_pair = gather_rest(held_pair)
            shard_value = [half(w_value, core), swap(half(w_value, 1 - core), 1)]
            shard_value = jnp.concatenate(shard_value, axis=0)
            grads_mine, grads_other = half(grad_heads, core), swap(half(grad_heads, 1 - core), 1)
        elif step == 2:
            shard_value, normed = together(shard_value, normed)
            held_value = gather_start({0: shard_value})

    grad_out = blank((2 * group, cols), BF)
    grad_out = lax.dynamic_update_slice_in_dim(grad_out, grads_mine, core * group, 0)
    grad_out = lax.dynamic_update_slice_in_dim(grad_out, grads_other, (1 - core) * group, 0)
    gains = jnp.stack([q_gain, k_gain])

    full_pair = whole(held_pair)
    pair = jnp.dot(normed, full_pair, preferred_element_type=F32)
    turned_value = attention_call(first_kernel, (pair, grad_out), gains, cols)

    def products(turned, r, offsets, addends=((), ()), turn=False):
        units = [[unit_of(r ^ f) for f in side] for side in offsets]
        return product_call(turned, normed, rows, units, addends, turn)

    blocks_of_four = range(0, n_dp, 8)

    def messages(turned, to_x, to_y):
        return [products(turned, r, (to_x, to_y)) for r in blocks_of_four]

    def late_messages(turned, far, turn=False):
        return [
            products(turned, r, ((3,), (4,)), (((from_y, 0),), ((from_x, 0),)), turn)
            for r, (from_x, from_y) in zip(blocks_of_four, far)
        ]

    def send(messages, x=2, y=4):
        return [[swap(to_x, x), swap(to_y, y)] for to_x, to_y in messages]

    def scatter_end(turned, early, unit, late):
        def own(r, turn):
            (early_x, early_y), (late_x, late_y) = early[r // 8], late[r // 8]
            addends = (((early_x, unit), (late_y, 0)), ((early_y, unit), (late_x, 0)))
            return products(turned, r, ((0,), (1,)), addends, turn)

        if n_dp == 8:
            return own(0, True)
        totals = {r: own(r, False) for r in blocks_of_four}
        bit = n_dp // 2
        while bit >= 8:
            for r in [r for r in totals if r < bit]:
                passed = [swap(total, bit) for total in totals.pop(r ^ bit)]
                totals[r] = [
                    (a.astype(F32) + b.astype(F32)).astype(BF) for a, b in zip(totals[r], passed)
                ]
            bit //= 2
        return [total.T for total in totals[0]]

    held_value, turned_value = together(held_value, turned_value)
    pieces = {r ^ f: part[f * rows : (f + 1) * rows] for r, part in held_value.items() for f in (0, 1)}
    relayed = [r ^ f for r in blocks_of_four for f in (2, 5)]
    pieces.update(zip(relayed, together(*[pieces[r] for r in relayed])))
    held_value = gather_rest(pieces)
    first_value = send(messages(turned_value, (6, 2), (7, 5)))
    full_value = whole(held_value)
    values = jnp.dot(normed, full_value, preferred_element_type=F32).astype(BF)
    turned_pair = attention_call(rest_kernel, (pair, grad_out, values), gains, 2 * cols)

    def back_odd(step, turned_pair, turned_value):
        at = level_at(step + 1) * own
        chosen = [
            jnp.concatenate(
                [lax.dynamic_slice_in_dim(turned, g * group + at, own, 1) for g in range(2)], axis=1
            )
            for turned in (turned_pair, turned_value)
        ]
        return chosen, back_call(*chosen, full_pair, full_value, rows, True, (), BF)

    def back_even(chosen, passed, dtype):
        return back_call(*chosen, full_pair, full_value, rows, False, (passed,), dtype)

    chosen, sent, partial = {}, {}, {}
    chosen[0], sent[0] = back_odd(0, turned_pair, turned_value)
    chosen[1], sent[1] = back_odd(1, turned_pair, turned_value)
    late_value = late_messages(turned_value, first_value)
    late_value, sent = together(late_value, sent)
    late_value = send(late_value)
    passed = {step: swap(sent[step], 1) for step in range(2)}
    far_pair = messages(turned_pair, (6,), (7,))
    far_pair, passed = together(far_pair, passed)
    message = back_even(chosen[0], passed[0], BF)
    message, far_pair, turned_pair, turned_value = together(message, far_pair, turned_pair, turned_value)
    arrived, far_pair = ring_on(message), send(far_pair)

    turned_pair, turned_value, late_value = together(turned_pair, turned_value, late_value)
    for step in range(2, 4):
        chosen[step], sent[step] = back_odd(step, turned_pair, turned_value)
    ends_value = scatter_end(turned_value, first_value, 1, late_value)
    partial[1] = back_even(chosen[1], passed[1], BF)
    early_pair = messages(turned_pair, (2,), (5,))
    for step in range(1, n_mp - 1):
        if step == 1:
            partial[1], early_pair, sent, far_pair, ends_value = together(
                partial[1], early_pair, sent, far_pair, ends_value
            )
        elif step == 2:
            partial[2], late_pair, own_pair = together(partial[2], late_pair, own_pair)
        message = (partial[step].astype(F32) + arrived.astype(F32)).astype(BF)
        if step == 1:
            message, early_pair, sent, turned_pair, turned_value = together(
                message, early_pair, sent, turned_pair, turned_value
            )
            early_pair = send(early_pair, y=5)
        elif step == 2:
            message, late_pair, own_pair, ends_value, early_pair = together(
                message, late_pair, own_pair, ends_value, early_pair
            )
            late_pair = send(late_pair, x=3)
            own_pair = [[even, swap(odd, 1)] for even, odd in own_pair]
            passed_value = swap(ends_value[1], 1)
        arrived = ring_on(message)
        if step + 2 < n_mp:
            near = [step + 1, step + 2] if step + 3 == n_mp else [step + 1]
            for level_step in near:
                passed[level_step] = swap(sent[level_step], 1)
            here = [passed[level_step] for level_step in near]
            turned_pair, turned_value, here = together(turned_pair, turned_value, here)
            passed.update(zip(near, here))
            for level_step in near:
                dtype = F32 if level_step == n_mp - 1 else BF
                partial[level_step] = back_even(chosen[level_step], passed[level_step], dtype)
            if step + 3 == n_mp:
                partial[n_mp - 2], partial[n_mp - 1] = together(partial[n_mp - 2], partial[n_mp - 1])
            else:
                chosen[step + 3], sent[step + 3] = back_odd(step + 3, turned_pair, turned_value)
            if step == 1:
                late_pair = late_messages(turned_pair, far_pair, True)
                own_pair = messages(turned_pair, (0,), (1,))
    out_value = place_call(core, ends_value[0], passed_value, cols, 0)
    here, there = {}, {}
    for r, (own_even, own_odd), (even_x, odd_y) in zip(blocks_of_four, own_pair, early_pair):
        here[r] = (own_even.astype(F32) + even_x.astype(F32)).astype(BF).T
        there[r] = (own_odd.astype(F32) + odd_y.astype(F32)).astype(BF).T
    arrived, out_value, here, there = together(arrived, out_value, here, there)
    total = partial[n_mp - 1] + arrived.astype(F32)

    mine = lax.dynamic_slice_in_dim(total, core * own, own, 1)
    other = lax.dynamic_slice_in_dim(total, (1 - core) * own, own, 1).astype(BF)
    other = swap(other, 1)

    for r, (odd_x, even_y) in zip(blocks_of_four, late_pair):
        here[r], there[r] = [here[r], even_y], [there[r], odd_x]
    bit = n_dp // 2
    while bit >= 8:
        for parts in (here, there):
            for r in [r for r in parts if r >= bit]:
                parts[r ^ bit].append(swap(sum(p.astype(F32) for p in parts.pop(r)).astype(BF), bit))
        bit //= 2
    out_query, out_key = gather_call(core, here[0], there[0], cols)
    other, out_query, out_key = together(other, out_query, out_key)
    grad_tokens = finish_call(place, mine, other, unit_rows, row_spread, norm_gain, rows)
    return (grad_tokens, out_query, out_key, out_value)


def solution(mesh):
    matrix = P("dp", "mp")
    token_rows = P(("dp", "mp"), None)
    return jax.shard_map(
        functools.partial(per_device, mesh.shape["dp"], mesh.shape["mp"]),
        mesh=mesh,
        in_specs=(token_rows, P(), P(), P(), matrix, matrix, matrix, matrix),
        out_specs=(token_rows, matrix, matrix, matrix),
        check_vma=False,
    )
```

```python
import functools

import jax
import jax.numpy as jnp
from jax import lax
from jax.experimental import pallas as pl
from jax.experimental.pallas import tpu as pltpu
from jax.sharding import PartitionSpec as P

PATCH = 256
BF = jnp.bfloat16
F32 = jnp.float32


def normalize(row_data, gain_vector):
    average = jnp.mean(row_data, axis=-1, keepdims=True)
    centred = row_data - average
    inv_spread = lax.rsqrt(jnp.mean(centred * centred, axis=-1, keepdims=True) + 1e-06)
    unit_data = centred * inv_spread
    return (unit_data * gain_vector, unit_data, inv_spread)


def normalize_back(grad_out, unit_data, inv_spread, gain_vector):
    scaled = grad_out * gain_vector
    inner_term = jnp.mean(scaled * unit_data, axis=-1, keepdims=True)
    return (scaled - jnp.mean(scaled, axis=-1, keepdims=True) - unit_data * inner_term) * inv_spread


def dot_nt(a, b):
    return lax.dot_general(a, b, (((1,), (1,)), ((), ())), preferred_element_type=F32)


def dot_tn(a, b):
    return lax.dot_general(a, b, (((0,), (0,)), ((), ())), preferred_element_type=F32)


def params(mib):
    return pltpu.CompilerParams(vmem_limit_bytes=mib * 2**20)


def cost(flops, bytes_accessed):
    return pl.CostEstimate(flops=flops // 6, bytes_accessed=bytes_accessed // 6, transcendentals=0)


def blank(shape, dtype):
    return pl.pallas_call(
        lambda out_ref: None,
        out_shape=jax.ShapeDtypeStruct(shape, dtype),
        out_specs=pl.BlockSpec(memory_space=pl.ANY),
    )()


def attention_of(query_bf, key_bf):
    scores = dot_nt(key_bf, query_bf) * query_bf.shape[-1] ** (-0.5)
    raised = jnp.exp(scores - jnp.max(scores, axis=0, keepdims=True))
    return raised * (1.0 / jnp.sum(raised, axis=0, keepdims=True))


def first_kernel(qk_ref, g_ref, gains_ref, turned_ref):
    head, cols = gains_ref.shape[1], g_ref.shape[1]
    for h in range(cols // head):
        at, key_at = pl.ds(h * head, head), pl.ds(cols + h * head, head)
        query_bf = normalize(qk_ref[:, at], gains_ref[0:1])[0].astype(BF)
        key_bf = normalize(qk_ref[:, key_at], gains_ref[1:2])[0].astype(BF)
        attention = attention_of(query_bf, key_bf).astype(BF)
        grad_value = jnp.dot(attention, g_ref[:, at], preferred_element_type=F32)
        turned_ref[at, :] = grad_value.T.astype(BF)


def rest_kernel(qk_ref, g_ref, v_ref, gains_ref, turned_ref):
    head, cols = gains_ref.shape[1], g_ref.shape[1]
    factor = head ** (-0.5)
    q_gain, k_gain = gains_ref[0:1], gains_ref[1:2]
    for h in range(cols // head):
        at, key_at = pl.ds(h * head, head), pl.ds(cols + h * head, head)
        query_normed, query_unit, query_spread = normalize(qk_ref[:, at], q_gain)
        key_normed, key_unit, key_spread = normalize(qk_ref[:, key_at], k_gain)
        query_bf, key_bf = query_normed.astype(BF), key_normed.astype(BF)
        attention = attention_of(query_bf, key_bf)
        grad_probs = dot_nt(v_ref[:, at], g_ref[:, at])
        delta = jnp.sum(attention * grad_probs, axis=0, keepdims=True)
        grad_scores = (attention * (grad_probs - delta) * factor).astype(BF)
        grad_kn = jnp.dot(grad_scores, query_bf, preferred_element_type=F32)
        grad_qn = dot_tn(grad_scores, key_bf)
        grad_query = normalize_back(grad_qn, query_unit, query_spread, q_gain)
        grad_key = normalize_back(grad_kn, key_unit, key_spread, k_gain)
        turned_ref[at, :] = grad_query.T.astype(BF)
        turned_ref[key_at, :] = grad_key.T.astype(BF)


def attention_call(kernel, arrays, gains, out_rows):
    tokens, columns = arrays[1].shape
    head = gains.shape[-1]
    pairs = (tokens // PATCH) * (columns // head)
    return pl.pallas_call(
        kernel,
        grid=(tokens // PATCH,),
        in_specs=[pl.BlockSpec((PATCH, array.shape[1]), lambda i: (i, 0)) for array in arrays]
        + [pl.BlockSpec(gains.shape, lambda i: (0, 0))],
        out_specs=pl.BlockSpec((out_rows, PATCH), lambda i: (0, i)),
        out_shape=jax.ShapeDtypeStruct((out_rows, tokens), BF),
        compiler_params=params(12),
        cost_estimate=cost(pairs * 8 * PATCH * PATCH * head, 4 * len(arrays) * arrays[0].size),
    )(*arrays, gains)


def product_kernel(n_add, turn, turned_ref, *refs):
    turned = turned_ref[...]
    outs = refs[-2:]
    for side in range(2):
        total = jnp.dot(turned, refs[side][...], preferred_element_type=F32)
        for ref in refs[2 + side * n_add : 2 + (side + 1) * n_add]:
            total = total + ref[...].astype(F32)
        outs[side][...] = (total.T if turn else total).astype(BF)


def product_call(turned, normed, rows, units, addends=((), ()), turn=False):
    columns, tokens = turned.shape
    tile = 256 if rows % 256 == 0 else 128
    count, n_add, steps = len(units[0]), len(addends[0]), rows // tile

    def side(first, last):
        return pl.BlockSpec((tokens, tile), lambda u, i: (0, (first + u * (last - first)) * steps + i))

    def added(which):
        return pl.BlockSpec((columns, tile), lambda u, i: (which, i))

    if turn:
        shape, out = (rows, columns), pl.BlockSpec((tile, columns), lambda u, i: (i, 0))
    else:
        shape, out = (count * columns, rows), pl.BlockSpec((columns, tile), lambda u, i: (u, i))
    addends = [*addends[0], *addends[1]]
    return pl.pallas_call(
        functools.partial(product_kernel, n_add, turn),
        grid=(count, steps),
        in_specs=[
            pl.BlockSpec((columns, tokens), lambda u, i: (0, 0)),
            *[side(chosen[0], chosen[-1]) for chosen in units],
            *[added(which) for _, which in addends],
        ],
        out_specs=[out] * 2,
        out_shape=[jax.ShapeDtypeStruct(shape, BF)] * 2,
        compiler_params=params(14),
        cost_estimate=cost(
            4 * count * columns * tokens * rows,
            2 * columns * tokens + 4 * count * tokens * rows + (4 + 4 * n_add) * columns * rows,
        ),
    )(turned, normed, normed, *[array for array, _ in addends])


def back_kernel(pair_ref, value_ref, w_pair_ref, w_value_ref, *refs):
    total = jnp.dot(w_pair_ref[...], pair_ref[...], preferred_element_type=F32)
    total = total + jnp.dot(w_value_ref[...], value_ref[...], preferred_element_type=F32)
    for ref in refs[:-1]:
        total = total + ref[...].astype(F32)
    refs[-1][...] = total.astype(refs[-1].dtype)


def back_call(pair, value, w_pair, w_value, rows, odd, addends, dtype):
    level_tokens = pair.shape[1]
    units = w_pair.shape[0] // rows // 2
    first = units if odd else 0
    block = pl.BlockSpec((rows, level_tokens), lambda i: (i, 0))
    return pl.pallas_call(
        back_kernel,
        grid=(units,),
        in_specs=[
            pl.BlockSpec(pair.shape, lambda i: (0, 0)),
            pl.BlockSpec(value.shape, lambda i: (0, 0)),
            pl.BlockSpec((rows, w_pair.shape[1]), lambda i: (first + i, 0)),
            pl.BlockSpec((rows, w_value.shape[1]), lambda i: (first + i, 0)),
        ]
        + [block] * len(addends),
        out_specs=block,
        out_shape=jax.ShapeDtypeStruct((units * rows, level_tokens), dtype),
        compiler_params=params(11),
        cost_estimate=cost(
            2 * units * rows * level_tokens * (pair.shape[0] + value.shape[0]),
            2 * units * rows * (pair.shape[0] + value.shape[0] + 3 * level_tokens),
        ),
    )(pair, value, w_pair, w_value, *addends)


def gather_kernel(cols, n_parts, core_ref, *refs):
    parts, outs = refs[: 2 * n_parts], refs[2 * n_parts :]
    here = pl.program_id(0) == core_ref[0]

    def store(blocks):
        total = blocks[0][...].astype(F32)
        for block in blocks[1:]:
            total = total + block[...].astype(F32)
        for k, out in enumerate(outs):
            out[...] = total[k * cols : (k + 1) * cols].T.astype(BF)

    @pl.when(here)
    def _():
        store(parts[:n_parts])

    @pl.when(jnp.logical_not(here))
    def _():
        store(parts[n_parts:])


def gather_call(core, mine, other, cols):
    columns, rows = mine[0].shape
    tile = 256 if rows % 256 == 0 else 128
    here = pl.BlockSpec(
        (columns, tile), lambda h, i, core_ref: (0, jnp.where(h == core_ref[0], i, rows // tile * h - h))
    )
    there = pl.BlockSpec(
        (columns, tile), lambda h, i, core_ref: (0, jnp.where(h != core_ref[0], i, rows // tile * h - h))
    )
    return pl.pallas_call(
        functools.partial(gather_kernel, cols, len(mine)),
        grid_spec=pltpu.PrefetchScalarGridSpec(
            num_scalar_prefetch=1,
            grid=(2, rows // tile),
            in_specs=[here] * len(mine) + [there] * len(other),
            out_specs=[pl.BlockSpec((tile, cols), lambda h, i, core_ref: (i, h))] * (columns // cols),
        ),
        out_shape=[jax.ShapeDtypeStruct((rows, 2 * cols), BF)] * (columns // cols),
        compiler_params=params(40),
    )(core.reshape(1), *mine, *other)


def place_kernel(core_ref, mine_ref, other_ref, out_ref):
    here = pl.program_id(0) == core_ref[0]

    @pl.when(here)
    def _():
        out_ref[...] = mine_ref[...]

    @pl.when(jnp.logical_not(here))
    def _():
        out_ref[...] = other_ref[...]


def place_call(core, mine, other, cols, part):
    rows = mine.shape[0]
    block = pl.BlockSpec((rows, cols), lambda i, core_ref: (0, part))
    return pl.pallas_call(
        place_kernel,
        grid_spec=pltpu.PrefetchScalarGridSpec(
            num_scalar_prefetch=1,
            grid=(2,),
            in_specs=[block, block],
            out_specs=pl.BlockSpec((rows, cols), lambda i, core_ref: (0, i)),
        ),
        out_shape=jax.ShapeDtypeStruct((rows, 2 * cols), BF),
        compiler_params=params(12),
    )(core.reshape(1), mine, other)


def finish_kernel(rows, n_dp, place_ref, mine_ref, other_ref, unit_ref, spread_ref, gain_ref, out_ref, held):
    n_chips = n_dp // 2
    held[: n_chips * rows] = mine_ref[...]
    held[n_chips * rows :] = other_ref[...].astype(F32)
    place = place_ref[0]
    columns = []
    total, inner = 0.0, 0.0
    for b in range(n_dp):
        r = b ^ place
        unit = (r & 1) * n_chips + (r >> 1)
        at = pl.ds(b * rows, rows)
        grad = held[pl.ds(pl.multiple_of(unit * rows, rows), rows), :].T
        scaled = grad * gain_ref[:, at]
        total = total + jnp.sum(scaled, axis=-1, keepdims=True)
        inner = inner + jnp.sum(scaled * unit_ref[:, at], axis=-1, keepdims=True)
        columns.append(scaled)
    average, inner = total * (1.0 / (n_dp * rows)), inner * (1.0 / (n_dp * rows))
    for b in range(n_dp):
        at = pl.ds(b * rows, rows)
        result = (columns[b] - average - unit_ref[:, at] * inner) * spread_ref[...]
        out_ref[:, at] = result.astype(BF)


def finish_call(place, mine, other, unit_rows, row_spread, norm_gain, rows):
    own, width = unit_rows.shape
    vmem = pl.BlockSpec(memory_space=pltpu.VMEM)
    return pl.pallas_call(
        functools.partial(finish_kernel, rows, width // rows),
        in_specs=[pl.BlockSpec(memory_space=pltpu.SMEM)] + [vmem] * 5,
        out_specs=vmem,
        out_shape=jax.ShapeDtypeStruct((own, width), BF),
        scratch_shapes=[pltpu.VMEM((width, own), F32)],
        compiler_params=params(20),
    )(place.reshape(1), mine, other, unit_rows, row_spread, norm_gain.reshape(1, width))


def per_device(n_dp, n_mp, tokens, norm_gain, q_gain, k_gain, w_query, w_key, w_value, grad_heads):
    own, width = tokens.shape
    rows, cols = w_query.shape[0], w_query.shape[1] // 2
    n_chips = n_dp // 2
    group = n_mp * own
    place = lax.axis_index("dp")
    core = place & 1

    def swap(array, bit):
        return lax.ppermute(array, "dp", [(i, i ^ bit) for i in range(n_dp)])

    def half(array, which):
        return lax.dynamic_slice_in_dim(array, which * cols, cols, 1)

    def together(*arrays):
        return lax.optimization_barrier(arrays)

    ring = list(range(0, n_mp, 2)) + list(range(n_mp - 1, 0, -2))
    level = lax.axis_index("mp")
    spot = jnp.where(level & 1 == 0, level >> 1, n_mp - 1 - (level >> 1))
    ring_pairs = [(ring[i], ring[(i + 1) % n_mp]) for i in range(n_mp)]

    def level_at(back):
        at = lax.rem(spot + 2 * n_mp - back, n_mp)
        return jnp.where(at < n_mp // 2, 2 * at, 2 * (n_mp - 1 - at) + 1)

    def ring_on(array):
        return lax.ppermute(array, "mp", ring_pairs)

    def unit_of(r):
        return (r & 1) * n_chips + (r >> 1)

    def feature_block(array, r):
        return lax.dynamic_slice_in_dim(array, (place ^ r) * rows, rows, 1)

    def columns_of(weights, which):
        return jnp.concatenate([half(w, which) for w in weights], axis=1)

    def gather_start(held):
        held = dict(held)
        bit = 8
        while bit < n_dp:
            held.update({r ^ bit: swap(part, bit) for r, part in list(held.items())})
            bit *= 2
        for r, part in list(held.items()):
            held[r ^ 2] = swap(part, 2)
            held[r ^ 4] = swap(part, 4)
        return held

    def gather_rest(held):
        held = dict(held)
        for r in range(0, n_dp, 8):
            held[r ^ 6] = swap(held[r ^ 2], 4)
            held[r ^ 7] = swap(held[r ^ 5], 2)
        return held

    def whole(held):
        return jnp.concatenate([held[r] for r in (*range(0, n_dp, 2), *range(1, n_dp, 2))], axis=0)

    pair_weights = (w_query, w_key)
    own_pair, sent_pair = columns_of(pair_weights, core), columns_of(pair_weights, 1 - core)
    tokens, own_pair, sent_pair = together(tokens, own_pair, sent_pair)
    held_pair = gather_start({0: own_pair})
    other_pair = swap(sent_pair, 1)

    normed_own, unit_rows, row_spread = normalize(tokens.astype(F32), norm_gain)
    normed_own = normed_own.astype(BF)
    even = jnp.concatenate([feature_block(normed_own, r) for r in range(0, n_dp, 2)], axis=1)
    odd = jnp.concatenate([feature_block(normed_own, r) for r in range(1, n_dp, 2)], axis=1)
    block = jnp.concatenate([even, swap(odd, 1)], axis=0)

    normed = blank((2 * group, width), BF)

    def put(normed, block, step):
        beside = swap(block, 1)
        start = level_at(step) * own
        mine, other = core * group + start, (1 - core) * group + start
        for piece, at, column in (
            (block[:own], mine, 0),
            (block[own:], other, 0),
            (beside[:own], other, width // 2),
            (beside[own:], mine, width // 2),
        ):
            normed = lax.dynamic_update_slice(normed, piece, (at, column))
        return normed

    held_pair, normed = together(held_pair, normed)
    held_pair.update(gather_start({1: other_pair}))
    normed = put(normed, block, 0)
    for step in range(1, n_mp):
        block = ring_on(block)
        normed = put(normed, block, step)
        if step == 1:
            held_pair, normed, w_value, grad_heads = together(held_pair, normed, w_value, grad_heads)
            held_pair = gather_rest(held_pair)
            shard_value = [half(w_value, core), swap(half(w_value, 1 - core), 1)]
            shard_value = jnp.concatenate(shard_value, axis=0)
            grads_mine, grads_other = half(grad_heads, core), swap(half(grad_heads, 1 - core), 1)
        elif step == 2:
            shard_value, normed = together(shard_value, normed)
            held_value = gather_start({0: shard_value})

    grad_out = blank((2 * group, cols), BF)
    grad_out = lax.dynamic_update_slice_in_dim(grad_out, grads_mine, core * group, 0)
    grad_out = lax.dynamic_update_slice_in_dim(grad_out, grads_other, (1 - core) * group, 0)
    gains = jnp.stack([q_gain, k_gain])

    full_pair = whole(held_pair)
    pair = jnp.dot(normed, full_pair, preferred_element_type=F32)
    turned_value = attention_call(first_kernel, (pair, grad_out), gains, cols)

    def products(turned, r, offsets, addends=((), ()), turn=False):
        units = [[unit_of(r ^ f) for f in side] for side in offsets]
        return product_call(turned, normed, rows, units, addends, turn)

    blocks_of_four = range(0, n_dp, 8)

    def messages(turned, to_x, to_y):
        return [products(turned, r, (to_x, to_y)) for r in blocks_of_four]

    def late_messages(turned, far):
        return [
            products(turned, r, ((3,), (4,)), (((from_y, 0),), ((from_x, 0),)))
            for r, (from_x, from_y) in zip(blocks_of_four, far)
        ]

    def send(messages, x=2, y=4):
        return [[swap(to_x, x), swap(to_y, y)] for to_x, to_y in messages]

    def scatter_end(turned, early, unit, late):
        def own(r, turn):
            (early_x, early_y), (late_x, late_y) = early[r // 8], late[r // 8]
            addends = (((early_x, unit), (late_y, 0)), ((early_y, unit), (late_x, 0)))
            return products(turned, r, ((0,), (1,)), addends, turn)

        if n_dp == 8:
            return own(0, True)
        totals = {r: own(r, False) for r in blocks_of_four}
        bit = n_dp // 2
        while bit >= 8:
            for r in [r for r in totals if r < bit]:
                passed = [swap(total, bit) for total in totals.pop(r ^ bit)]
                totals[r] = [
                    (a.astype(F32) + b.astype(F32)).astype(BF) for a, b in zip(totals[r], passed)
                ]
            bit //= 2
        return [total.T for total in totals[0]]

    held_value, turned_value = together(held_value, turned_value)
    pieces = {r ^ f: part[f * rows : (f + 1) * rows] for r, part in held_value.items() for f in (0, 1)}
    relayed = [r ^ f for r in blocks_of_four for f in (2, 5)]
    pieces.update(zip(relayed, together(*[pieces[r] for r in relayed])))
    held_value = gather_rest(pieces)
    first_value = send(messages(turned_value, (6, 2), (7, 5)))
    full_value = whole(held_value)
    values = jnp.dot(normed, full_value, preferred_element_type=F32).astype(BF)
    turned_pair = attention_call(rest_kernel, (pair, grad_out, values), gains, 2 * cols)

    def back_odd(step, turned_pair, turned_value):
        at = level_at(step + 1) * own
        chosen = [
            jnp.concatenate(
                [lax.dynamic_slice_in_dim(turned, g * group + at, own, 1) for g in range(2)], axis=1
            )
            for turned in (turned_pair, turned_value)
        ]
        return chosen, back_call(*chosen, full_pair, full_value, rows, True, (), BF)

    def back_even(chosen, passed, dtype):
        return back_call(*chosen, full_pair, full_value, rows, False, (passed,), dtype)

    chosen, sent, partial = {}, {}, {}
    chosen[0], sent[0] = back_odd(0, turned_pair, turned_value)
    chosen[1], sent[1] = back_odd(1, turned_pair, turned_value)
    late_value = late_messages(turned_value, first_value)
    late_value, sent = together(late_value, sent)
    late_value = send(late_value)
    passed = {step: swap(sent[step], 1) for step in range(2)}
    far_pair = messages(turned_pair, (6,), (7,))
    far_pair, passed = together(far_pair, passed)
    message = back_even(chosen[0], passed[0], BF)
    message, far_pair, turned_pair, turned_value = together(message, far_pair, turned_pair, turned_value)
    arrived, far_pair = ring_on(message), send(far_pair)

    turned_pair, turned_value, late_value = together(turned_pair, turned_value, late_value)
    for step in range(2, 4):
        chosen[step], sent[step] = back_odd(step, turned_pair, turned_value)
    partial[1] = back_even(chosen[1], passed[1], BF)
    early_pair = messages(turned_pair, (2,), (5,))
    for step in range(1, n_mp - 1):
        if step == 1:
            partial[1], early_pair, sent = together(partial[1], early_pair, sent)
        elif step == 2:
            partial[2], late_pair, own_pair, ends_value = together(
                partial[2], late_pair, own_pair, ends_value
            )
        message = (partial[step].astype(F32) + arrived.astype(F32)).astype(BF)
        if step == 1:
            message, early_pair, sent, turned_pair, turned_value, far_pair = together(
                message, early_pair, sent, turned_pair, turned_value, far_pair
            )
            early_pair = send(early_pair, y=5)
        elif step == 2:
            message, late_pair, own_pair, ends_value, early_pair = together(
                message, late_pair, own_pair, ends_value, early_pair
            )
            late_pair = send(late_pair, x=3)
            own_pair = [[even, swap(odd, 1)] for even, odd in own_pair]
            passed_value = swap(ends_value[1], 1)
        arrived = ring_on(message)
        if step + 2 < n_mp:
            near = [step + 1, step + 2] if step + 3 == n_mp else [step + 1]
            for level_step in near:
                passed[level_step] = swap(sent[level_step], 1)
            here = [passed[level_step] for level_step in near]
            turned_pair, turned_value, here = together(turned_pair, turned_value, here)
            passed.update(zip(near, here))
            for level_step in near:
                dtype = F32 if level_step == n_mp - 1 else BF
                partial[level_step] = back_even(chosen[level_step], passed[level_step], dtype)
            if step + 3 == n_mp:
                partial[n_mp - 2], partial[n_mp - 1] = together(partial[n_mp - 2], partial[n_mp - 1])
            else:
                chosen[step + 3], sent[step + 3] = back_odd(step + 3, turned_pair, turned_value)
            if step == 1:
                late_pair = late_messages(turned_pair, far_pair)
                own_pair = messages(turned_pair, (0,), (1,))
                ends_value = scatter_end(turned_value, first_value, 1, late_value)
    out_value = place_call(core, ends_value[0], passed_value, cols, 0)
    here, there = {}, {}
    for r, (own_even, own_odd), (even_x, odd_y) in zip(blocks_of_four, own_pair, early_pair):
        here[r] = (own_even.astype(F32) + even_x.astype(F32)).astype(BF)
        there[r] = (own_odd.astype(F32) + odd_y.astype(F32)).astype(BF)
    arrived, out_value, here, there = together(arrived, out_value, here, there)
    total = partial[n_mp - 1] + arrived.astype(F32)

    mine = lax.dynamic_slice_in_dim(total, core * own, own, 1)
    other = lax.dynamic_slice_in_dim(total, (1 - core) * own, own, 1).astype(BF)
    other = swap(other, 1)

    for r, (odd_x, even_y) in zip(blocks_of_four, late_pair):
        here[r], there[r] = [here[r], even_y], [there[r], odd_x]
    bit = n_dp // 2
    while bit >= 8:
        for parts in (here, there):
            for r in [r for r in parts if r >= bit]:
                parts[r ^ bit].append(swap(sum(p.astype(F32) for p in parts.pop(r)).astype(BF), bit))
        bit //= 2
    out_query, out_key = gather_call(core, here[0], there[0], cols)
    other, out_query, out_key = together(other, out_query, out_key)
    grad_tokens = finish_call(place, mine, other, unit_rows, row_spread, norm_gain, rows)
    return (grad_tokens, out_query, out_key, out_value)


def solution(mesh):
    matrix = P("dp", "mp")
    token_rows = P(("dp", "mp"), None)
    return jax.shard_map(
        functools.partial(per_device, mesh.shape["dp"], mesh.shape["mp"]),
        mesh=mesh,
        in_specs=(token_rows, P(), P(), P(), matrix, matrix, matrix, matrix),
        out_specs=(token_rows, matrix, matrix, matrix),
        check_vma=False,
    )
```

```python
import functools

import jax
import jax.numpy as jnp
from jax import lax
from jax.experimental import pallas as pl
from jax.experimental.pallas import tpu as pltpu
from jax.sharding import PartitionSpec as P

PATCH = 256
BF = jnp.bfloat16
F32 = jnp.float32


def normalize(row_data, gain_vector):
    average = jnp.mean(row_data, axis=-1, keepdims=True)
    centred = row_data - average
    inv_spread = lax.rsqrt(jnp.mean(centred * centred, axis=-1, keepdims=True) + 1e-06)
    unit_data = centred * inv_spread
    return (unit_data * gain_vector, unit_data, inv_spread)


def normalize_back(grad_out, unit_data, inv_spread, gain_vector):
    scaled = grad_out * gain_vector
    inner_term = jnp.mean(scaled * unit_data, axis=-1, keepdims=True)
    return (scaled - jnp.mean(scaled, axis=-1, keepdims=True) - unit_data * inner_term) * inv_spread


def dot_nt(a, b):
    return lax.dot_general(a, b, (((1,), (1,)), ((), ())), preferred_element_type=F32)


def dot_tn(a, b):
    return lax.dot_general(a, b, (((0,), (0,)), ((), ())), preferred_element_type=F32)


def params(mib):
    return pltpu.CompilerParams(vmem_limit_bytes=mib * 2**20)


def cost(flops, bytes_accessed):
    return pl.CostEstimate(flops=flops // 6, bytes_accessed=bytes_accessed // 6, transcendentals=0)


def blank(shape, dtype):
    return pl.pallas_call(
        lambda out_ref: None,
        out_shape=jax.ShapeDtypeStruct(shape, dtype),
        out_specs=pl.BlockSpec(memory_space=pl.ANY),
    )()


def attention_of(query_bf, key_bf):
    scores = dot_nt(key_bf, query_bf) * query_bf.shape[-1] ** (-0.5)
    raised = jnp.exp(scores - jnp.max(scores, axis=0, keepdims=True))
    return raised * (1.0 / jnp.sum(raised, axis=0, keepdims=True))


def first_kernel(qk_ref, g_ref, gains_ref, turned_ref):
    head, cols = gains_ref.shape[1], g_ref.shape[1]
    for h in range(cols // head):
        at, key_at = pl.ds(h * head, head), pl.ds(cols + h * head, head)
        query_bf = normalize(qk_ref[:, at], gains_ref[0:1])[0].astype(BF)
        key_bf = normalize(qk_ref[:, key_at], gains_ref[1:2])[0].astype(BF)
        attention = attention_of(query_bf, key_bf).astype(BF)
        grad_value = jnp.dot(attention, g_ref[:, at], preferred_element_type=F32)
        turned_ref[at, :] = grad_value.T.astype(BF)


def rest_kernel(qk_ref, g_ref, v_ref, gains_ref, turned_ref):
    head, cols = gains_ref.shape[1], g_ref.shape[1]
    factor = head ** (-0.5)
    q_gain, k_gain = gains_ref[0:1], gains_ref[1:2]
    for h in range(cols // head):
        at, key_at = pl.ds(h * head, head), pl.ds(cols + h * head, head)
        query_normed, query_unit, query_spread = normalize(qk_ref[:, at], q_gain)
        key_normed, key_unit, key_spread = normalize(qk_ref[:, key_at], k_gain)
        query_bf, key_bf = query_normed.astype(BF), key_normed.astype(BF)
        attention = attention_of(query_bf, key_bf)
        grad_probs = dot_nt(v_ref[:, at], g_ref[:, at])
        delta = jnp.sum(attention * grad_probs, axis=0, keepdims=True)
        grad_scores = (attention * (grad_probs - delta) * factor).astype(BF)
        grad_kn = jnp.dot(grad_scores, query_bf, preferred_element_type=F32)
        grad_qn = dot_tn(grad_scores, key_bf)
        grad_query = normalize_back(grad_qn, query_unit, query_spread, q_gain)
        grad_key = normalize_back(grad_kn, key_unit, key_spread, k_gain)
        turned_ref[at, :] = grad_query.T.astype(BF)
        turned_ref[key_at, :] = grad_key.T.astype(BF)


def attention_call(kernel, arrays, gains, out_rows):
    tokens, columns = arrays[1].shape
    head = gains.shape[-1]
    pairs = (tokens // PATCH) * (columns // head)
    return pl.pallas_call(
        kernel,
        grid=(tokens // PATCH,),
        in_specs=[pl.BlockSpec((PATCH, array.shape[1]), lambda i: (i, 0)) for array in arrays]
        + [pl.BlockSpec(gains.shape, lambda i: (0, 0))],
        out_specs=pl.BlockSpec((out_rows, PATCH), lambda i: (0, i)),
        out_shape=jax.ShapeDtypeStruct((out_rows, tokens), BF),
        compiler_params=params(12),
        cost_estimate=cost(pairs * 8 * PATCH * PATCH * head, 4 * len(arrays) * arrays[0].size),
    )(*arrays, gains)


def product_kernel(n_add, turn, turned_ref, *refs):
    turned = turned_ref[...]
    outs = refs[-2:]
    for side in range(2):
        total = jnp.dot(turned, refs[side][...], preferred_element_type=F32)
        for ref in refs[2 + side * n_add : 2 + (side + 1) * n_add]:
            total = total + ref[...].astype(F32)
        outs[side][...] = (total.T if turn else total).astype(BF)


def product_call(turned, normed, rows, units, addends=((), ()), turn=False):
    columns, tokens = turned.shape
    tile = 256 if rows % 256 == 0 else 128
    count, n_add, steps = len(units[0]), len(addends[0]), rows // tile

    def side(first, last):
        return pl.BlockSpec((tokens, tile), lambda u, i: (0, (first + u * (last - first)) * steps + i))

    def added(which):
        return pl.BlockSpec((columns, tile), lambda u, i: (which, i))

    if turn:
        shape, out = (rows, columns), pl.BlockSpec((tile, columns), lambda u, i: (i, 0))
    else:
        shape, out = (count * columns, rows), pl.BlockSpec((columns, tile), lambda u, i: (u, i))
    addends = [*addends[0], *addends[1]]
    return pl.pallas_call(
        functools.partial(product_kernel, n_add, turn),
        grid=(count, steps),
        in_specs=[
            pl.BlockSpec((columns, tokens), lambda u, i: (0, 0)),
            *[side(chosen[0], chosen[-1]) for chosen in units],
            *[added(which) for _, which in addends],
        ],
        out_specs=[out] * 2,
        out_shape=[jax.ShapeDtypeStruct(shape, BF)] * 2,
        compiler_params=params(14),
        cost_estimate=cost(
            4 * count * columns * tokens * rows,
            2 * columns * tokens + 4 * count * tokens * rows + (4 + 4 * n_add) * columns * rows,
        ),
    )(turned, normed, normed, *[array for array, _ in addends])


def back_kernel(pair_ref, value_ref, w_pair_ref, w_value_ref, *refs):
    total = jnp.dot(w_pair_ref[...], pair_ref[...], preferred_element_type=F32)
    total = total + jnp.dot(w_value_ref[...], value_ref[...], preferred_element_type=F32)
    for ref in refs[:-1]:
        total = total + ref[...].astype(F32)
    refs[-1][...] = total.astype(refs[-1].dtype)


def back_call(pair, value, w_pair, w_value, rows, odd, addends, dtype):
    level_tokens = pair.shape[1]
    units = w_pair.shape[0] // rows // 2
    first = units if odd else 0
    block = pl.BlockSpec((rows, level_tokens), lambda i: (i, 0))
    return pl.pallas_call(
        back_kernel,
        grid=(units,),
        in_specs=[
            pl.BlockSpec(pair.shape, lambda i: (0, 0)),
            pl.BlockSpec(value.shape, lambda i: (0, 0)),
            pl.BlockSpec((rows, w_pair.shape[1]), lambda i: (first + i, 0)),
            pl.BlockSpec((rows, w_value.shape[1]), lambda i: (first + i, 0)),
        ]
        + [block] * len(addends),
        out_specs=block,
        out_shape=jax.ShapeDtypeStruct((units * rows, level_tokens), dtype),
        compiler_params=params(11),
        cost_estimate=cost(
            2 * units * rows * level_tokens * (pair.shape[0] + value.shape[0]),
            2 * units * rows * (pair.shape[0] + value.shape[0] + 3 * level_tokens),
        ),
    )(pair, value, w_pair, w_value, *addends)


def gather_kernel(cols, n_parts, core_ref, *refs):
    parts, outs = refs[: 2 * n_parts], refs[2 * n_parts :]
    here = pl.program_id(0) == core_ref[0]

    def store(blocks):
        total = blocks[0][...].astype(F32)
        for block in blocks[1:]:
            total = total + block[...].astype(F32)
        for k, out in enumerate(outs):
            out[...] = total[k * cols : (k + 1) * cols].astype(BF).T

    @pl.when(here)
    def _():
        store(parts[:n_parts])

    @pl.when(jnp.logical_not(here))
    def _():
        store(parts[n_parts:])


def gather_call(core, mine, other, cols):
    columns, rows = mine[0].shape
    tile = 256 if rows % 256 == 0 else 128
    here = pl.BlockSpec(
        (columns, tile), lambda h, i, core_ref: (0, jnp.where(h == core_ref[0], i, rows // tile * h - h))
    )
    there = pl.BlockSpec(
        (columns, tile), lambda h, i, core_ref: (0, jnp.where(h != core_ref[0], i, rows // tile * h - h))
    )
    return pl.pallas_call(
        functools.partial(gather_kernel, cols, len(mine)),
        grid_spec=pltpu.PrefetchScalarGridSpec(
            num_scalar_prefetch=1,
            grid=(2, rows // tile),
            in_specs=[here] * len(mine) + [there] * len(other),
            out_specs=[pl.BlockSpec((tile, cols), lambda h, i, core_ref: (i, h))] * (columns // cols),
        ),
        out_shape=[jax.ShapeDtypeStruct((rows, 2 * cols), BF)] * (columns // cols),
        compiler_params=params(40),
    )(core.reshape(1), *mine, *other)


def place_kernel(core_ref, mine_ref, other_ref, out_ref):
    here = pl.program_id(0) == core_ref[0]

    @pl.when(here)
    def _():
        out_ref[...] = mine_ref[...]

    @pl.when(jnp.logical_not(here))
    def _():
        out_ref[...] = other_ref[...]


def place_call(core, mine, other, cols, part):
    rows = mine.shape[0]
    block = pl.BlockSpec((rows, cols), lambda i, core_ref: (0, part))
    return pl.pallas_call(
        place_kernel,
        grid_spec=pltpu.PrefetchScalarGridSpec(
            num_scalar_prefetch=1,
            grid=(2,),
            in_specs=[block, block],
            out_specs=pl.BlockSpec((rows, cols), lambda i, core_ref: (0, i)),
        ),
        out_shape=jax.ShapeDtypeStruct((rows, 2 * cols), BF),
        compiler_params=params(12),
    )(core.reshape(1), mine, other)


def finish_kernel(rows, n_dp, place_ref, mine_ref, other_ref, unit_ref, spread_ref, gain_ref, out_ref, held):
    n_chips = n_dp // 2
    held[: n_chips * rows] = mine_ref[...]
    held[n_chips * rows :] = other_ref[...].astype(F32)
    place = place_ref[0]
    columns = []
    total, inner = 0.0, 0.0
    for b in range(n_dp):
        r = b ^ place
        unit = (r & 1) * n_chips + (r >> 1)
        at = pl.ds(b * rows, rows)
        grad = held[pl.ds(pl.multiple_of(unit * rows, rows), rows), :].T
        scaled = grad * gain_ref[:, at]
        total = total + jnp.sum(scaled, axis=-1, keepdims=True)
        inner = inner + jnp.sum(scaled * unit_ref[:, at], axis=-1, keepdims=True)
        columns.append(scaled)
    average, inner = total * (1.0 / (n_dp * rows)), inner * (1.0 / (n_dp * rows))
    for b in range(n_dp):
        at = pl.ds(b * rows, rows)
        result = (columns[b] - average - unit_ref[:, at] * inner) * spread_ref[...]
        out_ref[:, at] = result.astype(BF)


def finish_call(place, mine, other, unit_rows, row_spread, norm_gain, rows):
    own, width = unit_rows.shape
    vmem = pl.BlockSpec(memory_space=pltpu.VMEM)
    return pl.pallas_call(
        functools.partial(finish_kernel, rows, width // rows),
        in_specs=[pl.BlockSpec(memory_space=pltpu.SMEM)] + [vmem] * 5,
        out_specs=vmem,
        out_shape=jax.ShapeDtypeStruct((own, width), BF),
        scratch_shapes=[pltpu.VMEM((width, own), F32)],
        compiler_params=params(20),
    )(place.reshape(1), mine, other, unit_rows, row_spread, norm_gain.reshape(1, width))


def per_device(n_dp, n_mp, tokens, norm_gain, q_gain, k_gain, w_query, w_key, w_value, grad_heads):
    own, width = tokens.shape
    rows, cols = w_query.shape[0], w_query.shape[1] // 2
    n_chips = n_dp // 2
    group = n_mp * own
    place = lax.axis_index("dp")
    core = place & 1

    def swap(array, bit):
        return lax.ppermute(array, "dp", [(i, i ^ bit) for i in range(n_dp)])

    def half(array, which):
        return lax.dynamic_slice_in_dim(array, which * cols, cols, 1)

    def together(*arrays):
        return lax.optimization_barrier(arrays)

    ring = list(range(0, n_mp, 2)) + list(range(n_mp - 1, 0, -2))
    level = lax.axis_index("mp")
    spot = jnp.where(level & 1 == 0, level >> 1, n_mp - 1 - (level >> 1))
    ring_pairs = [(ring[i], ring[(i + 1) % n_mp]) for i in range(n_mp)]

    def level_at(back):
        at = lax.rem(spot + 2 * n_mp - back, n_mp)
        return jnp.where(at < n_mp // 2, 2 * at, 2 * (n_mp - 1 - at) + 1)

    def ring_on(array):
        return lax.ppermute(array, "mp", ring_pairs)

    def unit_of(r):
        return (r & 1) * n_chips + (r >> 1)

    def feature_block(array, r):
        return lax.dynamic_slice_in_dim(array, (place ^ r) * rows, rows, 1)

    def columns_of(weights, which):
        return jnp.concatenate([half(w, which) for w in weights], axis=1)

    def gather_start(held):
        held = dict(held)
        bit = 8
        while bit < n_dp:
            held.update({r ^ bit: swap(part, bit) for r, part in list(held.items())})
            bit *= 2
        for r, part in list(held.items()):
            held[r ^ 2] = swap(part, 2)
            held[r ^ 4] = swap(part, 4)
        return held

    def gather_rest(held):
        held = dict(held)
        for r in range(0, n_dp, 8):
            held[r ^ 6] = swap(held[r ^ 2], 4)
            held[r ^ 7] = swap(held[r ^ 5], 2)
        return held

    def whole(held):
        return jnp.concatenate([held[r] for r in (*range(0, n_dp, 2), *range(1, n_dp, 2))], axis=0)

    pair_weights = (w_query, w_key)
    own_pair, sent_pair = columns_of(pair_weights, core), columns_of(pair_weights, 1 - core)
    tokens, own_pair, sent_pair = together(tokens, own_pair, sent_pair)
    held_pair = gather_start({0: own_pair})
    other_pair = swap(sent_pair, 1)

    normed_own, unit_rows, row_spread = normalize(tokens.astype(F32), norm_gain)
    normed_own = normed_own.astype(BF)
    even = jnp.concatenate([feature_block(normed_own, r) for r in range(0, n_dp, 2)], axis=1)
    odd = jnp.concatenate([feature_block(normed_own, r) for r in range(1, n_dp, 2)], axis=1)
    block = jnp.concatenate([even, swap(odd, 1)], axis=0)

    normed = blank((2 * group, width), BF)

    def put(normed, block, step):
        beside = swap(block, 1)
        start = level_at(step) * own
        mine, other = core * group + start, (1 - core) * group + start
        for piece, at, column in (
            (block[:own], mine, 0),
            (block[own:], other, 0),
            (beside[:own], other, width // 2),
            (beside[own:], mine, width // 2),
        ):
            normed = lax.dynamic_update_slice(normed, piece, (at, column))
        return normed

    held_pair, normed = together(held_pair, normed)
    held_pair.update(gather_start({1: other_pair}))
    normed = put(normed, block, 0)
    for step in range(1, n_mp):
        block = ring_on(block)
        normed = put(normed, block, step)
        if step == 1:
            held_pair, normed, w_value, grad_heads = together(held_pair, normed, w_value, grad_heads)
            held_pair = gather_rest(held_pair)
            shard_value = [half(w_value, core), swap(half(w_value, 1 - core), 1)]
            shard_value = jnp.concatenate(shard_value, axis=0)
            grads_mine, grads_other = half(grad_heads, core), swap(half(grad_heads, 1 - core), 1)
        elif step == 2:
            shard_value, normed = together(shard_value, normed)
            held_value = gather_start({0: shard_value})

    grad_out = blank((2 * group, cols), BF)
    grad_out = lax.dynamic_update_slice_in_dim(grad_out, grads_mine, core * group, 0)
    grad_out = lax.dynamic_update_slice_in_dim(grad_out, grads_other, (1 - core) * group, 0)
    gains = jnp.stack([q_gain, k_gain])

    full_pair = whole(held_pair)
    pair = jnp.dot(normed, full_pair, preferred_element_type=F32)
    turned_value = attention_call(first_kernel, (pair, grad_out), gains, cols)

    def products(turned, r, offsets, addends=((), ()), turn=False):
        units = [[unit_of(r ^ f) for f in side] for side in offsets]
        return product_call(turned, normed, rows, units, addends, turn)

    blocks_of_four = range(0, n_dp, 8)

    def messages(turned, to_x, to_y):
        return [products(turned, r, (to_x, to_y)) for r in blocks_of_four]

    def late_messages(turned, far):
        return [
            products(turned, r, ((3,), (4,)), (((from_y, 0),), ((from_x, 0),)))
            for r, (from_x, from_y) in zip(blocks_of_four, far)
        ]

    def send(messages, x=2, y=4):
        return [[swap(to_x, x), swap(to_y, y)] for to_x, to_y in messages]

    def scatter_end(turned, early, unit, late):
        def own(r, turn):
            (early_x, early_y), (late_x, late_y) = early[r // 8], late[r // 8]
            addends = (((early_x, unit), (late_y, 0)), ((early_y, unit), (late_x, 0)))
            return products(turned, r, ((0,), (1,)), addends, turn)

        if n_dp == 8:
            return own(0, True)
        totals = {r: own(r, False) for r in blocks_of_four}
        bit = n_dp // 2
        while bit >= 8:
            for r in [r for r in totals if r < bit]:
                passed = [swap(total, bit) for total in totals.pop(r ^ bit)]
                totals[r] = [
                    (a.astype(F32) + b.astype(F32)).astype(BF) for a, b in zip(totals[r], passed)
                ]
            bit //= 2
        return [total.T for total in totals[0]]

    held_value, turned_value = together(held_value, turned_value)
    pieces = {r ^ f: part[f * rows : (f + 1) * rows] for r, part in held_value.items() for f in (0, 1)}
    relayed = [r ^ f for r in blocks_of_four for f in (2, 5)]
    pieces.update(zip(relayed, together(*[pieces[r] for r in relayed])))
    held_value = gather_rest(pieces)
    first_value = send(messages(turned_value, (6, 2), (7, 5)))
    full_value = whole(held_value)
    values = jnp.dot(normed, full_value, preferred_element_type=F32).astype(BF)
    turned_pair = attention_call(rest_kernel, (pair, grad_out, values), gains, 2 * cols)

    def back_odd(step, turned_pair, turned_value):
        at = level_at(step + 1) * own
        chosen = [
            jnp.concatenate(
                [lax.dynamic_slice_in_dim(turned, g * group + at, own, 1) for g in range(2)], axis=1
            )
            for turned in (turned_pair, turned_value)
        ]
        return chosen, back_call(*chosen, full_pair, full_value, rows, True, (), BF)

    def back_even(chosen, passed, dtype):
        return back_call(*chosen, full_pair, full_value, rows, False, (passed,), dtype)

    chosen, sent, partial = {}, {}, {}
    chosen[0], sent[0] = back_odd(0, turned_pair, turned_value)
    chosen[1], sent[1] = back_odd(1, turned_pair, turned_value)
    late_value = late_messages(turned_value, first_value)
    late_value, sent = together(late_value, sent)
    late_value = send(late_value)
    passed = {step: swap(sent[step], 1) for step in range(2)}
    far_pair = messages(turned_pair, (6,), (7,))
    far_pair, passed = together(far_pair, passed)
    message = back_even(chosen[0], passed[0], BF)
    message, far_pair, turned_pair, turned_value = together(message, far_pair, turned_pair, turned_value)
    arrived, far_pair = ring_on(message), send(far_pair)

    turned_pair, turned_value, late_value = together(turned_pair, turned_value, late_value)
    for step in range(2, 4):
        chosen[step], sent[step] = back_odd(step, turned_pair, turned_value)
    partial[1] = back_even(chosen[1], passed[1], BF)
    early_pair = messages(turned_pair, (2,), (5,))
    for step in range(1, n_mp - 1):
        if step == 1:
            partial[1], early_pair, sent = together(partial[1], early_pair, sent)
        elif step == 2:
            partial[2], late_pair, own_pair, ends_value = together(
                partial[2], late_pair, own_pair, ends_value
            )
        message = (partial[step].astype(F32) + arrived.astype(F32)).astype(BF)
        if step == 1:
            message, early_pair, sent, turned_pair, turned_value, far_pair = together(
                message, early_pair, sent, turned_pair, turned_value, far_pair
            )
            early_pair = send(early_pair, y=5)
        elif step == 2:
            message, late_pair, own_pair, ends_value, early_pair = together(
                message, late_pair, own_pair, ends_value, early_pair
            )
            late_pair = send(late_pair, x=3)
            own_pair = [[even, swap(odd, 1)] for even, odd in own_pair]
            passed_value = swap(ends_value[1], 1)
        arrived = ring_on(message)
        if step + 2 < n_mp:
            near = [step + 1, step + 2] if step + 3 == n_mp else [step + 1]
            for level_step in near:
                passed[level_step] = swap(sent[level_step], 1)
            here = [passed[level_step] for level_step in near]
            turned_pair, turned_value, here = together(turned_pair, turned_value, here)
            passed.update(zip(near, here))
            for level_step in near:
                dtype = F32 if level_step == n_mp - 1 else BF
                partial[level_step] = back_even(chosen[level_step], passed[level_step], dtype)
            if step + 3 == n_mp:
                partial[n_mp - 2], partial[n_mp - 1] = together(partial[n_mp - 2], partial[n_mp - 1])
            else:
                chosen[step + 3], sent[step + 3] = back_odd(step + 3, turned_pair, turned_value)
            if step == 1:
                late_pair = late_messages(turned_pair, far_pair)
                own_pair = messages(turned_pair, (0,), (1,))
                ends_value = scatter_end(turned_value, first_value, 1, late_value)
    out_value = place_call(core, ends_value[0], passed_value, cols, 0)
    here, there = {}, {}
    for r, (own_even, own_odd), (even_x, odd_y) in zip(blocks_of_four, own_pair, early_pair):
        here[r] = (own_even.astype(F32) + even_x.astype(F32)).astype(BF)
        there[r] = (own_odd.astype(F32) + odd_y.astype(F32)).astype(BF)
    arrived, out_value, here, there = together(arrived, out_value, here, there)
    total = partial[n_mp - 1] + arrived.astype(F32)

    mine = lax.dynamic_slice_in_dim(total, core * own, own, 1)
    other = lax.dynamic_slice_in_dim(total, (1 - core) * own, own, 1).astype(BF)
    other = swap(other, 1)

    for r, (odd_x, even_y) in zip(blocks_of_four, late_pair):
        here[r], there[r] = [here[r], even_y], [there[r], odd_x]
    bit = n_dp // 2
    while bit >= 8:
        for parts in (here, there):
            for r in [r for r in parts if r >= bit]:
                parts[r ^ bit].append(swap(sum(p.astype(F32) for p in parts.pop(r)).astype(BF), bit))
        bit //= 2
    out_query, out_key = gather_call(core, here[0], there[0], cols)
    other, out_query, out_key = together(other, out_query, out_key)
    grad_tokens = finish_call(place, mine, other, unit_rows, row_spread, norm_gain, rows)
    return (grad_tokens, out_query, out_key, out_value)


def solution(mesh):
    matrix = P("dp", "mp")
    token_rows = P(("dp", "mp"), None)
    return jax.shard_map(
        functools.partial(per_device, mesh.shape["dp"], mesh.shape["mp"]),
        mesh=mesh,
        in_specs=(token_rows, P(), P(), P(), matrix, matrix, matrix, matrix),
        out_specs=(token_rows, matrix, matrix, matrix),
        check_vma=False,
    )
```
